128 devices in a mesh: dp: 32 (over z, x, y_lo), mp: 4 (over y_hi, core).
Axes of the slice: x: 4, y: 4 (y_hi: 2, y_lo: 2; y = y_hi * 2 + y_lo), z: 4, core: 2. Of those that a mesh axis runs over, the one named last changes fastest.
Arguments:
- vision_layer_entry: bfloat16 [16384, 1024], P('dp'), may hold values from -6 to 6
- latent_preact_values: bfloat16 [16384, 4096], P('dp', 'mp'), may hold values from -6 to 6
- final_layer_result: bfloat16 [16384, 1024], P('dp'), may hold values from -6 to 6
- caption_vectors_raw: bfloat16 [16384, 1024], P(('dp', 'mp')), may hold values from -0.19921875 to 0.19921875
- sharpness_factor: float32 [1], replicated, may hold values from 8 to 20
- offset_term: float32 [1], replicated, may hold values from -10 to -4
- first_feedforward_matrix: bfloat16 [1024, 4096], P(None, 'mp'), may hold values from -0.1875 to 0.1875
- second_feedforward_matrix: bfloat16 [4096, 1024], P('mp'), may hold values from -0.09375 to 0.09375
- mapper_matrix: bfloat16 [1024, 1024], P(None, 'mp'), may hold values from -0.1875 to 0.1875
- first_matrix_velocity: bfloat16 [1024, 4096], P(None, 'mp'), may hold values from -6 to 6
- second_matrix_velocity: bfloat16 [4096, 1024], P('mp'), may hold values from -6 to 6
- mapper_velocity: bfloat16 [1024, 1024], P(None, 'mp'), may hold values from -6 to 6
Outputs:
- update_up: bfloat16 [1024, 4096], P(None, 'mp')
- update_down: bfloat16 [4096, 1024], P('mp')
- update_proj: bfloat16 [1024, 1024], P(None, 'mp')
- renewed_up: bfloat16 [1024, 4096], P(None, 'mp')
- renewed_down: bfloat16 [4096, 1024], P('mp')
- renewed_proj: bfloat16 [1024, 1024], P(None, 'mp')
- text_grad: float32 [16384, 1024], P(('dp', 'mp'))
The draws below stay inside these ranges and needn't reach their ends.
All inputs are finite; a program needn't handle non-finite values.
Results may differ from the reference program's by a relative error of at most 0.02.
Values may be sent and summed in bfloat16 or wider, within the bound.
A program may use at most 128 MiB of HBM per device.

```python
import jax
import jax.numpy as jnp
from jax import lax

WIDTH = 1024
HIDDEN_SIZE = 4096
EMBED = 1024
IMG_GRP = 512
BATCH = 16384
N_DP = 32


def shard_levels(own_key, dims, cuts, least, high):
    def one(position, blocks):
        steps = jax.random.uniform(jax.random.fold_in(jax.random.fold_in(own_key, 6), position), (blocks,), jnp.float32, least / len(cuts), high / len(cuts))
        return jnp.repeat(jnp.exp(steps), dims[position] // blocks).reshape((-1,) + (1,) * (len(dims) - position - 1))

    loudness = one(*cuts[0])
    for cut in cuts[1:]:
        loudness = loudness * one(*cut)
    return loudness


def gaussian(rng, shape, deviation, bound, cuts=(), held_as=jnp.bfloat16):
    drawn = deviation * jax.random.normal(rng, shape, jnp.float32)
    if cuts:
        drawn = drawn * shard_levels(rng, shape, cuts, -0.22, 0.18)
    return jnp.clip(drawn, -bound, bound).astype(held_as)


def setup_inputs(seed: int = 0) -> dict:
    keys = jax.random.split(jax.random.key(seed), 13)
    return {
        "vision_layer_entry": gaussian(keys[0], (BATCH, WIDTH), 1.0, 6.0, ((0, 32),)),
        "latent_preact_values": gaussian(keys[1], (BATCH, HIDDEN_SIZE), 1.0, 6.0, ((0, 32), (1, 4))),
        "final_layer_result": gaussian(keys[2], (BATCH, WIDTH), 1.0, 6.0, ((0, 32),)),
        "caption_vectors_raw": gaussian(keys[3], (BATCH, EMBED), 0.03125, 0.19921875, ((0, 128),)),
        "sharpness_factor": jnp.clip(jax.random.uniform(keys[4], (1,), jnp.float32, 8.0, 20.0), 8.0, 20.0),
        "offset_term": jnp.clip(jax.random.uniform(keys[5], (1,), jnp.float32, -10.0, -4.0), -10.0, -4.0),
        "first_feedforward_matrix": gaussian(keys[6], (WIDTH, HIDDEN_SIZE), WIDTH ** -0.5, 0.1875, ((1, 4),)),
        "second_feedforward_matrix": gaussian(keys[7], (HIDDEN_SIZE, WIDTH), HIDDEN_SIZE ** -0.5, 0.09375, ((0, 4),)),
        "mapper_matrix": gaussian(keys[8], (WIDTH, EMBED), WIDTH ** -0.5, 0.1875, ((1, 4),)),
        "first_matrix_velocity": gaussian(keys[9], (WIDTH, HIDDEN_SIZE), 1.0, 6.0, ((1, 4),)),
        "second_matrix_velocity": gaussian(keys[10], (HIDDEN_SIZE, WIDTH), 1.0, 6.0, ((0, 4),)),
        "mapper_velocity": gaussian(keys[11], (WIDTH, EMBED), 1.0, 6.0, ((1, 4),)),
    }


def unit_rows(values):
    factor = lax.rsqrt(lax.optimization_barrier(jnp.sum(values * values, axis=1, keepdims=True)) + 1e-06)
    return (values * factor, factor)

def couple_derivs(vision_members, caption_members, matched_flag, similarity_scaling, offset_amount):
    similarity_grade = lax.dot_general(vision_members, caption_members, (((1,), (1,)), ((), ())), preferred_element_type=jnp.float32)
    raw_similarity = similarity_scaling * similarity_grade + offset_amount
    label = jnp.where(matched_flag, 1.0, -1.0).astype(jnp.float32)
    gradient_ratio = -label * jax.nn.sigmoid(-label * raw_similarity)
    return (similarity_scaling * gradient_ratio).astype(jnp.bfloat16)

def lion_step(weight, moment, grad, axis):
    moment_wide = moment.astype(jnp.float32)
    blend = 0.9 * moment_wide + 0.1 * grad
    spread = jnp.sqrt(lax.optimization_barrier(jnp.mean(blend * blend, axis=axis, keepdims=True)) + 1e-06)
    soft = blend / jnp.sqrt(blend * blend + 0.25 * spread * (0.25 * spread))
    update = (soft + 1.0 * weight.astype(jnp.float32)).astype(jnp.bfloat16)
    renewed = (0.99 * moment_wide + 0.01 * grad).astype(jnp.bfloat16)
    return (update, renewed)

def contract_rows(left, right):
    return lax.dot_general(left, right, (((0,), (0,)), ((), ())), preferred_element_type=jnp.float32)

def contract_cols(left, right):
    return lax.dot_general(left, right, (((1,), (1,)), ((), ())), preferred_element_type=jnp.float32)

def reference(vision_layer_entry, latent_preact_values, final_layer_result, caption_vectors_raw, sharpness_factor, offset_term, first_feedforward_matrix, second_feedforward_matrix, mapper_matrix, first_matrix_velocity, second_matrix_velocity, mapper_velocity):
    similarity_scaling = sharpness_factor[0]
    offset_amount = offset_term[0]
    embedded = jnp.dot(final_layer_result, mapper_matrix, preferred_element_type=jnp.float32).astype(jnp.bfloat16)
    vision_members, image_scale = unit_rows(embedded.astype(jnp.float32))
    vision_reduced = vision_members.astype(jnp.bfloat16)
    caption_members, text_scale = unit_rows(caption_vectors_raw.astype(jnp.float32))
    caption_reduced = caption_members.astype(jnp.bfloat16)
    blocks = vision_reduced.reshape(N_DP, IMG_GRP, EMBED)
    starts = jnp.arange(N_DP, dtype=jnp.int32) * IMG_GRP
    columns = jnp.arange(BATCH, dtype=jnp.int32)

    def visit(text_acc, pieces):
        vision_final_layer, first = pieces
        matched_flag = (first + jnp.arange(IMG_GRP, dtype=jnp.int32))[:, None] == columns[None, :]
        parameter_tensors = couple_derivs(vision_final_layer, caption_reduced, matched_flag, similarity_scaling, offset_amount)
        image_part = jnp.dot(parameter_tensors, caption_reduced, preferred_element_type=jnp.float32)
        text_acc = text_acc + contract_rows(parameter_tensors, vision_final_layer)
        return (text_acc, image_part)
    text_acc, image_parts = lax.scan(visit, jnp.zeros((BATCH, EMBED), jnp.float32), (blocks, starts))
    image_dz = image_parts.reshape(BATCH, EMBED)
    text_grad = text_scale * (text_acc - caption_members * lax.optimization_barrier(jnp.sum(caption_members * text_acc, axis=1, keepdims=True)))
    image_grad = (image_scale * (image_dz - vision_members * lax.optimization_barrier(jnp.sum(vision_members * image_dz, axis=1, keepdims=True)))).astype(jnp.bfloat16)
    grad_proj = contract_rows(final_layer_result, image_grad)
    back = contract_cols(image_grad, mapper_matrix).astype(jnp.bfloat16)
    active, gelu_back = jax.vjp(jax.nn.gelu, latent_preact_values.astype(jnp.float32))
    grad_down = contract_rows(active.astype(jnp.bfloat16), back)
    inner = contract_cols(back, second_feedforward_matrix)
    pre_grad = gelu_back(inner)[0].astype(jnp.bfloat16)
    grad_up = contract_rows(vision_layer_entry, pre_grad)
    update_up, renewed_up = lion_step(first_feedforward_matrix, first_matrix_velocity, grad_up, 0)
    update_down, renewed_down = lion_step(second_feedforward_matrix, second_matrix_velocity, grad_down, 1)
    update_proj, renewed_proj = lion_step(mapper_matrix, mapper_velocity, grad_proj, 0)
    return (update_up, update_down, update_proj, renewed_up, renewed_down, renewed_proj, text_grad)
```

```python
import functools

import jax
import jax.numpy as jnp
from jax import lax
from jax.experimental import pallas as pl
from jax.experimental.pallas import tpu as pltpu
from jax.sharding import PartitionSpec as P

MESH = pl.DeviceIdType.MESH
F32 = jnp.float32
BF16 = jnp.bfloat16
VMEM = pl.BlockSpec(memory_space=pltpu.VMEM)
SMEM = pl.BlockSpec(memory_space=pltpu.SMEM)

TEXT_STEPS = ((0, 1), (1, 0), (3, 0), (1, 1), (3, 1), (2, 0), (2, 1))
IMAGE_STEPS = (1, 3, 2)


def place():
    d = lax.axis_index("dp")
    m = lax.axis_index("mp")
    return d // 8, (d // 2) % 4, d % 2, m // 2, m % 2


def device(z, x, lo, hi, core):
    return ((z % 4) * 4 + x % 4) * 2 + lo % 2, (hi % 2) * 2 + core % 2


def remote(src, dst, send, recv, to):
    return pltpu.make_async_remote_copy(
        src_ref=src, dst_ref=dst, send_sem=send, recv_sem=recv, device_id=to, device_id_type=MESH
    )


def nn(a, b):
    return jnp.dot(a, b, preferred_element_type=F32)


def nt(a, b):
    return lax.dot_general(a, b, (((1,), (1,)), ((), ())), preferred_element_type=F32)


def tn(a, b):
    return lax.dot_general(a, b, (((0,), (0,)), ((), ())), preferred_element_type=F32)


def pair_kernel(
    sharp,
    offset,
    caption,
    final,
    mapper,
    grad_out,
    mapper_out,
    text_out,
    texts,
    images,
    weights,
    maps,
    embed,
    units,
    scale,
    text_unit,
    text_scale,
    image_own,
    image_send,
    image_recv,
    text_own,
    text_send,
    text_recv,
    text_part,
    cross_send,
    cross_recv,
    grads,
    t_s,
    t_r,
    f_s,
    f_r,
    m_s,
    m_r,
    a_s,
    a_r,
    i_s,
    i_r,
    x_s,
    x_r,
    r_s,
    r_r,
    c_s,
    c_r,
    g_s,
    g_r,
):
    z, x, lo, hi, core = place()
    sibling = device(z, x, lo, hi, core + 1)
    across = device(z, x, lo, hi + 1, core)
    beside = device(z, x, lo + 1, hi + 1, core)
    text_to = [device(z + a, x, lo + b, hi, core) for a, b in TEXT_STEPS]
    text_from = [device(z + 4 - a, x, lo + b, hi, core) for a, b in TEXT_STEPS]
    image_to = [device(z, x + a, lo, hi, core) for a in IMAGE_STEPS]
    image_from = [device(z, x + 4 - a, lo, hi, core) for a in IMAGE_STEPS]

    barrier = pltpu.get_barrier_semaphore()
    partners = text_to + image_to + [sibling, across, beside]
    for one in partners:
        pl.semaphore_signal(barrier, inc=1, device_id=one, device_id_type=MESH)

    raw = caption[...].astype(F32)
    ts = lax.rsqrt(jnp.sum(raw * raw, axis=1, keepdims=True) + 1e-06)
    tu = raw * ts
    text_unit[...] = tu
    text_scale[...] = ts
    texts[0:128, :] = tu.astype(BF16)
    maps[0] = mapper[...]

    pl.semaphore_wait(barrier, len(partners))

    map_copies = [
        remote(maps.at[0], maps.at[2], m_s.at[1], m_r.at[1], beside),
        remote(maps.at[0], maps.at[1], m_s.at[0], m_r.at[0], sibling),
    ]
    for one in map_copies:
        one.start()
    text_copies = [
        remote(texts.at[pl.ds(0, 128)], texts.at[pl.ds(128 * (k + 1), 128)], t_s.at[k], t_r.at[k], to)
        for k, to in enumerate(text_to)
    ]
    for one in text_copies:
        one.start()
    forward = [
        remote(
            texts.at[pl.ds(128 * k, 128)],
            texts.at[pl.ds(1024 + 128 * k, 128)],
            f_s.at[k],
            f_r.at[k],
            sibling,
        )
        for k in range(8)
    ]
    forward[0].start()

    half = pl.ds(core * 256, 256)

    def embed_with(k, h, c):
        column = pl.multiple_of((h % 2) * 512 + (c % 2) * 256, 256)
        embed[:, pl.ds(column, 256)] = nn(final[half, :], maps[k]).astype(BF16)

    embed_with(0, hi, core)
    map_copies[1].wait_recv()
    embed_with(1, hi, core + 1)
    map_copies[0].wait_recv()
    pass_map = remote(maps.at[2], maps.at[3], m_s.at[2], m_r.at[2], sibling)
    pass_map.start()
    embed_with(2, hi + 1, core)
    pass_map.wait_recv()
    embed_with(3, hi + 1, core + 1)

    wide = embed[...].astype(F32)
    s = lax.rsqrt(jnp.sum(wide * wide, axis=1, keepdims=True) + 1e-06)
    u = wide * s
    units[...] = u
    scale[...] = s
    images[0:256, :] = u.astype(BF16)

    image_copies = [
        remote(images.at[pl.ds(0, 256)], images.at[pl.ds(256 * (k + 1), 256)], a_s.at[k], a_r.at[k], to)
        for k, to in enumerate(image_to)
    ]
    for one in image_copies:
        one.start()

    mapper_out[hi * 2 + core] = maps[0]
    mapper_out[hi * 2 + (1 - core)] = maps[1]
    mapper_out[(1 - hi) * 2 + core] = maps[2]
    mapper_out[(1 - hi) * 2 + (1 - core)] = maps[3]

    for k in range(7):
        text_copies[k].wait_recv()
        forward[k + 1].start()
    for k in range(8):
        forward[k].wait_recv()

    factor = sharp[0]
    shift = offset[0]

    def pair_weights(b):
        rows = pl.ds(256 * b, 256)

        def chunk(j, _):
            cols = pl.ds(pl.multiple_of(j * 512, 512), 512)
            logits = factor * nt(images[rows, :], texts[cols, :]) + shift
            w = factor / (1.0 + jnp.exp(-logits))
            if b == 0:
                row = lax.broadcasted_iota(jnp.int32, (256, 512), 0)
                col = lax.broadcasted_iota(jnp.int32, (256, 512), 1)
                cls = jnp.where(j == 0, core, 1 - core)
                on = jnp.logical_and(core == hi, j % 2 == 0).astype(jnp.int32)
                hit = (row == cls * 128 + col) & (col < 128 * on)
                w = jnp.where(hit, -factor / (1.0 + jnp.exp(logits)), w)
            weights[rows, cols] = w.astype(BF16)
            return 0

        lax.fori_loop(0, 4, chunk, 0)

    def image_part(b, out):
        rows = pl.ds(256 * b, 256)

        def chunk(j, _):
            cols = pl.ds(pl.multiple_of(j * 256, 256), 256)
            out[:, cols] = nn(weights[rows, :], texts[:, cols]).astype(out.dtype)
            return 0

        lax.fori_loop(0, 4, chunk, 0)

    pair_weights(0)
    image_part(0, image_own)
    image_back = [
        remote(image_send.at[k], image_recv.at[k], i_s.at[k], i_r.at[k], image_from[k]) for k in range(3)
    ]
    for k in range(3):
        image_copies[k].wait_recv()
        pair_weights(k + 1)
        image_part(k + 1, image_send.at[k])
        image_back[k].start()

    def text_chunk(base, out):
        def chunk(j, _):
            rows = pl.ds(pl.multiple_of(j * 256, 256), 256)
            cols = pl.ds(pl.multiple_of(base + j * 256, 256), 256)
            out[rows, :] = tn(weights[:, cols], images[...]).astype(out.dtype)
            return 0

        lax.fori_loop(0, 4, chunk, 0)

    text_chunk(1024, cross_send)
    cross = remote(cross_send, cross_recv, x_s, x_r, sibling)
    cross.start()
    text_chunk(0, text_own)
    cross.wait_recv()

    def add_cross(j, _):
        rows = pl.ds(pl.multiple_of(j * 128, 128), 128)
        total = text_own[rows, :] + cross_recv[rows, :].astype(F32)
        text_own[rows, :] = total
        text_send[rows, :] = total.astype(BF16)
        return 0

    lax.fori_loop(0, 8, add_cross, 0)
    text_back = [
        remote(text_send.at[pl.ds(128 * (k + 1), 128)], text_recv.at[k], r_s.at[k], r_r.at[k], text_from[k])
        for k in range(7)
    ]
    for one in text_back:
        one.start()

    for k in range(3):
        image_back[k].wait_recv()

    mine = pl.ds(pl.multiple_of(hi * 128, 128), 128)
    theirs = pl.ds(pl.multiple_of((1 - hi) * 128, 128), 128)

    def image_sum(rows):
        total = image_own[rows, :]
        for k in range(3):
            total = total + image_recv[k, rows, :].astype(F32)
        return total

    text_part[...] = image_sum(theirs).astype(BF16)
    swap = remote(text_part, grads.at[0], c_s, c_r, across)
    swap.start()
    image_own[mine, :] = image_sum(mine)
    swap.wait_recv()
    dz = image_own[mine, :] + grads[0].astype(F32)
    u = units[mine, :]
    grad = scale[mine, :] * (dz - u * jnp.sum(u * dz, axis=1, keepdims=True))
    grads[1] = grad.astype(BF16)
    spread = [
        remote(grads.at[1], grads.at[2], g_s.at[0], g_r.at[0], across),
        remote(grads.at[1], grads.at[3], g_s.at[1], g_r.at[1], sibling),
    ]
    for one in spread:
        one.start()

    for k in range(7):
        text_back[k].wait_recv()
    dz = text_own[0:128, :]
    for k in range(7):
        dz = dz + text_recv[k].astype(F32)
    tu = text_unit[...]
    text_out[...] = text_scale[...] * (dz - tu * jnp.sum(tu * dz, axis=1, keepdims=True))

    spread[0].wait_recv()
    last = remote(grads.at[2], grads.at[4], g_s.at[2], g_r.at[2], sibling)
    last.start()
    spread[1].wait_recv()
    last.wait_recv()

    def put(k, h, c):
        grad_out[pl.ds(pl.multiple_of(c * 256 + h * 128, 128), 128), :] = grads[k]

    put(1, hi, core)
    put(2, 1 - hi, core)
    put(3, hi, 1 - core)
    put(4, 1 - hi, 1 - core)

    for one in (
        map_copies + [pass_map] + text_copies + forward + image_copies + image_back
        + [cross] + text_back + [swap] + spread + [last]
    ):
        one.wait_send()


def pairs(sharp, offset, caption, final, mapper):
    dma = pltpu.SemaphoreType.DMA
    return pl.pallas_call(
        pair_kernel,
        name="pairs",
        out_shape=(
            jax.ShapeDtypeStruct((512, 1024), BF16),
            jax.ShapeDtypeStruct((4, 1024, 256), BF16),
            jax.ShapeDtypeStruct((128, 1024), F32),
        ),
        in_specs=[SMEM, SMEM, VMEM, VMEM, VMEM],
        out_specs=(VMEM, VMEM, VMEM),
        scratch_shapes=[
            pltpu.VMEM((2048, 1024), BF16),
            pltpu.VMEM((1024, 1024), BF16),
            pltpu.VMEM((1024, 2048), BF16),
            pltpu.VMEM((4, 1024, 256), BF16),
            pltpu.VMEM((256, 1024), BF16),
            pltpu.VMEM((256, 1024), F32),
            pltpu.VMEM((256, 1), F32),
            pltpu.VMEM((128, 1024), F32),
            pltpu.VMEM((128, 1), F32),
            pltpu.VMEM((256, 1024), F32),
            pltpu.VMEM((3, 256, 1024), BF16),
            pltpu.VMEM((3, 256, 1024), BF16),
            pltpu.VMEM((1024, 1024), F32),
            pltpu.VMEM((1024, 1024), BF16),
            pltpu.VMEM((7, 128, 1024), BF16),
            pltpu.VMEM((128, 1024), BF16),
            pltpu.VMEM((1024, 1024), BF16),
            pltpu.VMEM((1024, 1024), BF16),
            pltpu.VMEM((5, 128, 1024), BF16),
            dma((7,)), dma((7,)),
            dma((8,)), dma((8,)),
            dma((3,)), dma((3,)),
            dma((3,)), dma((3,)),
            dma((3,)), dma((3,)),
            dma, dma,
            dma((7,)), dma((7,)),
            dma, dma,
            dma((3,)), dma((3,)),
        ],
        compiler_params=pltpu.CompilerParams(
            collective_id=0, has_side_effects=True, vmem_limit_bytes=56 * 2**20
        ),
    )(sharp, offset, caption, final, mapper)


def lion_step(weight, moment, grad, axis):
    moment_wide = moment.astype(F32)
    blend = 0.9 * moment_wide + 0.1 * grad
    spread = jnp.sqrt(jnp.mean(blend * blend, axis=axis, keepdims=True) + 1e-06)
    soft = blend / jnp.sqrt(blend * blend + 0.25 * spread * (0.25 * spread))
    update = (soft + 1.0 * weight.astype(F32)).astype(BF16)
    renewed = (0.99 * moment_wide + 0.01 * grad).astype(BF16)
    return (update, renewed)


def per_device(
    vision_layer_entry,
    latent_preact_values,
    final_layer_result,
    caption_vectors_raw,
    sharpness_factor,
    offset_term,
    first_feedforward_matrix,
    second_feedforward_matrix,
    mapper_matrix,
    first_matrix_velocity,
    second_matrix_velocity,
    mapper_velocity,
):
    image_grad, maps, text_grad = pairs(
        sharpness_factor, offset_term, caption_vectors_raw, final_layer_result, mapper_matrix
    )
    column = lax.axis_index("mp")
    own_columns = lax.dynamic_slice_in_dim(image_grad, column * 256, 256, 1)
    grad_proj = tn(final_layer_result, own_columns)
    mapper_full = jnp.concatenate([maps[k] for k in range(4)], axis=1)
    back = nt(image_grad, mapper_full).astype(BF16)
    active, gelu_back = jax.vjp(jax.nn.gelu, latent_preact_values.astype(F32))
    grad_down = tn(active.astype(BF16), back)
    inner = nt(back, second_feedforward_matrix)
    pre_grad = gelu_back(inner)[0].astype(BF16)
    grad_up = tn(vision_layer_entry, pre_grad)
    grad_up, grad_down, grad_proj = (
        lax.psum(grad_up.astype(BF16), "dp").astype(F32),
        lax.psum(grad_down.astype(BF16), "dp").astype(F32),
        lax.psum(grad_proj.astype(BF16), "dp").astype(F32),
    )
    update_up, renewed_up = lion_step(first_feedforward_matrix, first_matrix_velocity, grad_up, 0)
    update_down, renewed_down = lion_step(
        second_feedforward_matrix, second_matrix_velocity, grad_down, 1
    )
    update_proj, renewed_proj = lion_step(mapper_matrix, mapper_velocity, grad_proj, 0)
    return (update_up, update_down, update_proj, renewed_up, renewed_down, renewed_proj, text_grad)


def solution(mesh):
    return jax.shard_map(
        per_device,
        mesh=mesh,
        in_specs=(
            P("dp", None),
            P("dp", "mp"),
            P("dp", None),
            P(("dp", "mp"), None),
            P(),
            P(),
            P(None, "mp"),
            P("mp", None),
            P(None, "mp"),
            P(None, "mp"),
            P("mp", None),
            P(None, "mp"),
        ),
        out_specs=(
            P(None, "mp"),
            P("mp", None),
            P(None, "mp"),
            P(None, "mp"),
            P("mp", None),
            P(None, "mp"),
            P(("dp", "mp"), None),
        ),
        check_vma=False,
    )
```

```python
import functools

import jax
import jax.numpy as jnp
from jax import lax
from jax.experimental import pallas as pl
from jax.experimental.pallas import tpu as pltpu
from jax.sharding import PartitionSpec as P

MESH = pl.DeviceIdType.MESH
F32 = jnp.float32
BF16 = jnp.bfloat16
VMEM = pl.BlockSpec(memory_space=pltpu.VMEM)
SMEM = pl.BlockSpec(memory_space=pltpu.SMEM)

TEXT_STEPS = ((0, 1), (1, 0), (3, 0), (1, 1), (3, 1), (2, 0), (2, 1))
IMAGE_STEPS = (1, 3, 2)


def place():
    d = lax.axis_index("dp")
    m = lax.axis_index("mp")
    return d // 8, (d // 2) % 4, d % 2, m // 2, m % 2


def device(z, x, lo, hi, core):
    return ((z % 4) * 4 + x % 4) * 2 + lo % 2, (hi % 2) * 2 + core % 2


def remote(src, dst, send, recv, to):
    return pltpu.make_async_remote_copy(
        src_ref=src, dst_ref=dst, send_sem=send, recv_sem=recv, device_id=to, device_id_type=MESH
    )


def nn(a, b):
    return jnp.dot(a, b, preferred_element_type=F32)


def nt(a, b):
    return lax.dot_general(a, b, (((1,), (1,)), ((), ())), preferred_element_type=F32)


def tn(a, b):
    return lax.dot_general(a, b, (((0,), (0,)), ((), ())), preferred_element_type=F32)


def map_columns(hi, core):
    return pl.ds(pl.multiple_of((hi % 2) * 512 + (core % 2) * 256, 256), 256)


def pair_kernel(
    sharp,
    offset,
    caption,
    final,
    mapper,
    grad_out,
    mapper_out,
    text_out,
    texts,
    images,
    weights,
    maps,
    embed,
    units,
    scale,
    text_unit,
    text_scale,
    image_own,
    image_send,
    image_recv,
    text_own,
    text_send,
    text_recv,
    text_part,
    cross_send,
    cross_recv,
    grads,
    t_s,
    t_r,
    f_s,
    f_r,
    m_s,
    m_r,
    a_s,
    a_r,
    i_s,
    i_r,
    x_s,
    x_r,
    r_s,
    r_r,
    c_s,
    c_r,
    g_s,
    g_r,
):
    z, x, lo, hi, core = place()
    sibling = device(z, x, lo, hi, core + 1)
    across = device(z, x, lo, hi + 1, core)
    beside = device(z, x, lo + 1, hi + 1, core)
    text_to = [device(z + a, x, lo + b, hi, core) for a, b in TEXT_STEPS]
    text_from = [device(z + 4 - a, x, lo + b, hi, core) for a, b in TEXT_STEPS]
    image_to = [device(z, x + a, lo, hi, core) for a in IMAGE_STEPS]
    image_from = [device(z, x + 4 - a, lo, hi, core) for a in IMAGE_STEPS]

    barrier = pltpu.get_barrier_semaphore()
    partners = text_to + image_to + [sibling, across, beside]
    for one in partners:
        pl.semaphore_signal(barrier, inc=1, device_id=one, device_id_type=MESH)

    raw = caption[...].astype(F32)
    ts = lax.rsqrt(jnp.sum(raw * raw, axis=1, keepdims=True) + 1e-06)
    tu = raw * ts
    text_unit[...] = tu
    text_scale[...] = ts
    texts[0:128, :] = tu.astype(BF16)
    maps[0] = mapper[...]

    pl.semaphore_wait(barrier, len(partners))

    map_copies = [
        remote(maps.at[0], maps.at[2], m_s.at[1], m_r.at[1], beside),
        remote(maps.at[0], maps.at[1], m_s.at[0], m_r.at[0], sibling),
    ]
    for one in map_copies:
        one.start()
    text_copies = [
        remote(texts.at[pl.ds(0, 128)], texts.at[pl.ds(128 * (k + 1), 128)], t_s.at[k], t_r.at[k], to)
        for k, to in enumerate(text_to)
    ]
    for one in text_copies:
        one.start()
    forward = [
        remote(
            texts.at[pl.ds(128 * k, 128)],
            texts.at[pl.ds(1024 + 128 * k, 128)],
            f_s.at[k],
            f_r.at[k],
            sibling,
        )
        for k in range(8)
    ]
    forward[0].start()

    half = pl.ds(core * 256, 256)

    def embed_with(k, h, c):
        embed[:, map_columns(h, c)] = nn(final[half, :], maps[k]).astype(BF16)

    embed_with(0, hi, core)
    map_copies[1].wait_recv()
    embed_with(1, hi, core + 1)
    map_copies[0].wait_recv()
    pass_map = remote(maps.at[2], maps.at[3], m_s.at[2], m_r.at[2], sibling)
    pass_map.start()
    embed_with(2, hi + 1, core)
    pass_map.wait_recv()
    embed_with(3, hi + 1, core + 1)

    wide = embed[...].astype(F32)
    s = lax.rsqrt(jnp.sum(wide * wide, axis=1, keepdims=True) + 1e-06)
    u = wide * s
    units[...] = u
    scale[...] = s
    images[0:256, :] = u.astype(BF16)

    image_copies = [
        remote(images.at[pl.ds(0, 256)], images.at[pl.ds(256 * (k + 1), 256)], a_s.at[k], a_r.at[k], to)
        for k, to in enumerate(image_to)
    ]
    for one in image_copies:
        one.start()

    mapper_out[:, map_columns(hi, core)] = maps[0]
    mapper_out[:, map_columns(hi, core + 1)] = maps[1]
    mapper_out[:, map_columns(hi + 1, core)] = maps[2]
    mapper_out[:, map_columns(hi + 1, core + 1)] = maps[3]

    for k in range(7):
        text_copies[k].wait_recv()
        forward[k + 1].start()
    for k in range(8):
        forward[k].wait_recv()

    factor = sharp[0]
    shift = offset[0]

    def pair_weights(b):
        rows = pl.ds(256 * b, 256)

        def chunk(j, _):
            cols = pl.ds(pl.multiple_of(j * 512, 512), 512)
            logits = factor * nt(images[rows, :], texts[cols, :]) + shift
            w = factor / (1.0 + jnp.exp(-logits))
            if b == 0:
                row = lax.broadcasted_iota(jnp.int32, (256, 512), 0)
                col = lax.broadcasted_iota(jnp.int32, (256, 512), 1)
                cls = jnp.where(j == 0, core, 1 - core)
                on = jnp.logical_and(core == hi, j % 2 == 0).astype(jnp.int32)
                hit = (row == cls * 128 + col) & (col < 128 * on)
                w = jnp.where(hit, -factor / (1.0 + jnp.exp(logits)), w)
            weights[rows, cols] = w.astype(BF16)
            return 0

        lax.fori_loop(0, 4, chunk, 0)

    def image_part(b, out):
        rows = pl.ds(256 * b, 256)

        def chunk(j, _):
            cols = pl.ds(pl.multiple_of(j * 256, 256), 256)
            out[:, cols] = nn(weights[rows, :], texts[:, cols]).astype(out.dtype)
            return 0

        lax.fori_loop(0, 4, chunk, 0)

    pair_weights(0)
    image_part(0, image_own)
    image_back = [
        remote(image_send.at[k], image_recv.at[k], i_s.at[k], i_r.at[k], image_from[k]) for k in range(3)
    ]
    for k in range(3):
        image_copies[k].wait_recv()
        pair_weights(k + 1)
        image_part(k + 1, image_send.at[k])
        image_back[k].start()

    def text_chunk(base, out):
        def chunk(j, _):
            rows = pl.ds(pl.multiple_of(j * 256, 256), 256)
            cols = pl.ds(pl.multiple_of(base + j * 256, 256), 256)
            out[rows, :] = tn(weights[:, cols], images[...]).astype(out.dtype)
            return 0

        lax.fori_loop(0, 4, chunk, 0)

    text_chunk(1024, cross_send)
    cross = remote(cross_send, cross_recv, x_s, x_r, sibling)
    cross.start()
    text_chunk(0, text_own)
    cross.wait_recv()

    def add_cross(j, _):
        rows = pl.ds(pl.multiple_of(j * 128, 128), 128)
        total = text_own[rows, :] + cross_recv[rows, :].astype(F32)
        text_own[rows, :] = total
        text_send[rows, :] = total.astype(BF16)
        return 0

    lax.fori_loop(0, 8, add_cross, 0)
    text_back = [
        remote(text_send.at[pl.ds(128 * (k + 1), 128)], text_recv.at[k], r_s.at[k], r_r.at[k], text_from[k])
        for k in range(7)
    ]
    for one in text_back:
        one.start()

    for k in range(3):
        image_back[k].wait_recv()

    mine = pl.ds(pl.multiple_of(hi * 128, 128), 128)
    theirs = pl.ds(pl.multiple_of((1 - hi) * 128, 128), 128)

    def image_sum(rows):
        total = image_own[rows, :]
        for k in range(3):
            total = total + image_recv[k, rows, :].astype(F32)
        return total

    text_part[...] = image_sum(theirs).astype(BF16)
    swap = remote(text_part, grads.at[0], c_s, c_r, across)
    swap.start()
    image_own[mine, :] = image_sum(mine)
    swap.wait_recv()
    dz = image_own[mine, :] + grads[0].astype(F32)
    u = units[mine, :]
    grad = scale[mine, :] * (dz - u * jnp.sum(u * dz, axis=1, keepdims=True))
    grads[1] = grad.astype(BF16)
    spread = [
        remote(grads.at[1], grads.at[2], g_s.at[0], g_r.at[0], across),
        remote(grads.at[1], grads.at[3], g_s.at[1], g_r.at[1], sibling),
    ]
    for one in spread:
        one.start()

    for k in range(7):
        text_back[k].wait_recv()
    dz = text_own[0:128, :]
    for k in range(7):
        dz = dz + text_recv[k].astype(F32)
    tu = text_unit[...]
    text_out[...] = text_scale[...] * (dz - tu * jnp.sum(tu * dz, axis=1, keepdims=True))

    spread[0].wait_recv()
    last = remote(grads.at[2], grads.at[4], g_s.at[2], g_r.at[2], sibling)
    last.start()
    spread[1].wait_recv()
    last.wait_recv()

    def put(k, h, c):
        grad_out[pl.ds(pl.multiple_of(c * 256 + h * 128, 128), 128), :] = grads[k]

    put(1, hi, core)
    put(2, 1 - hi, core)
    put(3, hi, 1 - core)
    put(4, 1 - hi, 1 - core)

    for one in (
        map_copies + [pass_map] + text_copies + forward + image_copies + image_back
        + [cross] + text_back + [swap] + spread + [last]
    ):
        one.wait_send()


def pairs(sharp, offset, caption, final, mapper):
    dma = pltpu.SemaphoreType.DMA
    return pl.pallas_call(
        pair_kernel,
        name="pairs",
        out_shape=(
            jax.ShapeDtypeStruct((512, 1024), BF16),
            jax.ShapeDtypeStruct((1024, 1024), BF16),
            jax.ShapeDtypeStruct((128, 1024), F32),
        ),
        in_specs=[SMEM, SMEM, VMEM, VMEM, VMEM],
        out_specs=(VMEM, VMEM, VMEM),
        scratch_shapes=[
            pltpu.VMEM((2048, 1024), BF16),
            pltpu.VMEM((1024, 1024), BF16),
            pltpu.VMEM((1024, 2048), BF16),
            pltpu.VMEM((4, 1024, 256), BF16),
            pltpu.VMEM((256, 1024), BF16),
            pltpu.VMEM((256, 1024), F32),
            pltpu.VMEM((256, 1), F32),
            pltpu.VMEM((128, 1024), F32),
            pltpu.VMEM((128, 1), F32),
            pltpu.VMEM((256, 1024), F32),
            pltpu.VMEM((3, 256, 1024), BF16),
            pltpu.VMEM((3, 256, 1024), BF16),
            pltpu.VMEM((1024, 1024), F32),
            pltpu.VMEM((1024, 1024), BF16),
            pltpu.VMEM((7, 128, 1024), BF16),
            pltpu.VMEM((128, 1024), BF16),
            pltpu.VMEM((1024, 1024), BF16),
            pltpu.VMEM((1024, 1024), BF16),
            pltpu.VMEM((5, 128, 1024), BF16),
            dma((7,)), dma((7,)),
            dma((8,)), dma((8,)),
            dma((3,)), dma((3,)),
            dma((3,)), dma((3,)),
            dma((3,)), dma((3,)),
            dma, dma,
            dma((7,)), dma((7,)),
            dma, dma,
            dma((3,)), dma((3,)),
        ],
        compiler_params=pltpu.CompilerParams(
            collective_id=0, has_side_effects=True, vmem_limit_bytes=56 * 2**20
        ),
    )(sharp, offset, caption, final, mapper)


def gelu_parts(value):
    slope = 0.7978845608028654
    square = value * value
    t = jnp.tanh(slope * (value + 0.044715 * (square * value)))
    cdf = 0.5 * (1.0 + t)
    derivative = cdf + 0.5 * value * (1.0 - t * t) * (slope * (1.0 + 3 * 0.044715 * square))
    return value * cdf, derivative


PART = 1152
STRIP = 288
TILE = 144


def grad_kernel(
    image_grad,
    mapper,
    latent,
    second,
    entry,
    final,
    total_out,
    back,
    active,
    pre,
    grads,
    done,
    far_in,
    near_in,
    strip,
    side_out,
    side_in,
    tile,
    tile_out,
    tile_in,
    far_s,
    far_r,
    near_s,
    near_r,
    side_s,
    side_r,
    tile_s,
    tile_r,
    t_s,
    t_r,
    q_s,
    q_r,
    p_s,
    p_r,
):
    z, x, lo, hi, core = place()

    def step(part, along_p, along_q):
        a, b = (along_p, along_q) if part == 0 else (along_q, along_p)
        return device(z + a, x + b, lo, hi, core)

    pair_lo = device(z, x, lo + 1, hi, core)
    barrier = pltpu.get_barrier_semaphore()
    partners = [step(0, a, 0) for a in (1, 3, 2)] + [step(0, 0, a) for a in (1, 3, 2)] + [pair_lo]
    for one in partners:
        pl.semaphore_signal(barrier, inc=1, device_id=one, device_id_type=MESH)

    started = []

    def begin(copy):
        copy.start()
        started.append(copy)
        return copy

    def loop(count, body):
        def run(j, _):
            body(pl.ds(pl.multiple_of(j * 256, 256), 256))
            return 0

        lax.fori_loop(0, count, run, 0)

    first = (z, x)
    second_axis = (x, z)

    def strip_rows(part, offset):
        at = (first[part] + offset) % 4
        return pl.ds(pl.multiple_of(part * PART + at * STRIP, 16), STRIP)

    def side_columns(part, offset):
        at = (second_axis[part] + offset) % 4
        return pl.ds(pl.multiple_of(at * 256, 256), 256)

    left, right = pl.ds(0, 512), pl.ds(512, 512)

    def send_far(part):
        far = strip_rows(part, 2)
        up = begin(remote(grads.at[far, left], far_in.at[part, 0], far_s.at[part, 0], far_r.at[part, 0], step(part, 1, 0)))
        down = begin(remote(grads.at[far, right], far_in.at[part, 1], far_s.at[part, 1], far_r.at[part, 1], step(part, 3, 0)))
        n0 = begin(
            remote(
                grads.at[strip_rows(part, 1), right], near_in.at[part, 0, :, right],
                near_s.at[part, 0], near_r.at[part, 0], step(part, 1, 0),
            )
        )
        n1 = begin(
            remote(
                grads.at[strip_rows(part, 3), left], near_in.at[part, 1, :, left],
                near_s.at[part, 1], near_r.at[part, 1], step(part, 3, 0),
            )
        )
        return up, down, n0, n1

    def send_near(part, copies):
        out = []
        for k, (cols, offset) in enumerate(((left, 1), (right, 3))):
            copies[k].wait_recv()
            rows = strip_rows(part, offset)
            grads[rows, cols] = (grads[rows, cols].astype(F32) + far_in[part, k].astype(F32)).astype(BF16)
            out.append(
                begin(
                    remote(
                        grads.at[rows, cols], near_in.at[part, k, :, cols],
                        near_s.at[part, 2 + k], near_r.at[part, 2 + k], step(part, offset, 0),
                    )
                )
            )
        return out

    def send_side(part, copies, more):
        for one in copies[2:] + tuple(more):
            one.wait_recv()
        rows = strip_rows(part, 0)
        out = []
        for k, offset in enumerate((2, 1, 3, 0)):
            cols = side_columns(part, offset)
            total = (
                grads[rows, cols].astype(F32)
                + near_in[part, 0, :, cols].astype(F32)
                + near_in[part, 1, :, cols].astype(F32)
            )
            if offset == 0:
                strip[part] = total
            else:
                side_out[part, k] = total.astype(BF16)
                out.append(
                    begin(
                        remote(
                            side_out.at[part, k], side_in.at[part, k],
                            side_s.at[part, k], side_r.at[part, k], step(part, 0, offset),
                        )
                    )
                )
        return out

    mine = pl.ds(pl.multiple_of(lo * TILE, 16), TILE)
    theirs = pl.ds(pl.multiple_of((1 - lo) * TILE, 16), TILE)

    def send_tile(part, copies):
        for one in copies:
            one.wait_recv()

        def total(rows):
            value = strip[part, rows, :]
            for k in range(3):
                value = value + side_in[part, k, rows, :].astype(F32)
            return value

        tile_out[part] = total(theirs).astype(BF16)
        out = begin(remote(tile_out.at[part], tile_in.at[part], tile_s.at[part], tile_r.at[part], pair_lo))
        tile[part] = total(mine)
        return out

    def spread_tile(part, copy):
        copy.wait_recv()
        at = (part * PART + first[part] * STRIP) + lo * TILE
        rows = pl.ds(pl.multiple_of(at, 16), TILE)
        cols = side_columns(part, 0)
        done[rows, cols] = (tile[part] + tile_in[part].astype(F32)).astype(BF16)
        return begin(remote(done.at[rows, cols], done.at[rows, cols], t_s.at[part], t_r.at[part], pair_lo))

    def spread_side(part, copy):
        copy.wait_recv()
        block = done.at[strip_rows(part, 0), side_columns(part, 0)]
        return [
            begin(remote(block, block, q_s.at[part, k], q_r.at[part, k], step(part, 0, offset)))
            for k, offset in enumerate((2, 1, 3))
        ]

    def spread_strip(part, copies):
        for one in copies:
            one.wait_recv()
        out = []
        rows = strip_rows(part, 0)
        for k, (cols, offset) in enumerate(((left, 1), (right, 3), (right, 1), (left, 3))):
            block = done.at[rows, cols]
            out.append(begin(remote(block, block, p_s.at[part, k], p_r.at[part, k], step(part, offset, 0))))
        return out

    def spread_far(part, copies):
        out = []
        for k, (cols, offset) in enumerate(((left, 1), (right, 3))):
            copies[k].wait_recv()
            block = done.at[strip_rows(part, 4 - offset), cols]
            out.append(begin(remote(block, block, p_s.at[part, 4 + k], p_r.at[part, 4 + k], step(part, offset, 0))))
        return out

    def back_part(cols):
        back[:, cols] = nt(image_grad[...], mapper[cols, :]).astype(BF16)

    loop(4, back_part)

    def active_part(cols):
        value, derivative = gelu_parts(latent[:, cols].astype(F32))
        active[:, cols] = value.astype(BF16)
        pre[:, cols] = (nt(back[...], second[cols, :]) * derivative).astype(BF16)

    loop(4, active_part)

    own = image_grad[:, map_columns(hi, core)]

    def proj_part(cols):
        value = tn(final[:, cols], own).astype(BF16)
        grads[1024:1152, cols] = value[0:128]
        grads[2176:2304, cols] = value[128:256]

    loop(4, proj_part)

    def down_part(j, _):
        cols = pl.ds(pl.multiple_of(j * 256, 256), 256)
        rows = pl.ds(pl.multiple_of(PART + j * 256, 128), 256)
        grads[rows, :] = tn(active[:, cols], back[...]).astype(BF16)
        return 0

    lax.fori_loop(0, 4, down_part, 0)
    pl.semaphore_wait(barrier, len(partners))
    far_b = send_far(1)

    def up_part(cols):
        grads[cols, :] = tn(entry[:, cols], pre[...]).astype(BF16)

    loop(4, up_part)
    far_a = send_far(0)
    near_b = send_near(1, far_b)
    near_a = send_near(0, far_a)
    side_b = send_side(1, far_b, near_b)
    side_a = send_side(0, far_a, near_a)
    tile_b = send_tile(1, side_b)
    tile_a = send_tile(0, side_a)
    t_b = spread_tile(1, tile_b)
    t_a = spread_tile(0, tile_a)
    q_b = spread_side(1, t_b)
    q_a = spread_side(0, t_a)
    p_b = spread_strip(1, q_b)
    p_a = spread_strip(0, q_a)
    f_b = spread_far(1, p_b)
    f_a = spread_far(0, p_a)
    for one in p_b[2:] + p_a[2:] + f_b + f_a:
        one.wait_recv()
    for one in started:
        one.wait_send()
    total_out[...] = done[...]


def weight_grads(image_grad, mapper, latent, second, entry, final):
    dma = pltpu.SemaphoreType.DMA
    return pl.pallas_call(
        grad_kernel,
        name="weight_grads",
        out_shape=jax.ShapeDtypeStruct((2 * PART, 1024), BF16),
        in_specs=[VMEM] * 6,
        out_specs=VMEM,
        scratch_shapes=[
            pltpu.VMEM((512, 1024), BF16),
            pltpu.VMEM((512, 1024), BF16),
            pltpu.VMEM((512, 1024), BF16),
            pltpu.VMEM((2 * PART, 1024), BF16),
            pltpu.VMEM((2 * PART, 1024), BF16),
            pltpu.VMEM((2, 2, STRIP, 512), BF16),
            pltpu.VMEM((2, 2, STRIP, 1024), BF16),
            pltpu.VMEM((2, STRIP, 256), F32),
            pltpu.VMEM((2, 3, STRIP, 256), BF16),
            pltpu.VMEM((2, 3, STRIP, 256), BF16),
            pltpu.VMEM((2, TILE, 256), F32),
            pltpu.VMEM((2, TILE, 256), BF16),
            pltpu.VMEM((2, TILE, 256), BF16),
            dma((2, 2)), dma((2, 2)),
            dma((2, 4)), dma((2, 4)),
            dma((2, 3)), dma((2, 3)),
            dma((2,)), dma((2,)),
            dma((2,)), dma((2,)),
            dma((2, 3)), dma((2, 3)),
            dma((2, 6)), dma((2, 6)),
        ],
        compiler_params=pltpu.CompilerParams(
            collective_id=1, has_side_effects=True, vmem_limit_bytes=56 * 2**20
        ),
    )(image_grad, mapper, latent, second, entry, final)


def lion_block(weight, moment, grad, axis):
    grad = grad.astype(F32)
    moment = moment.astype(F32)
    blend = 0.9 * moment + 0.1 * grad
    square = blend * blend
    floor = 0.0625 * (jnp.mean(square, axis=axis, keepdims=True) + 1e-06)
    update = blend * lax.rsqrt(square + floor) + weight.astype(F32)
    return update.astype(BF16), (0.99 * moment + 0.01 * grad).astype(BF16)


def lion_kernel(
    g_up, g_down, g_proj_a, g_proj_b, w_up, w_down, w_proj, m_up, m_down, m_proj,
    u_up, u_down, u_proj, r_up, r_down, r_proj,
):
    u_up[...], r_up[...] = lion_block(w_up[...], m_up[...], g_up[...], 0)
    u_down[...], r_down[...] = lion_block(w_down[...], m_down[...], g_down[...], 1)

    @pl.when(pl.program_id(0) == 0)
    def _():
        grad = jnp.concatenate(
            [g[:, 256 * i : 256 * (i + 1)] for i in range(4) for g in (g_proj_a, g_proj_b)], axis=0
        )
        u_proj[...], r_proj[...] = lion_block(w_proj[...], m_proj[...], grad, 0)


def lion(total, weights, moments):
    column = pl.BlockSpec((1024, 128), lambda i: (0, i))
    row = pl.BlockSpec((128, 1024), lambda i: (i, 0))
    whole = pl.BlockSpec((1024, 256), lambda i: (0, 0))
    like = [column, row, whole]
    square = jax.ShapeDtypeStruct((1024, 1024), BF16)
    narrow = jax.ShapeDtypeStruct((1024, 256), BF16)
    return pl.pallas_call(
        lion_kernel,
        name="lion",
        grid=(8,),
        out_shape=(square, square, narrow, square, square, narrow),
        in_specs=[
            column,
            pl.BlockSpec((128, 1024), lambda i: (9 + i, 0)),
            pl.BlockSpec((128, 1024), lambda i: (8, 0)),
            pl.BlockSpec((128, 1024), lambda i: (17, 0)),
        ]
        + like
        + like,
        out_specs=tuple(like + like),
        compiler_params=pltpu.CompilerParams(vmem_limit_bytes=32 * 2**20),
    )(total, total, total, total, *weights, *moments)


def per_device(
    vision_layer_entry,
    latent_preact_values,
    final_layer_result,
    caption_vectors_raw,
    sharpness_factor,
    offset_term,
    first_feedforward_matrix,
    second_feedforward_matrix,
    mapper_matrix,
    first_matrix_velocity,
    second_matrix_velocity,
    mapper_velocity,
):
    image_grad, mapper_full, text_grad = pairs(
        sharpness_factor, offset_term, caption_vectors_raw, final_layer_result, mapper_matrix
    )
    total = weight_grads(
        image_grad,
        mapper_full,
        latent_preact_values,
        second_feedforward_matrix,
        vision_layer_entry,
        final_layer_result,
    )
    results = lion(
        total,
        (first_feedforward_matrix, second_feedforward_matrix, mapper_matrix),
        (first_matrix_velocity, second_matrix_velocity, mapper_velocity),
    )
    return (*results, text_grad)


def solution(mesh):
    return jax.shard_map(
        per_device,
        mesh=mesh,
        in_specs=(
            P("dp", None),
            P("dp", "mp"),
            P("dp", None),
            P(("dp", "mp"), None),
            P(),
            P(),
            P(None, "mp"),
            P("mp", None),
            P(None, "mp"),
            P(None, "mp"),
            P("mp", None),
            P(None, "mp"),
        ),
        out_specs=(
            P(None, "mp"),
            P("mp", None),
            P(None, "mp"),
            P(None, "mp"),
            P("mp", None),
            P(None, "mp"),
            P(("dp", "mp"), None),
        ),
        check_vma=False,
    )
```

```python
import types

import jax
import jax.numpy as jnp
from jax import lax
from jax.experimental import pallas as pl
from jax.experimental.pallas import tpu as pltpu
from jax.sharding import PartitionSpec as P

MESH = pl.DeviceIdType.MESH
F32 = jnp.float32
BF16 = jnp.bfloat16
VMEM = pl.BlockSpec(memory_space=pltpu.VMEM)
SMEM = pl.BlockSpec(memory_space=pltpu.SMEM)
ANY = pl.BlockSpec(memory_space=pl.ANY)

PART = 1152
STRIP = 288
TILE = 144
COPIES = 160


def nn(a, b):
    return jnp.dot(a, b, preferred_element_type=F32)


def nt(a, b):
    return lax.dot_general(a, b, (((1,), (1,)), ((), ())), preferred_element_type=F32)


def tn(a, b):
    return lax.dot_general(a, b, (((0,), (0,)), ((), ())), preferred_element_type=F32)


def cut(start, size, unit=16):
    return pl.ds(start if isinstance(start, int) else pl.multiple_of(start, unit), size)


def loop(count, body, size=256):
    def run(j, _):
        body(cut(j * size, size, size))
        return 0

    lax.fori_loop(0, count, run, 0)


def gelu_parts(value):
    slope = 0.7978845608028654
    square = value * value
    t = jnp.tanh(slope * (value + 0.044715 * (square * value)))
    cdf = 0.5 * (1.0 + t)
    derivative = cdf + 0.5 * value * (1.0 - t * t) * (slope * (1.0 + 3 * 0.044715 * square))
    return value * cdf, derivative


class Links:
    def __init__(self, send, recv):
        d = lax.axis_index("dp")
        m = lax.axis_index("mp")
        self.z, self.x, self.lo = d // 8, (d // 2) % 4, d % 2
        self.hi, self.core = m // 2, m % 2
        self.y = self.hi * 2 + self.lo
        self.send, self.recv = send, recv
        self.started = []

    def at(self, z=0, x=0, y=0, core=0):
        row = (self.y + y) % 4
        dp = (((self.z + z) % 4) * 4 + (self.x + x) % 4) * 2 + row % 2
        return dp, (row // 2) * 2 + (self.core + core) % 2

    def copy(self, src, dst, to):
        k = len(self.started)
        one = pltpu.make_async_remote_copy(
            src_ref=src,
            dst_ref=dst,
            send_sem=self.send.at[k],
            recv_sem=self.recv.at[k],
            device_id=to,
            device_id_type=MESH,
        )
        one.start()
        self.started.append(one)
        return one


class RingSum:
    def __init__(self, links, src, block, far_in, near_in, on, off):
        self.links, self.src, self.block = links, src, block
        self.far_in, self.near_in, self.on, self.off = far_in, near_in, on, off
        self.half = far_in.shape[1]

    def part(self, k, i):
        return self.near_in.at[k, pl.ds(i * self.half, self.half)]

    def start(self):
        copy, src, block = self.links.copy, self.src, self.block
        self.far = [
            copy(src.at[block(2, 0)], self.far_in.at[0], self.on),
            copy(src.at[block(2, 1)], self.far_in.at[1], self.off),
        ]
        self.near = [
            copy(src.at[block(1, 1)], self.part(0, 1), self.on),
            copy(src.at[block(3, 0)], self.part(1, 0), self.off),
        ]

    def middle(self):
        for i, k, to in ((0, 1, self.on), (1, 3, self.off)):
            self.far[i].wait_recv()
            at = self.block(k, i)
            self.src[at] = (self.src[at].astype(F32) + self.far_in[i].astype(F32)).astype(BF16)
            self.near.append(self.links.copy(self.src.at[at], self.part(i, i), to))

    def arrive(self):
        for one in self.near:
            one.wait_recv()

    def total(self, i, cols=slice(None)):
        rows = pl.ds(i * self.half, self.half)
        at = self.block(0, i)
        own = self.src[at] if cols == slice(None) else self.src[at[0], cols]
        return (
            own.astype(F32)
            + self.near_in[0, rows, cols].astype(F32)
            + self.near_in[1, rows, cols].astype(F32)
        )


def step_kernel(
    sharp, offset, caption, final, mapper, latent_in, second_in, entry_in, total_out, text_out, *scratch
):
    r = types.SimpleNamespace(**dict(zip(SCRATCH, scratch)))
    net = Links(r.send, r.recv)
    hi, core = net.hi, net.core
    copy = net.copy
    sibling = net.at(core=1)
    z_on, z_off = net.at(z=1), net.at(z=3)
    x_on, x_off = net.at(x=1), net.at(x=3)
    y_on, y_off = net.at(y=1), net.at(y=3)
    across = net.at(y=2)
    pair_lo = net.at(y=1 - 2 * net.lo + 4)
    beside = net.at(y=2 * net.lo + 3)
    quarter = hi * 2 + core

    def rows_of(h, c):
        return cut(((h % 2) * 2 + c % 2) * 128, 128, 128)

    def cols_of(h, c):
        return cut(((h % 2) * 2 + c % 2) * 256, 256, 256)

    barrier = pltpu.get_barrier_semaphore()
    partners = [sibling, z_on, z_off, net.at(z=2), x_on, x_off, net.at(x=2), y_on, y_off, across]
    partners.append(net.at(y=2, core=1))
    for one in partners:
        pl.semaphore_signal(barrier, inc=1, device_id=one, device_id_type=MESH)
    loads = [
        pltpu.make_async_copy(src, dst, r.load.at[k])
        for k, (src, dst) in enumerate(
            ((latent_in, r.latent), (second_in, r.second), (entry_in, r.entry))
        )
    ]
    for one in loads:
        one.start()

    r.columns[...] = nn(final[...], mapper[...]).astype(BF16)
    raw = caption[...].astype(F32)
    text_scale = lax.rsqrt(jnp.sum(raw * raw, axis=1, keepdims=True) + 1e-06)
    unit = raw * text_scale
    r.text_scale[...] = text_scale
    r.text_unit[...] = unit
    unit = unit.astype(BF16)
    r.texts[0:64, :] = unit[0:64]
    r.texts[256:320, :] = unit[64:128]
    r.mapper[:, cols_of(hi, core)] = mapper[...]
    r.embed[:, cols_of(hi, core)] = r.columns[rows_of(hi, core), :]
    pl.semaphore_wait(barrier, len(partners))

    def give(h, c, to):
        return copy(r.columns.at[rows_of(h, c)], r.embed.at[:, cols_of(hi, core)], to)

    embed_copies = [
        give(hi + 1, core, across),
        give(hi + 1, core + 1, net.at(y=2, core=1)),
        give(hi, core + 1, sibling),
    ]

    rings = (((y_on, y_off), (z_on, z_off)), ((z_on, z_off), (y_on, y_off)))

    def slot(half, s, p, part=None):
        start = s * 512 + half * 256 + p * 64
        return pl.ds(start, 64) if part is None else pl.ds(start + 32 * part, 32)

    got = {}

    def text_copy(half, src, dst, to, part=None):
        one = copy(r.texts.at[slot(half, *src, part)], r.texts.at[slot(half, *dst, part)], to)
        got.setdefault((half, dst), []).append(one)

    def arrived(half, s, p):
        for one in got[half, (s, p)]:
            one.wait_recv()

    def text_first(half):
        on, off = rings[half][0]
        text_copy(half, (0, 0), (0, 1), on)
        text_copy(half, (0, 0), (0, 3), off)

    def text_second(half, p):
        on, off = rings[half][1]
        text_copy(half, (0, p), (1, p), on)
        text_copy(half, (0, p), (3, p), off)

    def text_far_first(half):
        on, off = rings[half][0]
        text_copy(half, (0, 1), (0, 2), on, 0)
        text_copy(half, (0, 3), (0, 2), off, 1)

    def text_far_second(half, p):
        on, off = rings[half][1]
        text_copy(half, (1, p), (2, p), on, 0)
        text_copy(half, (3, p), (2, p), off, 1)

    halves = (0, 1)
    for half in halves:
        text_first(half)
    for half in halves:
        text_second(half, 0)

    for one in embed_copies:
        one.wait_recv()
    wide = r.embed[...].astype(F32)
    image_scale = lax.rsqrt(jnp.sum(wide * wide, axis=1, keepdims=True) + 1e-06)
    unit = wide * image_scale
    r.image_scale[...] = image_scale
    r.image_unit[...] = unit
    r.images[0:128, :] = unit.astype(BF16)

    def image_slot(s, part=None):
        return pl.ds(s * 128, 128) if part is None else pl.ds(s * 128 + 64 * part, 64)

    def image_copy(src, dst, to, part=None):
        return copy(r.images.at[image_slot(src, part)], r.images.at[image_slot(dst, part)], to)

    image_on = [image_copy(0, 1, x_on, 0), image_copy(0, 1, x_on, 1)]
    image_off = [image_copy(0, 3, x_off, 1), image_copy(0, 3, x_off, 0)]
    shared = [image_copy(0, 4, sibling)]

    for half in halves:
        arrived(half, 0, 1)
        arrived(half, 0, 3)
        text_far_first(half)
        text_second(half, 1)
        text_second(half, 3)
    for half in halves:
        arrived(half, 1, 0)
        arrived(half, 3, 0)
        text_far_second(half, 0)

    image_on[0].wait_recv()
    image_far = [image_copy(1, 2, x_on, 0)]
    image_off[0].wait_recv()
    image_far.append(image_copy(3, 2, x_off, 1))
    image_on[1].wait_recv()
    image_off[1].wait_recv()
    shared += [image_copy(1, 5, sibling), image_copy(3, 7, sibling)]

    for half in halves:
        arrived(half, 0, 2)
        text_second(half, 2)

    loads[0].wait()

    def activate(cols):
        value, derivative = gelu_parts(r.latent[:, cols].astype(F32))
        r.active[:, cols] = value.astype(BF16)
        r.slope[:, cols] = derivative

    loop(4, activate)

    for half in halves:
        for p in (1, 3):
            arrived(half, 1, p)
            arrived(half, 3, p)
            text_far_second(half, p)
    for one in image_far:
        one.wait_recv()
    shared.append(image_copy(2, 6, sibling))
    for one in shared:
        one.wait_recv()

    factor = sharp[0]
    shift = offset[0]

    def pair_weights(group):
        texts = pl.ds(group * 512, 512)

        def chunk(rows):
            logits = factor * nt(r.images[rows, :], r.texts[texts, :]) + shift
            r.weights[rows, texts] = (factor / (1.0 + jnp.exp(-logits))).astype(BF16)

        loop(4, chunk)
        if group == 0:
            for half in halves:
                rows = pl.ds(half * 64, 64)
                cols = pl.ds(half * 256, 128)
                logits = factor * nt(r.images[rows, :], r.texts[cols, :]) + shift
                hit = lax.broadcasted_iota(jnp.int32, (64, 128), 0) == lax.broadcasted_iota(
                    jnp.int32, (64, 128), 1
                )
                label = jnp.where(hit, 1.0, -1.0)
                w = -label * factor / (1.0 + jnp.exp(label * logits))
                r.weights[rows, cols] = w.astype(BF16)

    def image_part(group):
        texts = pl.ds(group * 512, 512)

        def chunk(cols):
            part = nn(r.weights[:, texts], r.texts[texts, cols])
            if group:
                part = part + r.image_dz[:, cols]
            r.image_dz[:, cols] = part

        loop(4, chunk)

    pair_weights(0)
    image_part(0)
    for half in halves:
        arrived(half, 1, 2)
        arrived(half, 3, 2)
        text_far_second(half, 2)
    own_columns = r.mapper.at[:, cols_of(hi, core)]
    map_copies = [copy(own_columns, own_columns, beside), copy(own_columns, own_columns, sibling)]
    for group in (1, 3):
        pair_weights(group)
        image_part(group)
    for half in halves:
        for p in range(4):
            arrived(half, 2, p)
    pair_weights(2)
    texts = pl.ds(1024, 512)

    def last_sibling(cols):
        part = nn(r.weights[512:1024, texts], r.texts[texts, cols])
        r.cross_out[:, cols] = (part + r.image_dz[512:1024, cols]).astype(BF16)

    def last_own(cols):
        part = nn(r.weights[0:512, texts], r.texts[texts, cols])
        r.image_dz[0:512, cols] = part + r.image_dz[0:512, cols]

    loop(4, last_sibling)
    cross = copy(r.cross_out, r.cross_in, sibling)
    loop(4, last_own)
    cross.wait_recv()

    def image_block(k, i):
        return image_slot((4 - k) % 4, i), slice(None)

    image_ring = RingSum(net, r.image_sum, image_block, r.image_far, r.image_near, x_on, x_off)

    def image_total(s):
        rows = image_slot(s)
        r.image_sum[rows, :] = (r.image_dz[rows, :] + r.cross_in[rows, :].astype(F32)).astype(BF16)

    for s in (2, 1, 3):
        image_total(s)
    image_ring.start()
    image_total(0)

    def text_grads(group):
        def chunk(j, _):
            rows = cut(group * 512 + j * 256, 256, 256)
            r.text_dz[rows, :] = tn(r.weights[:, rows], r.images[...]).astype(BF16)
            return 0

        lax.fori_loop(0, 2, chunk, 0)

    def second_ring(half):
        def block(k, i):
            return pl.ds(((4 - k) % 4) * 512 + half * 256 + 128 * i, 128), slice(None)

        on, off = rings[half][1]
        return RingSum(net, r.text_dz, block, r.text_far.at[half], r.text_near.at[half], on, off)

    def first_ring(half):
        def block(k, i):
            return pl.ds(half * 256 + ((4 - k) % 4) * 64 + 32 * i, 32), slice(None)

        on, off = rings[half][0]
        return RingSum(net, r.text_sum, block, r.last_far.at[half], r.last_near.at[half], on, off)

    seconds = [second_ring(half) for half in halves]
    firsts = [first_ring(half) for half in halves]

    text_grads(2)
    image_ring.middle()
    text_grads(1)
    text_grads(3)
    for one in seconds:
        one.start()
    image_ring.arrive()
    dz = jnp.concatenate([image_ring.total(0), image_ring.total(1)], axis=0)
    unit = r.image_unit[...]
    grad = r.image_scale[...] * (dz - unit * jnp.sum(unit * dz, axis=1, keepdims=True))
    mine = rows_of(hi, core)
    r.image_grad[mine, :] = grad.astype(BF16)
    block = r.image_grad.at[mine]
    spread = [copy(block, block, across), copy(block, block, sibling)]
    text_grads(0)

    map_copies[0].wait_recv()
    other_columns = r.mapper.at[:, cols_of(hi + 1, core)]
    map_copies.append(copy(other_columns, other_columns, sibling))
    spread[0].wait_recv()
    block = r.image_grad.at[rows_of(hi + 1, core)]
    spread.append(copy(block, block, sibling))
    for one in seconds:
        one.middle()
    spread[1].wait_recv()
    spread[2].wait_recv()
    map_copies[1].wait_recv()
    map_copies[2].wait_recv()

    def back_part(cols):
        r.back[:, cols] = nt(r.image_grad[...], r.mapper[cols, :]).astype(BF16)

    loop(4, back_part)

    def proj_part(cols):
        value = tn(final[:, cols], r.image_grad[:, cols_of(hi, core)]).astype(BF16)
        r.grads[1024:1152, cols] = value[0:128]
        r.grads[2176:2304, cols] = value[128:256]

    loop(4, proj_part)

    def down_part(j, _):
        cols = cut(j * 256, 256, 256)
        r.grads[cut(PART + j * 256, 256, 128), :] = tn(r.active[:, cols], r.back[...]).astype(BF16)
        return 0

    lax.fori_loop(0, 4, down_part, 0)

    first = (net.z, net.x)
    other = (net.x, net.z)
    along = ((z_on, z_off), (x_on, x_off))

    def strip_rows(part, k, i=None):
        start = part * PART + ((first[part] + k) % 4) * STRIP
        return cut(start, STRIP) if i is None else cut(start + i * TILE, TILE)

    def side_columns(part, k):
        return cut(((other[part] + k) % 4) * 256, 256, 256)

    def grad_ring(part):
        def block(k, i):
            return strip_rows(part, k, i), slice(None)

        return RingSum(net, r.grads, block, r.grad_far.at[part], r.grad_near.at[part], *along[part])

    grad_rings = [grad_ring(part) for part in (0, 1)]
    grad_rings[1].start()
    loads[1].wait()

    def pre_part(cols):
        r.pre[:, cols] = (nt(r.back[...], r.second[cols, :]) * r.slope[:, cols]).astype(BF16)

    loop(4, pre_part)
    loads[2].wait()

    def up_part(cols):
        r.grads[cols, :] = tn(r.entry[:, cols], r.pre[...]).astype(BF16)

    loop(4, up_part)
    grad_rings[0].start()

    for half in halves:
        seconds[half].arrive()
        for i in (0, 1):
            r.text_sum[pl.ds(half * 256 + 128 * i, 128), :] = seconds[half].total(i).astype(BF16)
        firsts[half].start()
    grad_rings[1].middle()
    grad_rings[0].middle()
    for half in halves:
        firsts[half].middle()

    def side_to(part, k):
        return net.at(x=k) if part == 0 else net.at(z=k)

    order = (1, 0)
    sides = {}
    for part in order:
        ring = grad_rings[part]
        ring.arrive()
        sides[part] = []
        for n, k in enumerate((2, 1, 3, 0)):
            cols = side_columns(part, k)
            for i in (0, 1):
                rows = pl.ds(i * TILE, TILE)
                total = ring.total(i, cols)
                if k == 0:
                    r.strip[part, rows, :] = total
                else:
                    r.side_out[part, n, rows, :] = total.astype(BF16)
            if k:
                sides[part].append(copy(r.side_out.at[part, n], r.side_in.at[part, n], side_to(part, k)))

    for half in halves:
        firsts[half].arrive()
    dz = jnp.concatenate([firsts[half].total(i) for half in halves for i in (0, 1)], axis=0)
    unit = r.text_unit[...]
    text_out[...] = r.text_scale[...] * (dz - unit * jnp.sum(unit * dz, axis=1, keepdims=True))

    kept = cut(net.lo * TILE, TILE)
    given = cut((1 - net.lo) * TILE, TILE)
    tiles = {}
    for part in order:
        for one in sides[part]:
            one.wait_recv()

        def total(rows):
            value = r.strip[part, rows, :]
            for n in range(3):
                value = value + r.side_in[part, n, rows, :].astype(F32)
            return value

        r.tile_out[part] = total(given).astype(BF16)
        tiles[part] = copy(r.tile_out.at[part], r.tile_in.at[part], pair_lo)
        r.tile[part] = total(kept)

    spread_tile = {}
    for part in order:
        tiles[part].wait_recv()
        rows = cut(part * PART + first[part] * STRIP + net.lo * TILE, TILE)
        cols = side_columns(part, 0)
        r.done[rows, cols] = (r.tile[part] + r.tile_in[part].astype(F32)).astype(BF16)
        block = r.done.at[rows, cols]
        spread_tile[part] = copy(block, block, pair_lo)
    spread_side = {}
    for part in order:
        spread_tile[part].wait_recv()
        block = r.done.at[strip_rows(part, 0), side_columns(part, 0)]
        spread_side[part] = [copy(block, block, side_to(part, k)) for k in (2, 1, 3)]
    spread_strip = {}
    for part in order:
        for one in spread_side[part]:
            one.wait_recv()
        on, off = along[part]
        spread_strip[part] = []
        for i, to in ((0, on), (1, off), (1, on), (0, off)):
            block = r.done.at[strip_rows(part, 0, i)]
            spread_strip[part].append(copy(block, block, to))
    last = []
    for part in order:
        on, off = along[part]
        for i, k, to in ((0, 3, on), (1, 1, off)):
            spread_strip[part][i].wait_recv()
            block = r.done.at[strip_rows(part, k, i)]
            last.append(copy(block, block, to))
    for part in order:
        for one in spread_strip[part][2:]:
            one.wait_recv()
    for one in last:
        one.wait_recv()
    out = pltpu.make_async_copy(r.done, total_out, r.load.at[3])
    out.start()
    for one in net.started:
        one.wait_send()
    out.wait()


SCRATCH = dict(
    columns=((512, 256), BF16),
    texts=((2048, 1024), BF16),
    text_unit=((128, 1024), F32),
    text_scale=((128, 1), F32),
    embed=((128, 1024), BF16),
    image_unit=((128, 1024), F32),
    image_scale=((128, 1), F32),
    images=((1024, 1024), BF16),
    mapper=((1024, 1024), BF16),
    latent=((512, 1024), BF16),
    second=((1024, 1024), BF16),
    entry=((512, 1024), BF16),
    active=((512, 1024), BF16),
    slope=((512, 1024), F32),
    weights=((1024, 2048), BF16),
    image_dz=((1024, 1024), F32),
    cross_out=((512, 1024), BF16),
    cross_in=((512, 1024), BF16),
    image_sum=((512, 1024), BF16),
    image_far=((2, 64, 1024), BF16),
    image_near=((2, 128, 1024), BF16),
    text_dz=((2048, 1024), BF16),
    text_far=((2, 2, 128, 1024), BF16),
    text_near=((2, 2, 256, 1024), BF16),
    text_sum=((512, 1024), BF16),
    last_far=((2, 2, 32, 1024), BF16),
    last_near=((2, 2, 64, 1024), BF16),
    image_grad=((512, 1024), BF16),
    back=((512, 1024), BF16),
    pre=((512, 1024), BF16),
    grads=((2 * PART, 1024), BF16),
    done=((2 * PART, 1024), BF16),
    grad_far=((2, 2, TILE, 1024), BF16),
    grad_near=((2, 2, STRIP, 1024), BF16),
    strip=((2, STRIP, 256), F32),
    side_out=((2, 3, STRIP, 256), BF16),
    side_in=((2, 3, STRIP, 256), BF16),
    tile=((2, TILE, 256), F32),
    tile_out=((2, TILE, 256), BF16),
    tile_in=((2, TILE, 256), BF16),
    send=((COPIES,), None),
    recv=((COPIES,), None),
    load=((4,), None),
)


def step(sharp, offset, caption, final, mapper, latent, second, entry):
    return pl.pallas_call(
        step_kernel,
        name="pairs_and_weight_grads",
        out_shape=(
            jax.ShapeDtypeStruct((2 * PART, 1024), BF16),
            jax.ShapeDtypeStruct((128, 1024), F32),
        ),
        in_specs=[SMEM, SMEM, VMEM, VMEM, VMEM, ANY, ANY, ANY],
        out_specs=(ANY, VMEM),
        scratch_shapes=[
            pltpu.SemaphoreType.DMA(shape) if kind is None else pltpu.VMEM(shape, kind)
            for shape, kind in SCRATCH.values()
        ],
        compiler_params=pltpu.CompilerParams(
            collective_id=0, has_side_effects=True, vmem_limit_bytes=60 * 2**20
        ),
    )(sharp, offset, caption, final, mapper, latent, second, entry)


def lion_block(weight, moment, grad, axis):
    grad = grad.astype(F32)
    moment = moment.astype(F32)
    blend = 0.9 * moment + 0.1 * grad
    square = blend * blend
    floor = 0.0625 * (jnp.mean(square, axis=axis, keepdims=True) + 1e-06)
    update = blend * lax.rsqrt(square + floor) + weight.astype(F32)
    return update.astype(BF16), (0.99 * moment + 0.01 * grad).astype(BF16)


def lion_kernel(
    g_up, g_down, g_proj_a, g_proj_b, w_up, w_down, w_proj, m_up, m_down, m_proj,
    u_up, u_down, u_proj, r_up, r_down, r_proj,
):
    u_up[...], r_up[...] = lion_block(w_up[...], m_up[...], g_up[...], 0)
    u_down[...], r_down[...] = lion_block(w_down[...], m_down[...], g_down[...], 1)

    @pl.when(pl.program_id(0) == 0)
    def _():
        grad = jnp.concatenate(
            [g[:, 256 * i : 256 * (i + 1)] for i in range(4) for g in (g_proj_a, g_proj_b)], axis=0
        )
        u_proj[...], r_proj[...] = lion_block(w_proj[...], m_proj[...], grad, 0)


def lion(total, weights, moments):
    column = pl.BlockSpec((1024, 128), lambda i: (0, i))
    row = pl.BlockSpec((128, 1024), lambda i: (i, 0))
    whole = pl.BlockSpec((1024, 256), lambda i: (0, 0))
    like = [column, row, whole]
    square = jax.ShapeDtypeStruct((1024, 1024), BF16)
    narrow = jax.ShapeDtypeStruct((1024, 256), BF16)
    return pl.pallas_call(
        lion_kernel,
        name="lion",
        grid=(8,),
        out_shape=(square, square, narrow, square, square, narrow),
        in_specs=[
            column,
            pl.BlockSpec((128, 1024), lambda i: (9 + i, 0)),
            pl.BlockSpec((128, 1024), lambda i: (8, 0)),
            pl.BlockSpec((128, 1024), lambda i: (17, 0)),
        ]
        + like
        + like,
        out_specs=tuple(like + like),
        compiler_params=pltpu.CompilerParams(vmem_limit_bytes=60 * 2**20),
    )(total, total, total, total, *weights, *moments)


def per_device(
    vision_layer_entry,
    latent_preact_values,
    final_layer_result,
    caption_vectors_raw,
    sharpness_factor,
    offset_term,
    first_feedforward_matrix,
    second_feedforward_matrix,
    mapper_matrix,
    first_matrix_velocity,
    second_matrix_velocity,
    mapper_velocity,
):
    total, text_grad = step(
        sharpness_factor,
        offset_term,
        caption_vectors_raw,
        final_layer_result,
        mapper_matrix,
        latent_preact_values,
        second_feedforward_matrix,
        vision_layer_entry,
    )
    results = lion(
        total,
        (first_feedforward_matrix, second_feedforward_matrix, mapper_matrix),
        (first_matrix_velocity, second_matrix_velocity, mapper_velocity),
    )
    return (*results, text_grad)


def solution(mesh):
    return jax.shard_map(
        per_device,
        mesh=mesh,
        in_specs=(
            P("dp", None),
            P("dp", "mp"),
            P("dp", None),
            P(("dp", "mp"), None),
            P(),
            P(),
            P(None, "mp"),
            P("mp", None),
            P(None, "mp"),
            P(None, "mp"),
            P("mp", None),
            P(None, "mp"),
        ),
        out_specs=(
            P(None, "mp"),
            P("mp", None),
            P(None, "mp"),
            P(None, "mp"),
            P("mp", None),
            P(None, "mp"),
            P(("dp", "mp"), None),
        ),
        check_vma=False,
    )
```

```python
import types

import jax
import jax.numpy as jnp
from jax import lax
from jax.experimental import pallas as pl
from jax.experimental.pallas import tpu as pltpu
from jax.sharding import PartitionSpec as P

MESH = pl.DeviceIdType.MESH
F32 = jnp.float32
BF16 = jnp.bfloat16
VMEM = pl.BlockSpec(memory_space=pltpu.VMEM)
SMEM = pl.BlockSpec(memory_space=pltpu.SMEM)
ANY = pl.BlockSpec(memory_space=pl.ANY)

PART = 1152
STRIP = 288
TILE = 144
COPIES = 176
PLACE = (0, 1, 3, 2)


def nn(a, b):
    return jnp.dot(a, b, preferred_element_type=F32)


def nt(a, b):
    return lax.dot_general(a, b, (((1,), (1,)), ((), ())), preferred_element_type=F32)


def tn(a, b):
    return lax.dot_general(a, b, (((0,), (0,)), ((), ())), preferred_element_type=F32)


def cut(start, size, unit=16):
    return pl.ds(start if isinstance(start, int) else pl.multiple_of(start, unit), size)


def loop(count, body, size=256):
    def run(j, _):
        body(cut(j * size, size, size))
        return 0

    lax.fori_loop(0, count, run, 0)


def gelu_parts(value):
    slope = 0.7978845608028654
    square = value * value
    t = jnp.tanh(slope * (value + 0.044715 * (square * value)))
    cdf = 0.5 * (1.0 + t)
    derivative = cdf + 0.5 * value * (1.0 - t * t) * (slope * (1.0 + 3 * 0.044715 * square))
    return value * cdf, derivative


class Links:
    def __init__(self, send, recv):
        d = lax.axis_index("dp")
        m = lax.axis_index("mp")
        self.z, self.x, self.lo = d // 8, (d // 2) % 4, d % 2
        self.hi, self.core = m // 2, m % 2
        self.y = self.hi * 2 + self.lo
        self.send, self.recv = send, recv
        self.started = []

    def at(self, z=0, x=0, y=0, core=0):
        row = (self.y + y) % 4
        dp = (((self.z + z) % 4) * 4 + (self.x + x) % 4) * 2 + row % 2
        return dp, (row // 2) * 2 + (self.core + core) % 2

    def copy(self, src, dst, to):
        k = len(self.started)
        one = pltpu.make_async_remote_copy(
            src_ref=src,
            dst_ref=dst,
            send_sem=self.send.at[k],
            recv_sem=self.recv.at[k],
            device_id=to,
            device_id_type=MESH,
        )
        one.start()
        self.started.append(one)
        return one


class RingSum:
    def __init__(self, links, src, block, far_in, near_in, on, off):
        self.links, self.src, self.block = links, src, block
        self.far_in, self.near_in, self.on, self.off = far_in, near_in, on, off
        self.half = far_in.shape[1]

    def part(self, k, i):
        return self.near_in.at[k, pl.ds(i * self.half, self.half)]

    def start(self):
        self.start_far()
        self.start_near()

    def start_far(self):
        copy, src, block = self.links.copy, self.src, self.block
        self.far = [
            copy(src.at[block(2, 0)], self.far_in.at[0], self.on),
            copy(src.at[block(2, 1)], self.far_in.at[1], self.off),
        ]

    def start_near(self):
        copy, src, block = self.links.copy, self.src, self.block
        self.near = [
            copy(src.at[block(1, 1)], self.part(0, 1), self.on),
            copy(src.at[block(3, 0)], self.part(1, 0), self.off),
        ]

    def middle(self):
        for i, k, to in ((0, 1, self.on), (1, 3, self.off)):
            self.far[i].wait_recv()
            at = self.block(k, i)
            self.src[at] = (self.src[at].astype(F32) + self.far_in[i].astype(F32)).astype(BF16)
            self.near.append(self.links.copy(self.src.at[at], self.part(i, i), to))

    def arrive(self):
        for one in self.near:
            one.wait_recv()

    def total(self, i, cols=None, near=slice(None)):
        rows = pl.ds(i * self.half, self.half)
        at = self.block(0, i)
        own = self.src[at] if cols is None else self.src[at[0], cols]
        return (
            own.astype(F32)
            + self.near_in[0, rows, near].astype(F32)
            + self.near_in[1, rows, near].astype(F32)
        )


def step_kernel(
    sharp, offset, caption, final, mapper, latent_in, second_in, entry_in, total_out, text_out, *scratch
):
    r = types.SimpleNamespace(**dict(zip(SCRATCH, scratch)))
    net = Links(r.send, r.recv)
    hi, core = net.hi, net.core
    copy = net.copy
    sibling = net.at(core=1)
    z_on, z_off = net.at(z=1), net.at(z=3)
    x_on, x_off = net.at(x=1), net.at(x=3)
    y_on, y_off = net.at(y=1), net.at(y=3)
    across = net.at(y=2)
    pair_lo = net.at(y=1 - 2 * net.lo + 4)
    beside = net.at(y=2 * net.lo + 3)
    quarter = hi * 2 + core

    def rows_of(h, c):
        return cut(((h % 2) * 2 + c % 2) * 128, 128, 128)

    def cols_of(h, c):
        return cut(((h % 2) * 2 + c % 2) * 256, 256, 256)

    barrier = pltpu.get_barrier_semaphore()
    partners = [sibling, z_on, z_off, net.at(z=2), x_on, x_off, net.at(x=2), y_on, y_off, across]
    partners.append(net.at(y=2, core=1))
    for one in partners:
        pl.semaphore_signal(barrier, inc=1, device_id=one, device_id_type=MESH)
    loads = [
        pltpu.make_async_copy(src, dst, r.load.at[k])
        for k, (src, dst) in enumerate(
            ((latent_in, r.latent), (second_in, r.second), (entry_in, r.entry))
        )
    ]
    for one in loads:
        one.start()

    r.columns[...] = nn(final[...], mapper[...]).astype(BF16)
    raw = caption[...].astype(F32)
    text_scale = lax.rsqrt(jnp.sum(raw * raw, axis=1, keepdims=True) + 1e-06)
    unit = raw * text_scale
    r.text_scale[...] = text_scale
    r.text_unit[...] = unit
    unit = unit.astype(BF16)
    r.texts[0:64, :] = unit[0:64]
    r.texts[256:320, :] = unit[64:128]
    r.mapper[:, cols_of(hi, core)] = mapper[...]
    r.embed[:, cols_of(hi, core)] = r.columns[rows_of(hi, core), :]
    pl.semaphore_wait(barrier, len(partners))

    def give(h, c, to):
        return copy(r.columns.at[rows_of(h, c)], r.embed.at[:, cols_of(hi, core)], to)

    embed_copies = [
        give(hi + 1, core, across),
        give(hi + 1, core + 1, net.at(y=2, core=1)),
        give(hi, core + 1, sibling),
    ]

    rings = (((y_on, y_off), (z_on, z_off)), ((z_on, z_off), (y_on, y_off)))

    def slot(half, s, p, part=None):
        start = PLACE[s] * 512 + half * 256 + p * 64
        return pl.ds(start, 64) if part is None else pl.ds(start + 32 * part, 32)

    got = {}

    def text_copy(half, src, dst, to, part=None):
        one = copy(r.texts.at[slot(half, *src, part)], r.texts.at[slot(half, *dst, part)], to)
        got.setdefault((half, dst), []).append(one)

    def arrived(half, s, p):
        for one in got[half, (s, p)]:
            one.wait_recv()

    def text_first(half):
        on, off = rings[half][0]
        text_copy(half, (0, 0), (0, 1), on)
        text_copy(half, (0, 0), (0, 3), off)

    def text_second(half, p):
        on, off = rings[half][1]
        text_copy(half, (0, p), (1, p), on)
        text_copy(half, (0, p), (3, p), off)

    def text_far_first(half):
        on, off = rings[half][0]
        text_copy(half, (0, 1), (0, 2), on, 0)
        text_copy(half, (0, 3), (0, 2), off, 1)

    def text_far_second(half, p):
        on, off = rings[half][1]
        text_copy(half, (1, p), (2, p), on, 0)
        text_copy(half, (3, p), (2, p), off, 1)

    halves = (0, 1)
    text_first(1)
    text_second(0, 0)

    for one in embed_copies:
        one.wait_recv()
    wide = r.embed[...].astype(F32)
    image_scale = lax.rsqrt(jnp.sum(wide * wide, axis=1, keepdims=True) + 1e-06)
    unit = wide * image_scale
    r.images[0:128, :] = unit.astype(BF16)

    def image_slot(s, part=None):
        return pl.ds(s * 128, 128) if part is None else pl.ds(s * 128 + 64 * part, 64)

    def image_copy(src, dst, to, part=None):
        return copy(r.images.at[image_slot(src, part)], r.images.at[image_slot(dst, part)], to)

    image_on = [image_copy(0, 1, x_on, 0)]
    image_off = [image_copy(0, 3, x_off, 1)]
    image_on.append(image_copy(0, 1, x_on, 1))
    image_off.append(image_copy(0, 3, x_off, 0))
    text_first(0)
    text_second(1, 0)
    shared = [image_copy(0, 4, sibling)]
    r.image_scale[...] = image_scale
    r.image_unit[...] = unit

    for half in (1, 0):
        arrived(half, 0, 1)
        arrived(half, 0, 3)
        text_far_first(half)
        text_second(half, 1)
        text_second(half, 3)
        if half == 1:
            image_on[0].wait_recv()
            image_far = [image_copy(1, 2, x_on, 0)]
            image_off[0].wait_recv()
            image_far.append(image_copy(3, 2, x_off, 1))

    for half in (0, 1):
        arrived(half, 1, 0)
        arrived(half, 3, 0)
        text_far_second(half, 0)
    image_on[1].wait_recv()
    image_off[1].wait_recv()
    shared += [image_copy(1, 5, sibling), image_copy(3, 7, sibling)]
    for half in (1, 0):
        arrived(half, 0, 2)
        text_second(half, 2)
    for one in image_far:
        one.wait_recv()
    shared.append(image_copy(2, 6, sibling))

    for one in shared:
        one.wait_recv()

    factor = sharp[0]
    shift = offset[0]

    def pair_weights(s, first=0, count=1024):
        texts = pl.ds(PLACE[s] * 512, 512)

        def chunk(rows):
            logits = factor * nt(r.images[rows, :], r.texts[texts, :]) + shift
            r.weights[rows, texts] = (factor / (1.0 + jnp.exp(-logits))).astype(BF16)

        def run(j, _):
            chunk(cut(first + j * 512, 512, 512))
            return 0

        if count == 512:
            chunk(pl.ds(first, 512))
        else:
            lax.fori_loop(0, 2, run, 0)

    def matching_pairs():
        for half in halves:
            rows = pl.ds(half * 64, 64)
            cols = pl.ds(half * 256, 128)
            logits = factor * nt(r.images[rows, :], r.texts[cols, :]) + shift
            hit = lax.broadcasted_iota(jnp.int32, (64, 128), 0) == lax.broadcasted_iota(
                jnp.int32, (64, 128), 1
            )
            label = jnp.where(hit, 1.0, -1.0)
            w = -label * factor / (1.0 + jnp.exp(label * logits))
            r.weights[rows, cols] = w.astype(BF16)

    near_texts = pl.ds(0, 1536)
    far_texts = pl.ds(1536, 512)

    def image_part(cols):
        r.image_dz[:, cols] = nn(r.weights[:, near_texts], r.texts[near_texts, cols])

    pair_weights(0)
    matching_pairs()
    for p in (1, 3):
        for half in halves:
            arrived(half, 1, p)
            arrived(half, 3, p)
            text_far_second(half, p)
    loads[0].wait()

    def activate(cols):
        value, derivative = gelu_parts(r.latent[:, cols].astype(F32))
        r.active[:, cols] = value.astype(BF16)
        r.slope[:, cols] = derivative

    loop(4, activate)
    for half in halves:
        arrived(half, 1, 2)
        arrived(half, 3, 2)
        text_far_second(half, 2)
    pair_weights(1)
    pair_weights(3)
    own_columns = r.mapper.at[:, cols_of(hi, core)]
    map_copies = [copy(own_columns, own_columns, beside), copy(own_columns, own_columns, sibling)]
    loop(4, image_part)
    for p in range(4):
        for half in halves:
            arrived(half, 2, p)

    def last_sibling(cols):
        part = nn(r.weights[512:1024, far_texts], r.texts[far_texts, cols])
        r.cross_out[:, cols] = (part + r.image_dz[512:1024, cols]).astype(BF16)

    def last_own(cols):
        part = nn(r.weights[0:512, far_texts], r.texts[far_texts, cols])
        r.image_dz[0:512, cols] = part + r.image_dz[0:512, cols]

    pair_weights(2, 512, 512)
    loop(2, last_sibling, 512)
    cross = copy(r.cross_out, r.cross_in, sibling)
    pair_weights(2, 0, 512)
    loop(2, last_own, 512)
    cross.wait_recv()

    def image_block(k, i):
        return image_slot((4 - k) % 4, i), slice(None)

    image_ring = RingSum(net, r.image_sum, image_block, r.image_far, r.image_near, x_on, x_off)

    def image_total(s):
        rows = image_slot(s)
        r.image_sum[rows, :] = (r.image_dz[rows, :] + r.cross_in[rows, :].astype(F32)).astype(BF16)

    image_total(2)
    image_ring.start_far()
    image_total(1)
    image_total(3)
    image_ring.start_near()
    image_total(0)

    def text_grads(half, *groups):
        for s in groups:
            rows = pl.ds(PLACE[s] * 512 + half * 256, 256)
            r.text_dz[rows, :] = tn(r.weights[:, rows], r.images[...]).astype(BF16)

    def second_ring(half):
        def block(k, i):
            return pl.ds(PLACE[(4 - k) % 4] * 512 + half * 256 + 128 * i, 128), slice(None)

        on, off = rings[half][1]
        return RingSum(net, r.text_dz, block, r.text_far.at[half], r.text_near.at[half], on, off)

    def first_ring(half):
        def block(k, i):
            return pl.ds(half * 256 + ((4 - k) % 4) * 64 + 32 * i, 32), slice(None)

        on, off = rings[half][0]
        return RingSum(net, r.text_sum, block, r.last_far.at[half], r.last_near.at[half], on, off)

    seconds = [second_ring(half) for half in halves]
    firsts = [first_ring(half) for half in halves]

    text_grads(0, 2, 1, 3)
    seconds[0].start()
    text_grads(1, 2)
    image_ring.middle()
    text_grads(1, 1, 3)
    text_grads(0, 0)
    image_ring.arrive()
    dz = jnp.concatenate([image_ring.total(0), image_ring.total(1)], axis=0)
    unit = r.image_unit[...]
    grad = r.image_scale[...] * (dz - unit * jnp.sum(unit * dz, axis=1, keepdims=True))
    mine = rows_of(hi, core)
    r.image_grad[mine, :] = grad.astype(BF16)
    block = r.image_grad.at[mine]
    spread = [copy(block, block, across), copy(block, block, sibling)]
    text_grads(1, 0)

    map_copies[0].wait_recv()
    other_columns = r.mapper.at[:, cols_of(hi + 1, core)]
    map_copies.append(copy(other_columns, other_columns, sibling))
    seconds[0].middle()
    map_copies[1].wait_recv()
    map_copies[2].wait_recv()
    spread[1].wait_recv()

    def back_rows(h):
        rows = cut((h % 2) * 256, 256, 256)

        def part(cols):
            r.back[rows, cols] = nt(r.image_grad[rows, :], r.mapper[cols, :]).astype(BF16)

        loop(2, part, 512)

    back_rows(hi)
    spread[0].wait_recv()
    block = r.image_grad.at[rows_of(hi + 1, core)]
    spread.append(copy(block, block, sibling))
    seconds[1].start()
    spread[2].wait_recv()
    back_rows(hi + 1)

    first = (net.z, net.x)
    other = (net.x, net.z)
    along = ((z_on, z_off), (x_on, x_off))
    wide = (pl.ds(0, 512), pl.ds(512, 512))

    def strip_rows(part, k, i=None):
        start = part * PART + ((first[part] + k) % 4) * STRIP
        return cut(start, STRIP) if i is None else cut(start + i * TILE, TILE)

    def side_columns(part, c, k):
        return cut(c * 512 + ((other[part] + k) % 4) * 128, 128, 128)

    def grad_ring(part, c):
        def block(k, i):
            return strip_rows(part, k, i), wide[c]

        n = part * 2 + c
        return RingSum(net, r.grads, block, r.grad_far.at[n], r.grad_near.at[n], *along[part])

    chains = ((1, 0), (1, 1), (0, 0), (0, 1))
    grad_rings = {chain: grad_ring(*chain) for chain in chains}

    def proj_part(cols):
        value = tn(final[:, cols], r.image_grad[:, cols_of(hi, core)]).astype(BF16)
        r.grads[1024:1152, cols] = value[0:128]
        r.grads[2176:2304, cols] = value[128:256]

    def down(c):
        def part(j, _):
            cols = cut(j * 512, 512, 512)
            value = tn(r.active[:, cols], r.back[:, wide[c]])
            r.grads[cut(PART + j * 512, 512, 128), wide[c]] = value.astype(BF16)
            return 0

        lax.fori_loop(0, 2, part, 0)

    def up(c):
        value = nt(r.back[...], r.second[wide[c], :]) * r.slope[:, wide[c]]
        r.pre[:, wide[c]] = value.astype(BF16)

        def part(rows):
            r.grads[rows, wide[c]] = tn(r.entry[:, rows], r.pre[:, wide[c]]).astype(BF16)

        loop(2, part, 512)

    loop(4, proj_part)
    down(0)
    grad_rings[1, 0].start()
    loads[1].wait()
    loads[2].wait()
    up(0)
    grad_rings[0, 0].start()
    down(1)
    grad_rings[1, 0].middle()
    grad_rings[1, 1].start()
    up(1)
    grad_rings[0, 0].middle()
    grad_rings[0, 1].start()

    def text_first_sum(half):
        seconds[half].arrive()
        for i in (0, 1):
            r.text_sum[pl.ds(half * 256 + 128 * i, 128), :] = seconds[half].total(i).astype(BF16)
        firsts[half].start()

    seconds[1].middle()
    text_first_sum(0)

    def side_to(part, k):
        return net.at(x=k) if part == 0 else net.at(z=k)

    sides = {}

    def side(part, c):
        ring = grad_rings[part, c]
        ring.arrive()
        sides[part, c] = []
        for n, k in enumerate((2, 1, 3, 0)):
            cols = side_columns(part, c, k)
            near = cut(((other[part] + k) % 4) * 128, 128, 128)
            for i in (0, 1):
                rows = pl.ds(i * TILE, TILE)
                total = ring.total(i, cols, near)
                if k == 0:
                    r.strip[part, rows, wide_tile[c]] = total
                else:
                    r.side_out[part, n, rows, wide_tile[c]] = total.astype(BF16)
            if k:
                sides[part, c].append(
                    copy(
                        r.side_out.at[part, n, :, wide_tile[c]],
                        r.side_in.at[part, n, :, wide_tile[c]],
                        side_to(part, k),
                    )
                )

    wide_tile = (pl.ds(0, 128), pl.ds(128, 128))
    side(1, 0)
    grad_rings[1, 1].middle()
    firsts[0].middle()
    side(0, 0)
    grad_rings[0, 1].middle()

    kept = cut(net.lo * TILE, TILE)
    given = cut((1 - net.lo) * TILE, TILE)
    tiles = {}

    def tile(part, c):
        for one in sides[part, c]:
            one.wait_recv()
        at = wide_tile[c]

        def total(rows):
            value = r.strip[part, rows, at]
            for n in range(3):
                value = value + r.side_in[part, n, rows, at].astype(F32)
            return value

        r.tile_out[part, :, at] = total(given).astype(BF16)
        tiles[part, c] = copy(r.tile_out.at[part, :, at], r.tile_in.at[part, :, at], pair_lo)
        r.tile[part, :, at] = total(kept)

    spread_tile = {}

    def back_tile(part, c):
        tiles[part, c].wait_recv()
        at = wide_tile[c]
        rows = cut(part * PART + first[part] * STRIP + net.lo * TILE, TILE)
        cols = side_columns(part, c, 0)
        r.done[rows, cols] = (r.tile[part, :, at] + r.tile_in[part, :, at].astype(F32)).astype(BF16)
        block = r.done.at[rows, cols]
        spread_tile[part, c] = copy(block, block, pair_lo)

    spread_side = {}

    def back_side(part, c):
        spread_tile[part, c].wait_recv()
        block = r.done.at[strip_rows(part, 0), side_columns(part, c, 0)]
        spread_side[part, c] = [copy(block, block, side_to(part, k)) for k in (2, 1, 3)]

    spread_strip = {}

    def back_strip(part, c):
        for one in spread_side[part, c]:
            one.wait_recv()
        on, off = along[part]
        spread_strip[part, c] = []
        for i, to in ((0, on), (1, off), (1, on), (0, off)):
            block = r.done.at[strip_rows(part, 0, i), wide[c]]
            spread_strip[part, c].append(copy(block, block, to))

    last = []

    def back_far(part, c):
        on, off = along[part]
        for i, k, to in ((0, 3, on), (1, 1, off)):
            spread_strip[part, c][i].wait_recv()
            block = r.done.at[strip_rows(part, k, i), wide[c]]
            last.append(copy(block, block, to))

    tile(1, 0)
    side(1, 1)
    tile(0, 0)
    side(0, 1)
    back_tile(1, 0)
    back_tile(0, 0)
    tile(1, 1)
    back_side(1, 0)
    tile(0, 1)
    back_side(0, 0)
    back_tile(1, 1)
    back_tile(0, 1)
    back_strip(1, 0)
    back_side(1, 1)
    back_strip(0, 0)
    back_side(0, 1)
    text_first_sum(1)
    back_far(1, 0)
    back_far(0, 0)
    back_strip(1, 1)
    back_strip(0, 1)
    firsts[1].middle()

    for half in halves:
        firsts[half].arrive()
    dz = jnp.concatenate([firsts[half].total(i) for half in halves for i in (0, 1)], axis=0)
    unit = r.text_unit[...]
    text_out[...] = r.text_scale[...] * (dz - unit * jnp.sum(unit * dz, axis=1, keepdims=True))

    back_far(1, 1)
    back_far(0, 1)
    for chain in chains:
        for one in spread_strip[chain][2:]:
            one.wait_recv()
    for one in last:
        one.wait_recv()
    out = pltpu.make_async_copy(r.done, total_out, r.load.at[3])
    out.start()
    for one in net.started:
        one.wait_send()
    out.wait()


SCRATCH = dict(
    columns=((512, 256), BF16),
    texts=((2048, 1024), BF16),
    text_unit=((128, 1024), F32),
    text_scale=((128, 1), F32),
    embed=((128, 1024), BF16),
    image_unit=((128, 1024), F32),
    image_scale=((128, 1), F32),
    images=((1024, 1024), BF16),
    mapper=((1024, 1024), BF16),
    latent=((512, 1024), BF16),
    second=((1024, 1024), BF16),
    entry=((512, 1024), BF16),
    active=((512, 1024), BF16),
    slope=((512, 1024), F32),
    weights=((1024, 2048), BF16),
    image_dz=((1024, 1024), F32),
    cross_out=((512, 1024), BF16),
    cross_in=((512, 1024), BF16),
    image_sum=((512, 1024), BF16),
    image_far=((2, 64, 1024), BF16),
    image_near=((2, 128, 1024), BF16),
    text_dz=((2048, 1024), BF16),
    text_far=((2, 2, 128, 1024), BF16),
    text_near=((2, 2, 256, 1024), BF16),
    text_sum=((512, 1024), BF16),
    last_far=((2, 2, 32, 1024), BF16),
    last_near=((2, 2, 64, 1024), BF16),
    image_grad=((512, 1024), BF16),
    back=((512, 1024), BF16),
    pre=((512, 1024), BF16),
    grads=((2 * PART, 1024), BF16),
    done=((2 * PART, 1024), BF16),
    grad_far=((4, 2, TILE, 512), BF16),
    grad_near=((4, 2, STRIP, 512), BF16),
    strip=((2, STRIP, 256), F32),
    side_out=((2, 3, STRIP, 256), BF16),
    side_in=((2, 3, STRIP, 256), BF16),
    tile=((2, TILE, 256), F32),
    tile_out=((2, TILE, 256), BF16),
    tile_in=((2, TILE, 256), BF16),
    send=((COPIES,), None),
    recv=((COPIES,), None),
    load=((4,), None),
)


def step(sharp, offset, caption, final, mapper, latent, second, entry):
    return pl.pallas_call(
        step_kernel,
        name="pairs_and_weight_grads",
        out_shape=(
            jax.ShapeDtypeStruct((2 * PART, 1024), BF16),
            jax.ShapeDtypeStruct((128, 1024), F32),
        ),
        in_specs=[SMEM, SMEM, VMEM, VMEM, VMEM, ANY, ANY, ANY],
        out_specs=(ANY, VMEM),
        scratch_shapes=[
            pltpu.SemaphoreType.DMA(shape) if kind is None else pltpu.VMEM(shape, kind)
            for shape, kind in SCRATCH.values()
        ],
        compiler_params=pltpu.CompilerParams(
            collective_id=0, has_side_effects=True, vmem_limit_bytes=60 * 2**20
        ),
    )(sharp, offset, caption, final, mapper, latent, second, entry)


def lion_block(weight, moment, grad, axis):
    grad = grad.astype(F32)
    moment = moment.astype(F32)
    blend = 0.9 * moment + 0.1 * grad
    square = blend * blend
    floor = 0.0625 * (jnp.mean(square, axis=axis, keepdims=True) + 1e-06)
    update = blend * lax.rsqrt(square + floor) + weight.astype(F32)
    return update.astype(BF16), (0.99 * moment + 0.01 * grad).astype(BF16)


def lion_kernel(
    g_up, g_down, g_proj_a, g_proj_b, w_up, w_down, w_proj, m_up, m_down, m_proj,
    u_up, u_down, u_proj, r_up, r_down, r_proj,
):
    u_up[...], r_up[...] = lion_block(w_up[...], m_up[...], g_up[...], 0)
    u_down[...], r_down[...] = lion_block(w_down[...], m_down[...], g_down[...], 1)

    @pl.when(pl.program_id(0) == 0)
    def _():
        grad = jnp.concatenate(
            [g[:, 256 * i : 256 * (i + 1)] for i in range(4) for g in (g_proj_a, g_proj_b)], axis=0
        )
        u_proj[...], r_proj[...] = lion_block(w_proj[...], m_proj[...], grad, 0)


def lion(total, weights, moments):
    column = pl.BlockSpec((1024, 128), lambda i: (0, i))
    row = pl.BlockSpec((128, 1024), lambda i: (i, 0))
    whole = pl.BlockSpec((1024, 256), lambda i: (0, 0))
    like = [column, row, whole]
    square = jax.ShapeDtypeStruct((1024, 1024), BF16)
    narrow = jax.ShapeDtypeStruct((1024, 256), BF16)
    return pl.pallas_call(
        lion_kernel,
        name="lion",
        grid=(8,),
        out_shape=(square, square, narrow, square, square, narrow),
        in_specs=[
            column,
            pl.BlockSpec((128, 1024), lambda i: (9 + i, 0)),
            pl.BlockSpec((128, 1024), lambda i: (8, 0)),
            pl.BlockSpec((128, 1024), lambda i: (17, 0)),
        ]
        + like
        + like,
        out_specs=tuple(like + like),
        compiler_params=pltpu.CompilerParams(vmem_limit_bytes=60 * 2**20),
    )(total, total, total, total, *weights, *moments)


def per_device(
    vision_layer_entry,
    latent_preact_values,
    final_layer_result,
    caption_vectors_raw,
    sharpness_factor,
    offset_term,
    first_feedforward_matrix,
    second_feedforward_matrix,
    mapper_matrix,
    first_matrix_velocity,
    second_matrix_velocity,
    mapper_velocity,
):
    total, text_grad = step(
        sharpness_factor,
        offset_term,
        caption_vectors_raw,
        final_layer_result,
        mapper_matrix,
        latent_preact_values,
        second_feedforward_matrix,
        vision_layer_entry,
    )
    results = lion(
        total,
        (first_feedforward_matrix, second_feedforward_matrix, mapper_matrix),
        (first_matrix_velocity, second_matrix_velocity, mapper_velocity),
    )
    return (*results, text_grad)


def solution(mesh):
    return jax.shard_map(
        per_device,
        mesh=mesh,
        in_specs=(
            P("dp", None),
            P("dp", "mp"),
            P("dp", None),
            P(("dp", "mp"), None),
            P(),
            P(),
            P(None, "mp"),
            P("mp", None),
            P(None, "mp"),
            P(None, "mp"),
            P("mp", None),
            P(None, "mp"),
        ),
        out_specs=(
            P(None, "mp"),
            P("mp", None),
            P(None, "mp"),
            P(None, "mp"),
            P("mp", None),
            P(None, "mp"),
            P(("dp", "mp"), None),
        ),
        check_vma=False,
    )
```

```python
import types

import jax
import jax.numpy as jnp
from jax import lax
from jax.experimental import pallas as pl
from jax.experimental.pallas import tpu as pltpu
from jax.sharding import PartitionSpec as P

MESH = pl.DeviceIdType.MESH
F32 = jnp.float32
BF16 = jnp.bfloat16
VMEM = pl.BlockSpec(memory_space=pltpu.VMEM)
SMEM = pl.BlockSpec(memory_space=pltpu.SMEM)
ANY = pl.BlockSpec(memory_space=pl.ANY)

PART = 1152
STRIP = 288
TILE = 144
COPIES = 176
PLACE = (0, 1, 3, 2)


def nn(a, b):
    return jnp.dot(a, b, preferred_element_type=F32)


def nt(a, b):
    return lax.dot_general(a, b, (((1,), (1,)), ((), ())), preferred_element_type=F32)


def tn(a, b):
    return lax.dot_general(a, b, (((0,), (0,)), ((), ())), preferred_element_type=F32)


def cut(start, size, unit=16):
    return pl.ds(start if isinstance(start, int) else pl.multiple_of(start, unit), size)


def loop(count, body, size=256):
    def run(j, _):
        body(cut(j * size, size, size))
        return 0

    lax.fori_loop(0, count, run, 0)


def gelu_parts(value):
    slope = 0.7978845608028654
    square = value * value
    t = jnp.tanh(slope * (value + 0.044715 * (square * value)))
    cdf = 0.5 * (1.0 + t)
    derivative = cdf + 0.5 * value * (1.0 - t * t) * (slope * (1.0 + 3 * 0.044715 * square))
    return value * cdf, derivative


class Links:
    def __init__(self, send, recv):
        d = lax.axis_index("dp")
        m = lax.axis_index("mp")
        self.z, self.x, self.lo = d // 8, (d // 2) % 4, d % 2
        self.hi, self.core = m // 2, m % 2
        self.y = self.hi * 2 + self.lo
        self.send, self.recv = send, recv
        self.started = []

    def at(self, z=0, x=0, y=0, core=0):
        row = (self.y + y) % 4
        dp = (((self.z + z) % 4) * 4 + (self.x + x) % 4) * 2 + row % 2
        return dp, (row // 2) * 2 + (self.core + core) % 2

    def copy(self, src, dst, to):
        k = len(self.started)
        one = pltpu.make_async_remote_copy(
            src_ref=src,
            dst_ref=dst,
            send_sem=self.send.at[k],
            recv_sem=self.recv.at[k],
            device_id=to,
            device_id_type=MESH,
        )
        one.start()
        self.started.append(one)
        return one


class RingSum:
    def __init__(self, links, src, block, far_in, near_in, on, off):
        self.links, self.src, self.block = links, src, block
        self.far_in, self.near_in, self.on, self.off = far_in, near_in, on, off
        self.half = far_in.shape[1]

    def part(self, k, i):
        return self.near_in.at[k, pl.ds(i * self.half, self.half)]

    def start(self):
        self.start_far()
        self.start_near()

    def start_far(self):
        copy, src, block = self.links.copy, self.src, self.block
        self.far = [
            copy(src.at[block(2, 0)], self.far_in.at[0], self.on),
            copy(src.at[block(2, 1)], self.far_in.at[1], self.off),
        ]

    def start_near(self):
        copy, src, block = self.links.copy, self.src, self.block
        self.near = [
            copy(src.at[block(1, 1)], self.part(0, 1), self.on),
            copy(src.at[block(3, 0)], self.part(1, 0), self.off),
        ]

    def middle(self):
        for i, k, to in ((0, 1, self.on), (1, 3, self.off)):
            self.far[i].wait_recv()
            at = self.block(k, i)
            self.src[at] = (self.src[at].astype(F32) + self.far_in[i].astype(F32)).astype(BF16)
            self.near.append(self.links.copy(self.src.at[at], self.part(i, i), to))

    def arrive(self):
        for one in self.near:
            one.wait_recv()

    def total(self, i, cols=None, near=slice(None)):
        rows = pl.ds(i * self.half, self.half)
        at = self.block(0, i)
        own = self.src[at] if cols is None else self.src[at[0], cols]
        return (
            own.astype(F32)
            + self.near_in[0, rows, near].astype(F32)
            + self.near_in[1, rows, near].astype(F32)
        )


def step_kernel(
    sharp,
    offset,
    caption_in,
    final_in,
    mapper_in,
    latent_in,
    second_in,
    entry_in,
    total_out,
    text_out,
    *scratch,
):
    r = types.SimpleNamespace(**dict(zip(SCRATCH, scratch)))
    caption, final, mapper = r.caption, r.final, r.own_mapper
    early = [
        pltpu.make_async_copy(src, dst, r.load.at[7 + k])
        for k, (src, dst) in enumerate(((caption_in, caption), (mapper_in, mapper), (final_in, final)))
    ]
    for one in early:
        one.start()
    net = Links(r.send, r.recv)
    hi, core = net.hi, net.core
    copy = net.copy
    sibling = net.at(core=1)
    z_on, z_off = net.at(z=1), net.at(z=3)
    x_on, x_off = net.at(x=1), net.at(x=3)
    y_on, y_off = net.at(y=1), net.at(y=3)
    across = net.at(y=2)
    pair_lo = net.at(y=1 - 2 * net.lo + 4)
    beside = net.at(y=2 * net.lo + 3)
    quarter = hi * 2 + core

    def rows_of(h, c):
        return cut(((h % 2) * 2 + c % 2) * 128, 128, 128)

    def cols_of(h, c):
        return cut(((h % 2) * 2 + c % 2) * 256, 256, 256)

    barrier = pltpu.get_barrier_semaphore()
    partners = [sibling, z_on, z_off, net.at(z=2), x_on, x_off, net.at(x=2), y_on, y_off, across]
    partners.append(net.at(y=2, core=1))
    for one in partners:
        pl.semaphore_signal(barrier, inc=1, device_id=one, device_id_type=MESH)
    loads = [
        pltpu.make_async_copy(src, dst, r.load.at[k])
        for k, (src, dst) in enumerate(
            ((latent_in, r.latent), (second_in, r.second), (entry_in, r.entry))
        )
    ]
    for one in loads:
        one.start()

    early[0].wait()
    raw = caption[...].astype(F32)
    text_scale = lax.rsqrt(jnp.sum(raw * raw, axis=1, keepdims=True) + 1e-06)
    unit = raw * text_scale
    r.text_scale[...] = text_scale
    r.text_unit[...] = unit
    unit = unit.astype(BF16)
    r.texts[0:64, :] = unit[0:64]
    r.texts[256:320, :] = unit[64:128]
    early[1].wait()
    r.mapper[:, cols_of(hi, core)] = mapper[...]
    early[2].wait()
    r.columns[...] = nn(final[...], mapper[...]).astype(BF16)
    r.embed[:, cols_of(hi, core)] = r.columns[rows_of(hi, core), :]
    pl.semaphore_wait(barrier, len(partners))

    def give(h, c, to):
        return copy(r.columns.at[rows_of(h, c)], r.embed.at[:, cols_of(hi, core)], to)

    embed_copies = [
        give(hi + 1, core, across),
        give(hi + 1, core + 1, net.at(y=2, core=1)),
        give(hi, core + 1, sibling),
    ]

    rings = (((y_on, y_off), (z_on, z_off)), ((z_on, z_off), (y_on, y_off)))

    def slot(half, s, p, part=None):
        start = PLACE[s] * 512 + half * 256 + p * 64
        return pl.ds(start, 64) if part is None else pl.ds(start + 32 * part, 32)

    got = {}

    def text_copy(half, src, dst, to, part=None):
        one = copy(r.texts.at[slot(half, *src, part)], r.texts.at[slot(half, *dst, part)], to)
        got.setdefault((half, dst), []).append(one)

    def arrived(half, s, p):
        for one in got[half, (s, p)]:
            one.wait_recv()

    def text_first(half):
        on, off = rings[half][0]
        text_copy(half, (0, 0), (0, 1), on)
        text_copy(half, (0, 0), (0, 3), off)

    def text_second(half, p):
        on, off = rings[half][1]
        text_copy(half, (0, p), (1, p), on)
        text_copy(half, (0, p), (3, p), off)

    def text_far_first(half):
        on, off = rings[half][0]
        text_copy(half, (0, 1), (0, 2), on, 0)
        text_copy(half, (0, 3), (0, 2), off, 1)

    def text_far_second(half, p):
        on, off = rings[half][1]
        text_copy(half, (1, p), (2, p), on, 0)
        text_copy(half, (3, p), (2, p), off, 1)

    halves = (0, 1)
    text_first(1)
    text_second(0, 0)
    text_first(0)
    text_second(1, 0)

    for one in embed_copies:
        one.wait_recv()
    wide = r.embed[...].astype(F32)
    image_scale = lax.rsqrt(jnp.sum(wide * wide, axis=1, keepdims=True) + 1e-06)
    unit = wide * image_scale
    r.images[0:128, :] = unit.astype(BF16)

    def image_slot(s, part=None):
        return pl.ds(s * 128, 128) if part is None else pl.ds(s * 128 + 64 * part, 64)

    def image_copy(src, dst, to, part=None):
        return copy(r.images.at[image_slot(src, part)], r.images.at[image_slot(dst, part)], to)

    image_on = [image_copy(0, 1, x_on, 0)]
    image_off = [image_copy(0, 3, x_off, 1)]
    image_on.append(image_copy(0, 1, x_on, 1))
    image_off.append(image_copy(0, 3, x_off, 0))
    shared = [image_copy(0, 4, sibling)]
    r.image_scale[...] = image_scale
    r.image_unit[...] = unit

    for half in (1, 0):
        arrived(half, 0, 1)
        arrived(half, 0, 3)
        text_far_first(half)
        text_second(half, 1)
        text_second(half, 3)
        if half == 1:
            image_on[0].wait_recv()
            image_far = [image_copy(1, 2, x_on, 0)]
            image_off[0].wait_recv()
            image_far.append(image_copy(3, 2, x_off, 1))

    for half in (0, 1):
        arrived(half, 1, 0)
        arrived(half, 3, 0)
        text_far_second(half, 0)
    image_on[1].wait_recv()
    image_off[1].wait_recv()
    shared += [image_copy(1, 5, sibling), image_copy(3, 7, sibling)]
    for half in (1, 0):
        arrived(half, 0, 2)
        text_second(half, 2)
    for one in image_far:
        one.wait_recv()
    shared.append(image_copy(2, 6, sibling))

    factor = sharp[0]
    shift = offset[0]

    def pair_weights(s, first=0, count=1024):
        texts = pl.ds(PLACE[s] * 512, 512)

        def chunk(rows):
            logits = factor * nt(r.images[rows, :], r.texts[texts, :]) + shift
            r.weights[rows, texts] = (factor / (1.0 + jnp.exp(-logits))).astype(BF16)

        def run(j, _):
            chunk(cut(first + j * 512, 512, 512))
            return 0

        if count == 512:
            chunk(pl.ds(first, 512))
        else:
            lax.fori_loop(0, 2, run, 0)

    def matching_pairs():
        for half in halves:
            rows = pl.ds(half * 64, 64)
            cols = pl.ds(half * 256, 128)
            logits = factor * nt(r.images[rows, :], r.texts[cols, :]) + shift
            hit = lax.broadcasted_iota(jnp.int32, (64, 128), 0) == lax.broadcasted_iota(
                jnp.int32, (64, 128), 1
            )
            label = jnp.where(hit, 1.0, -1.0)
            w = -label * factor / (1.0 + jnp.exp(label * logits))
            r.weights[rows, cols] = w.astype(BF16)

    near_texts = pl.ds(0, 1536)
    far_texts = pl.ds(1536, 512)

    def image_part(cols):
        r.image_dz[:, cols] = nn(r.weights[:, near_texts], r.texts[near_texts, cols])

    pair_weights(0, 0, 512)
    matching_pairs()
    for one in shared:
        one.wait_recv()
    pair_weights(0, 512, 512)
    for p in (1, 3):
        for half in halves:
            arrived(half, 1, p)
            arrived(half, 3, p)
            text_far_second(half, p)
    loads[0].wait()

    def activate(cols):
        value, derivative = gelu_parts(r.latent[:, cols].astype(F32))
        r.active[:, cols] = value.astype(BF16)
        r.slope[:, cols] = derivative

    loop(4, activate)
    for half in halves:
        arrived(half, 1, 2)
        arrived(half, 3, 2)
        text_far_second(half, 2)
    pair_weights(1)
    pair_weights(3)
    own_columns = r.mapper.at[:, cols_of(hi, core)]
    map_copies = [copy(own_columns, own_columns, beside), copy(own_columns, own_columns, sibling)]
    loop(4, image_part)
    for p in range(4):
        for half in halves:
            arrived(half, 2, p)

    def last_sibling(cols):
        part = nn(r.weights[512:1024, far_texts], r.texts[far_texts, cols])
        r.cross_out[:, cols] = (part + r.image_dz[512:1024, cols]).astype(BF16)

    def last_own(cols):
        part = nn(r.weights[0:512, far_texts], r.texts[far_texts, cols])
        r.image_dz[0:512, cols] = part + r.image_dz[0:512, cols]

    pair_weights(2, 512, 512)
    loop(2, last_sibling, 512)
    cross = copy(r.cross_out, r.cross_in, sibling)
    pair_weights(2, 0, 512)
    loop(2, last_own, 512)
    cross.wait_recv()

    def image_block(k, i):
        return image_slot((4 - k) % 4, i), slice(None)

    image_ring = RingSum(net, r.image_sum, image_block, r.image_far, r.image_near, x_on, x_off)

    def image_total(s):
        rows = image_slot(s)
        r.image_sum[rows, :] = (r.image_dz[rows, :] + r.cross_in[rows, :].astype(F32)).astype(BF16)

    image_total(2)
    image_ring.start_far()
    image_total(1)
    image_total(3)
    image_ring.start_near()
    image_total(0)

    def text_grads(half, *groups):
        for s in groups:
            rows = pl.ds(PLACE[s] * 512 + half * 256, 256)
            r.text_dz[rows, :] = tn(r.weights[:, rows], r.images[...]).astype(BF16)

    def second_ring(half):
        def block(k, i):
            return pl.ds(PLACE[(4 - k) % 4] * 512 + half * 256 + 128 * i, 128), slice(None)

        on, off = rings[half][1]
        return RingSum(net, r.text_dz, block, r.text_far.at[half], r.text_near.at[half], on, off)

    def first_ring(half):
        def block(k, i):
            return pl.ds(half * 256 + ((4 - k) % 4) * 64 + 32 * i, 32), slice(None)

        on, off = rings[half][0]
        return RingSum(net, r.text_sum, block, r.last_far.at[half], r.last_near.at[half], on, off)

    seconds = [second_ring(half) for half in halves]
    firsts = [first_ring(half) for half in halves]

    text_grads(0, 2, 1, 3)
    seconds[0].start()
    text_grads(1, 2)
    image_ring.middle()
    text_grads(1, 1, 3)
    text_grads(0, 0)
    image_ring.arrive()
    dz = jnp.concatenate([image_ring.total(0), image_ring.total(1)], axis=0)
    unit = r.image_unit[...]
    grad = r.image_scale[...] * (dz - unit * jnp.sum(unit * dz, axis=1, keepdims=True))
    mine = rows_of(hi, core)
    r.image_grad[mine, :] = grad.astype(BF16)
    block = r.image_grad.at[mine]
    spread = [copy(block, block, across), copy(block, block, sibling)]
    text_grads(1, 0)

    map_copies[0].wait_recv()
    other_columns = r.mapper.at[:, cols_of(hi + 1, core)]
    map_copies.append(copy(other_columns, other_columns, sibling))
    seconds[0].middle()
    map_copies[1].wait_recv()
    map_copies[2].wait_recv()
    spread[1].wait_recv()

    def back_rows(h):
        rows = cut((h % 2) * 256, 256, 256)

        def part(cols):
            r.back[rows, cols] = nt(r.image_grad[rows, :], r.mapper[cols, :]).astype(BF16)

        loop(2, part, 512)

    back_rows(hi)
    spread[0].wait_recv()
    block = r.image_grad.at[rows_of(hi + 1, core)]
    spread.append(copy(block, block, sibling))
    seconds[1].start()
    spread[2].wait_recv()
    back_rows(hi + 1)

    first = (net.z, net.x)
    other = (net.x, net.z)
    along = ((z_on, z_off), (x_on, x_off))
    wide = (pl.ds(0, 512), pl.ds(512, 512))

    def strip_rows(part, k, i=None):
        start = part * PART + ((first[part] + k) % 4) * STRIP
        return cut(start, STRIP) if i is None else cut(start + i * TILE, TILE)

    def side_columns(part, c, k):
        return cut(c * 512 + ((other[part] + k) % 4) * 128, 128, 128)

    def grad_ring(part, c):
        def block(k, i):
            return strip_rows(part, k, i), wide[c]

        n = part * 2 + c
        return RingSum(net, r.grads, block, r.grad_far.at[n], r.grad_near.at[n], *along[part])

    chains = ((1, 0), (1, 1), (0, 0), (0, 1))
    grad_rings = {chain: grad_ring(*chain) for chain in chains}

    def proj_part(cols):
        value = tn(final[:, cols], r.image_grad[:, cols_of(hi, core)]).astype(BF16)
        r.grads[1024:1152, cols] = value[0:128]
        r.grads[2176:2304, cols] = value[128:256]

    def down(c):
        def part(j, _):
            cols = cut(j * 512, 512, 512)
            value = tn(r.active[:, cols], r.back[:, wide[c]])
            r.grads[cut(PART + j * 512, 512, 128), wide[c]] = value.astype(BF16)
            return 0

        lax.fori_loop(0, 2, part, 0)

    def up(c):
        value = nt(r.back[...], r.second[wide[c], :]) * r.slope[:, wide[c]]
        r.pre[:, wide[c]] = value.astype(BF16)

        def part(rows):
            r.grads[rows, wide[c]] = tn(r.entry[:, rows], r.pre[:, wide[c]]).astype(BF16)

        loop(2, part, 512)

    loop(4, proj_part)
    down(0)
    grad_rings[1, 0].start()
    loads[1].wait()
    loads[2].wait()
    up(0)
    grad_rings[0, 0].start()
    down(1)
    grad_rings[1, 0].middle()
    grad_rings[1, 1].start_far()
    up(1)
    grad_rings[0, 0].middle()
    grad_rings[0, 1].start_far()

    def text_first_sum(half):
        seconds[half].arrive()
        for i in (0, 1):
            r.text_sum[pl.ds(half * 256 + 128 * i, 128), :] = seconds[half].total(i).astype(BF16)
        firsts[half].start()

    seconds[1].middle()
    text_first_sum(0)

    def side_to(part, k):
        return net.at(x=k) if part == 0 else net.at(z=k)

    sides = {}

    def side(part, c):
        ring = grad_rings[part, c]
        ring.arrive()
        sides[part, c] = []
        for n, k in enumerate((2, 1, 3, 0)):
            cols = side_columns(part, c, k)
            near = cut(((other[part] + k) % 4) * 128, 128, 128)
            for i in (0, 1):
                rows = pl.ds(i * TILE, TILE)
                total = ring.total(i, cols, near)
                if k == 0:
                    r.strip[part, rows, wide_tile[c]] = total
                else:
                    r.side_out[part, n, rows, wide_tile[c]] = total.astype(BF16)
            if k:
                sides[part, c].append(
                    copy(
                        r.side_out.at[part, n, :, wide_tile[c]],
                        r.side_in.at[part, n, :, wide_tile[c]],
                        side_to(part, k),
                    )
                )

    wide_tile = (pl.ds(0, 128), pl.ds(128, 128))
    side(1, 0)
    grad_rings[0, 1].start_near()
    side(0, 0)
    grad_rings[1, 1].start_near()
    grad_rings[1, 1].middle()
    grad_rings[0, 1].middle()
    firsts[0].middle()

    kept = cut(net.lo * TILE, TILE)
    given = cut((1 - net.lo) * TILE, TILE)
    tiles = {}

    def tile(part, c):
        for one in sides[part, c]:
            one.wait_recv()
        at = wide_tile[c]

        def total(rows):
            value = r.strip[part, rows, at]
            for n in range(3):
                value = value + r.side_in[part, n, rows, at].astype(F32)
            return value

        r.tile_out[part, :, at] = total(given).astype(BF16)
        tiles[part, c] = copy(r.tile_out.at[part, :, at], r.tile_in.at[part, :, at], pair_lo)
        r.tile[part, :, at] = total(kept)

    spread_tile = {}

    def back_tile(part, c):
        tiles[part, c].wait_recv()
        at = wide_tile[c]
        rows = cut(part * PART + first[part] * STRIP + net.lo * TILE, TILE)
        cols = side_columns(part, c, 0)
        r.done[rows, cols] = (r.tile[part, :, at] + r.tile_in[part, :, at].astype(F32)).astype(BF16)
        block = r.done.at[rows, cols]
        spread_tile[part, c] = copy(block, block, pair_lo)

    spread_side = {}

    def back_side(part, c):
        spread_tile[part, c].wait_recv()
        block = r.done.at[strip_rows(part, 0), side_columns(part, c, 0)]
        spread_side[part, c] = [copy(block, block, side_to(part, k)) for k in (2, 1, 3)]

    spread_strip = {}

    def back_strip(part, c):
        for one in spread_side[part, c]:
            one.wait_recv()
        on, off = along[part]
        spread_strip[part, c] = []
        for i, to in ((0, on), (1, off), (1, on), (0, off)):
            block = r.done.at[strip_rows(part, 0, i), wide[c]]
            spread_strip[part, c].append(copy(block, block, to))

    last = []

    def back_far(part, c):
        on, off = along[part]
        for i, k, to in ((0, 3, on), (1, 1, off)):
            spread_strip[part, c][i].wait_recv()
            block = r.done.at[strip_rows(part, k, i), wide[c]]
            last.append(copy(block, block, to))

    tile(1, 0)
    tile(0, 0)
    back_tile(1, 0)
    side(1, 1)
    back_tile(0, 0)
    side(0, 1)
    back_side(1, 0)
    back_side(0, 0)
    tile(1, 1)
    tile(0, 1)
    back_strip(1, 0)
    back_strip(0, 0)
    back_tile(1, 1)
    back_tile(0, 1)
    back_side(1, 1)
    back_side(0, 1)
    back_far(1, 0)
    back_far(0, 0)
    text_first_sum(1)
    back_strip(1, 1)
    back_strip(0, 1)
    firsts[1].middle()

    for half in halves:
        firsts[half].arrive()
    dz = jnp.concatenate([firsts[half].total(i) for half in halves for i in (0, 1)], axis=0)
    unit = r.text_unit[...]
    text_out[...] = r.text_scale[...] * (dz - unit * jnp.sum(unit * dz, axis=1, keepdims=True))

    back_far(1, 1)
    back_far(0, 1)
    outs = []
    for n, (part, c) in enumerate(((1, 0), (0, 0), (1, 1), (0, 1))):
        for one in spread_strip[part, c][2:] + last[2 * n : 2 * n + 2]:
            one.wait_recv()
        block = (pl.ds(part * PART, PART), wide[c])
        outs.append(pltpu.make_async_copy(r.done.at[block], total_out.at[block], r.load.at[3 + n]))
        outs[-1].start()
    for one in net.started:
        one.wait_send()
    for one in outs:
        one.wait()


SCRATCH = dict(
    caption=((128, 1024), BF16),
    final=((512, 1024), BF16),
    own_mapper=((1024, 256), BF16),
    columns=((512, 256), BF16),
    texts=((2048, 1024), BF16),
    text_unit=((128, 1024), F32),
    text_scale=((128, 1), F32),
    embed=((128, 1024), BF16),
    image_unit=((128, 1024), F32),
    image_scale=((128, 1), F32),
    images=((1024, 1024), BF16),
    mapper=((1024, 1024), BF16),
    latent=((512, 1024), BF16),
    second=((1024, 1024), BF16),
    entry=((512, 1024), BF16),
    active=((512, 1024), BF16),
    slope=((512, 1024), F32),
    weights=((1024, 2048), BF16),
    image_dz=((1024, 1024), F32),
    cross_out=((512, 1024), BF16),
    cross_in=((512, 1024), BF16),
    image_sum=((512, 1024), BF16),
    image_far=((2, 64, 1024), BF16),
    image_near=((2, 128, 1024), BF16),
    text_dz=((2048, 1024), BF16),
    text_far=((2, 2, 128, 1024), BF16),
    text_near=((2, 2, 256, 1024), BF16),
    text_sum=((512, 1024), BF16),
    last_far=((2, 2, 32, 1024), BF16),
    last_near=((2, 2, 64, 1024), BF16),
    image_grad=((512, 1024), BF16),
    back=((512, 1024), BF16),
    pre=((512, 1024), BF16),
    grads=((2 * PART, 1024), BF16),
    done=((2 * PART, 1024), BF16),
    grad_far=((4, 2, TILE, 512), BF16),
    grad_near=((4, 2, STRIP, 512), BF16),
    strip=((2, STRIP, 256), F32),
    side_out=((2, 3, STRIP, 256), BF16),
    side_in=((2, 3, STRIP, 256), BF16),
    tile=((2, TILE, 256), F32),
    tile_out=((2, TILE, 256), BF16),
    tile_in=((2, TILE, 256), BF16),
    send=((COPIES,), None),
    recv=((COPIES,), None),
    load=((10,), None),
)


def step(sharp, offset, caption, final, mapper, latent, second, entry):
    return pl.pallas_call(
        step_kernel,
        name="pairs_and_weight_grads",
        out_shape=(
            jax.ShapeDtypeStruct((2 * PART, 1024), BF16),
            jax.ShapeDtypeStruct((128, 1024), F32),
        ),
        in_specs=[SMEM, SMEM] + [ANY] * 6,
        out_specs=(ANY, VMEM),
        scratch_shapes=[
            pltpu.SemaphoreType.DMA(shape) if kind is None else pltpu.VMEM(shape, kind)
            for shape, kind in SCRATCH.values()
        ],
        compiler_params=pltpu.CompilerParams(
            collective_id=0, has_side_effects=True, vmem_limit_bytes=60 * 2**20
        ),
    )(sharp, offset, caption, final, mapper, latent, second, entry)


LION = dict(
    total=((2 * PART, 1024), BF16),
    w_up=((1024, 1024), BF16),
    w_down=((1024, 1024), BF16),
    w_proj=((1024, 256), BF16),
    m_up=((1024, 1024), BF16),
    m_down=((1024, 1024), BF16),
    m_proj=((1024, 256), BF16),
)
LION_CUTS = 1
LION_OUT = ("u_up", "u_down", "u_proj", "r_up", "r_down", "r_proj")
LION_JOBS = 2 * LION_CUTS + 1


def lion_kernel(
    total, text, w_up, w_down, w_proj, m_up, m_down, m_proj,
    u_up, u_down, u_proj, r_up, r_down, r_proj, text_out, *scratch,
):
    held = dict(zip(LION, scratch))
    kept = dict(zip(LION_OUT, scratch[len(LION) :]))
    arrive, leave = scratch[-2:]
    given = dict(
        total=total, w_up=w_up, w_down=w_down, w_proj=w_proj, m_up=m_up, m_down=m_down, m_proj=m_proj
    )
    results = dict(u_up=u_up, u_down=u_down, u_proj=u_proj, r_up=r_up, r_down=r_down, r_proj=r_proj)
    size = 1024 // LION_CUTS
    whole = slice(None)

    def cuts(name, n):
        if name == "down":
            rows = pl.ds(n * size, size)
            return (rows, whole), [(pl.ds(PART + n * size, size), whole)]
        if name == "up":
            cols = pl.ds(n * size, size)
            return (whole, cols), [(pl.ds(0, 1024), cols)]
        return (whole, whole), [(pl.ds(1024, 128), whole), (pl.ds(PART + 1024, 128), whole)]

    jobs = [("down", n) for n in range(LION_CUTS)] + [("up", n) for n in range(LION_CUTS)]
    jobs.insert(0, ("proj", 0))
    loads = []
    for k, (name, n) in enumerate(jobs):
        at, grads = cuts(name, n)
        mine = [("w_" + name, at), ("m_" + name, at)] + [("total", one) for one in grads]
        loads.append(
            [
                pltpu.make_async_copy(given[key].at[part], held[key].at[part], arrive.at[k, i])
                for i, (key, part) in enumerate(mine)
            ]
        )
    fetched = pltpu.make_async_copy(text, scratch[-3], leave.at[LION_JOBS, 0])
    passed = pltpu.make_async_copy(scratch[-3], text_out, leave.at[LION_JOBS, 1])
    for one in loads[0] + loads[1] + [fetched]:
        one.start()
    for job in loads[2:]:
        for one in job:
            one.start()

    def blend(m, g):
        return 0.9 * m + 0.1 * g

    def finish(name, at, m, g, mix, floor):
        w = held["w_" + name][at].astype(F32)
        kept["u_" + name][at] = (mix * lax.rsqrt(mix * mix + floor) + w).astype(BF16)
        kept["r_" + name][at] = (0.99 * m + 0.01 * g).astype(BF16)

    def column_job(name, cols, width, grad, count):
        def read(j):
            at = (cut(j * 128, 128, 128), cols)
            g = grad(j)
            m = held["m_" + name][at].astype(F32)
            return at, m, g, blend(m, g)

        def add(j, acc):
            mix = read(j)[3]
            return acc + jnp.sum((mix * mix).reshape(16, 8, width), axis=0)

        acc = lax.fori_loop(0, count, add, jnp.zeros((8, width), F32), unroll=True)
        floor = 0.0625 * (jnp.sum(acc, axis=0, keepdims=True) * (1.0 / 1024) + 1e-06)

        def write(j, _):
            at, m, g, mix = read(j)
            finish(name, at, m, g, mix, floor)
            return 0

        lax.fori_loop(0, count, write, 0, unroll=True)

    stores = []
    for k, (name, n) in enumerate(jobs):
        for one in loads[k]:
            one.wait()
        at = cuts(name, n)[0]
        if name == "down":

            def rows(j, _):
                here = cut(n * size + j * 32, 32, 32)
                there = cut(PART + n * size + j * 32, 32, 32)
                m = held["m_down"][here, :].astype(F32)
                g = held["total"][there, :].astype(F32)
                mix = blend(m, g)
                floor = 0.0625 * (jnp.mean(mix * mix, axis=1, keepdims=True) + 1e-06)
                finish("down", (here, whole), m, g, mix, floor)
                return 0

            lax.fori_loop(0, size // 32, rows, 0, unroll=True)
        elif name == "up":
            cols = pl.ds(n * size, size)
            column_job("up", cols, size, lambda j: held["total"][cut(j * 128, 128, 128), cols].astype(F32), 8)
        else:
            def grad(j):
                rows = cut(1024 + (j % 2) * PART, 128, 128)
                return held["total"][rows, cut((j // 2) * 256, 256, 256)].astype(F32)

            column_job("proj", pl.ds(0, 256), 256, grad, 8)
        for i, key in enumerate(("u_" + name, "r_" + name)):
            stores.append(pltpu.make_async_copy(kept[key].at[at], results[key].at[at], leave.at[k, i]))
            stores[-1].start()
        if k == 1:
            fetched.wait()
            passed.start()
    for one in stores:
        one.wait()
    passed.wait()


def lion(total, text, weights, moments):
    square = jax.ShapeDtypeStruct((1024, 1024), BF16)
    narrow = jax.ShapeDtypeStruct((1024, 256), BF16)
    outs = (square, square, narrow, square, square, narrow)
    return pl.pallas_call(
        lion_kernel,
        name="lion",
        out_shape=(*outs, jax.ShapeDtypeStruct(text.shape, F32)),
        in_specs=[ANY] * 8,
        out_specs=(ANY,) * 7,
        scratch_shapes=[pltpu.VMEM(*one) for one in LION.values()]
        + [pltpu.VMEM(one.shape, BF16) for one in outs]
        + [pltpu.VMEM(text.shape, F32)]
        + [pltpu.SemaphoreType.DMA((LION_JOBS, 4)), pltpu.SemaphoreType.DMA((LION_JOBS + 1, 2))],
        compiler_params=pltpu.CompilerParams(vmem_limit_bytes=60 * 2**20),
    )(total, text, *weights, *moments)


def per_device(
    vision_layer_entry,
    latent_preact_values,
    final_layer_result,
    caption_vectors_raw,
    sharpness_factor,
    offset_term,
    first_feedforward_matrix,
    second_feedforward_matrix,
    mapper_matrix,
    first_matrix_velocity,
    second_matrix_velocity,
    mapper_velocity,
):
    total, text_grad = step(
        sharpness_factor,
        offset_term,
        caption_vectors_raw,
        final_layer_result,
        mapper_matrix,
        latent_preact_values,
        second_feedforward_matrix,
        vision_layer_entry,
    )
    return lion(
        total,
        text_grad,
        (first_feedforward_matrix, second_feedforward_matrix, mapper_matrix),
        (first_matrix_velocity, second_matrix_velocity, mapper_velocity),
    )


def solution(mesh):
    return jax.shard_map(
        per_device,
        mesh=mesh,
        in_specs=(
            P("dp", None),
            P("dp", "mp"),
            P("dp", None),
            P(("dp", "mp"), None),
            P(),
            P(),
            P(None, "mp"),
            P("mp", None),
            P(None, "mp"),
            P(None, "mp"),
            P("mp", None),
            P(None, "mp"),
        ),
        out_specs=(
            P(None, "mp"),
            P("mp", None),
            P(None, "mp"),
            P(None, "mp"),
            P("mp", None),
            P(None, "mp"),
            P(("dp", "mp"), None),
        ),
        check_vma=False,
    )
```

```python
import types

import jax
import jax.numpy as jnp
from jax import lax
from jax.experimental import pallas as pl
from jax.experimental.pallas import tpu as pltpu
from jax.sharding import PartitionSpec as P

MESH = pl.DeviceIdType.MESH
F32 = jnp.float32
BF16 = jnp.bfloat16
VMEM = pl.BlockSpec(memory_space=pltpu.VMEM)
SMEM = pl.BlockSpec(memory_space=pltpu.SMEM)
ANY = pl.BlockSpec(memory_space=pl.ANY)

PART = 1152
STRIP = 288
TILE = 144
COPIES = 200
PLACE = (0, 1, 3, 2)


def nn(a, b):
    return jnp.dot(a, b, preferred_element_type=F32)


def nt(a, b):
    return lax.dot_general(a, b, (((1,), (1,)), ((), ())), preferred_element_type=F32)


def tn(a, b):
    return lax.dot_general(a, b, (((0,), (0,)), ((), ())), preferred_element_type=F32)


def cut(start, size, unit=16):
    return pl.ds(start if isinstance(start, int) else pl.multiple_of(start, unit), size)


def loop(count, body, size=256):
    def run(j, _):
        body(cut(j * size, size, size))
        return 0

    lax.fori_loop(0, count, run, 0)


def gelu_parts(value):
    slope = 0.7978845608028654
    square = value * value
    t = jnp.tanh(slope * (value + 0.044715 * (square * value)))
    cdf = 0.5 * (1.0 + t)
    derivative = cdf + 0.5 * value * (1.0 - t * t) * (slope * (1.0 + 3 * 0.044715 * square))
    return value * cdf, derivative


class Links:
    def __init__(self, send, recv):
        d = lax.axis_index("dp")
        m = lax.axis_index("mp")
        self.z, self.x, self.lo = d // 8, (d // 2) % 4, d % 2
        self.hi, self.core = m // 2, m % 2
        self.y = self.hi * 2 + self.lo
        self.send, self.recv = send, recv
        self.started = []

    def at(self, z=0, x=0, y=0, core=0):
        row = (self.y + y) % 4
        dp = (((self.z + z) % 4) * 4 + (self.x + x) % 4) * 2 + row % 2
        return dp, (row // 2) * 2 + (self.core + core) % 2

    def copy(self, src, dst, to):
        k = len(self.started)
        assert k < COPIES
        one = pltpu.make_async_remote_copy(
            src_ref=src,
            dst_ref=dst,
            send_sem=self.send.at[k],
            recv_sem=self.recv.at[k],
            device_id=to,
            device_id_type=MESH,
        )
        one.start()
        self.started.append(one)
        return one


class RingSum:
    def __init__(self, links, src, block, far_in, near_in, on, off):
        self.links, self.src, self.block = links, src, block
        self.far_in, self.near_in, self.on, self.off = far_in, near_in, on, off
        self.half = far_in.shape[1]

    def part(self, k, i):
        return self.near_in.at[k, pl.ds(i * self.half, self.half)]

    def start(self):
        self.start_far()
        self.start_near()

    def start_far(self):
        copy, src, block = self.links.copy, self.src, self.block
        self.far = [
            copy(src.at[block(2, 0)], self.far_in.at[0], self.on),
            copy(src.at[block(2, 1)], self.far_in.at[1], self.off),
        ]

    def start_near(self):
        copy, src, block = self.links.copy, self.src, self.block
        self.near = [
            copy(src.at[block(1, 1)], self.part(0, 1), self.on),
            copy(src.at[block(3, 0)], self.part(1, 0), self.off),
        ]

    def middle(self):
        for i, k, to in ((0, 1, self.on), (1, 3, self.off)):
            self.far[i].wait_recv()
            at = self.block(k, i)
            self.src[at] = (self.src[at].astype(F32) + self.far_in[i].astype(F32)).astype(BF16)
            self.near.append(self.links.copy(self.src.at[at], self.part(i, i), to))

    def arrive(self):
        for one in self.near:
            one.wait_recv()

    def total(self, i, cols=None, near=slice(None)):
        rows = pl.ds(i * self.half, self.half)
        at = self.block(0, i)
        own = self.src[at] if cols is None else self.src[at[0], cols]
        return (
            own.astype(F32)
            + self.near_in[0, rows, near].astype(F32)
            + self.near_in[1, rows, near].astype(F32)
        )


def step_kernel(
    sharp,
    offset,
    caption_in,
    final_in,
    mapper_in,
    latent_in,
    second_in,
    entry_in,
    total_out,
    text_out,
    *scratch,
):
    r = types.SimpleNamespace(**dict(zip(SCRATCH, scratch)))
    caption, final, mapper = r.caption, r.final, r.own_mapper
    early = [
        pltpu.make_async_copy(src, dst, r.load.at[7 + k])
        for k, (src, dst) in enumerate(((caption_in, caption), (mapper_in, mapper), (final_in, final)))
    ]
    for one in early:
        one.start()
    net = Links(r.send, r.recv)
    hi, core = net.hi, net.core
    copy = net.copy
    sibling = net.at(core=1)
    z_on, z_off = net.at(z=1), net.at(z=3)
    x_on, x_off = net.at(x=1), net.at(x=3)
    y_on, y_off = net.at(y=1), net.at(y=3)
    across = net.at(y=2)
    pair_lo = net.at(y=1 - 2 * net.lo + 4)
    beside = net.at(y=2 * net.lo + 3)
    quarter = hi * 2 + core

    def rows_of(h, c):
        return cut(((h % 2) * 2 + c % 2) * 128, 128, 128)

    def cols_of(h, c):
        return cut(((h % 2) * 2 + c % 2) * 256, 256, 256)

    barrier = pltpu.get_barrier_semaphore()
    partners = [sibling, z_on, z_off, net.at(z=2), x_on, x_off, net.at(x=2), y_on, y_off, across]
    partners.append(net.at(y=2, core=1))
    for one in partners:
        pl.semaphore_signal(barrier, inc=1, device_id=one, device_id_type=MESH)
    loads = [
        pltpu.make_async_copy(src, dst, r.load.at[k])
        for k, (src, dst) in enumerate(
            ((latent_in, r.latent), (second_in, r.second), (entry_in, r.entry))
        )
    ]
    for one in loads:
        one.start()

    early[0].wait()
    raw = caption[...].astype(F32)
    text_scale = lax.rsqrt(jnp.sum(raw * raw, axis=1, keepdims=True) + 1e-06)
    unit = raw * text_scale
    r.text_scale[...] = text_scale
    r.text_unit[...] = unit
    unit = unit.astype(BF16)
    r.texts[0:64, :] = unit[0:64]
    r.texts[256:320, :] = unit[64:128]
    early[1].wait()
    r.mapper[:, cols_of(hi, core)] = mapper[...]
    early[2].wait()
    r.columns[...] = nn(final[...], mapper[...]).astype(BF16)
    r.embed[:, cols_of(hi, core)] = r.columns[rows_of(hi, core), :]
    pl.semaphore_wait(barrier, len(partners))

    def give(h, c, to):
        return copy(r.columns.at[rows_of(h, c)], r.embed.at[:, cols_of(hi, core)], to)

    embed_copies = [
        give(hi + 1, core, across),
        give(hi + 1, core + 1, net.at(y=2, core=1)),
        give(hi, core + 1, sibling),
    ]

    rings = (((y_on, y_off), (z_on, z_off)), ((z_on, z_off), (y_on, y_off)))

    def slot(half, s, p, part=None):
        start = PLACE[s] * 512 + half * 256 + p * 64
        return pl.ds(start, 64) if part is None else pl.ds(start + 32 * part, 32)

    got = {}

    def text_copy(half, src, dst, to, part=None):
        one = copy(r.texts.at[slot(half, *src, part)], r.texts.at[slot(half, *dst, part)], to)
        got.setdefault((half, dst), []).append(one)

    def arrived(half, s, p):
        for one in got[half, (s, p)]:
            one.wait_recv()

    def text_first(half):
        on, off = rings[half][0]
        text_copy(half, (0, 0), (0, 1), on)
        text_copy(half, (0, 0), (0, 3), off)

    def text_second(half, p):
        on, off = rings[half][1]
        text_copy(half, (0, p), (1, p), on)
        text_copy(half, (0, p), (3, p), off)

    def text_far_first(half):
        on, off = rings[half][0]
        text_copy(half, (0, 1), (0, 2), on, 0)
        text_copy(half, (0, 3), (0, 2), off, 1)

    def text_far_second(half, p):
        on, off = rings[half][1]
        text_copy(half, (1, p), (2, p), on, 0)
        text_copy(half, (3, p), (2, p), off, 1)

    halves = (0, 1)
    text_first(1)
    text_second(0, 0)
    text_first(0)
    text_second(1, 0)

    for one in embed_copies:
        one.wait_recv()
    wide = r.embed[...].astype(F32)
    image_scale = lax.rsqrt(jnp.sum(wide * wide, axis=1, keepdims=True) + 1e-06)
    unit = wide * image_scale
    r.images[0:128, :] = unit.astype(BF16)

    def image_slot(s, part=None):
        return pl.ds(s * 128, 128) if part is None else pl.ds(s * 128 + 64 * part, 64)

    def image_copy(src, dst, to, part=None):
        return copy(r.images.at[image_slot(src, part)], r.images.at[image_slot(dst, part)], to)

    image_on = [image_copy(0, 1, x_on, 0)]
    image_off = [image_copy(0, 3, x_off, 1)]
    image_on.append(image_copy(0, 1, x_on, 1))
    image_off.append(image_copy(0, 3, x_off, 0))
    shared = [image_copy(0, 4, sibling)]
    r.image_scale[...] = image_scale
    r.image_unit[...] = unit

    for half in (1, 0):
        arrived(half, 0, 1)
        arrived(half, 0, 3)
        text_far_first(half)
    for half in (0, 1):
        text_second(half, 1)
        text_second(half, 3)
    arrived(0, 1, 0)
    arrived(0, 3, 0)
    text_far_second(0, 0)
    image_on[0].wait_recv()
    image_far = [image_copy(1, 2, x_on, 0)]
    image_off[0].wait_recv()
    image_far.append(image_copy(3, 2, x_off, 1))
    for half in (1, 0):
        arrived(half, 0, 2)
        text_second(half, 2)
    arrived(1, 1, 0)
    arrived(1, 3, 0)
    text_far_second(1, 0)
    image_on[1].wait_recv()
    image_off[1].wait_recv()
    shared += [image_copy(1, 5, sibling), image_copy(3, 7, sibling)]

    loads[0].wait()

    def activate(cols):
        value, derivative = gelu_parts(r.latent[:, cols].astype(F32))
        r.active[:, cols] = value.astype(BF16)
        r.slope[:, cols] = derivative

    loop(4, activate)
    for one in image_far:
        one.wait_recv()
    shared.append(image_copy(2, 6, sibling))

    factor = sharp[0]
    shift = offset[0]

    def pair_weights(s, first=0, count=1024):
        texts = pl.ds(PLACE[s] * 512, 512)

        def chunk(rows):
            logits = factor * nt(r.images[rows, :], r.texts[texts, :]) + shift
            r.weights[rows, texts] = (factor / (1.0 + jnp.exp(-logits))).astype(BF16)

        def run(j, _):
            chunk(cut(first + j * 512, 512, 512))
            return 0

        if count == 512:
            chunk(pl.ds(first, 512))
        else:
            lax.fori_loop(0, 2, run, 0)

    def matching_pairs():
        for half in halves:
            rows = pl.ds(half * 64, 64)
            cols = pl.ds(half * 256, 128)
            logits = factor * nt(r.images[rows, :], r.texts[cols, :]) + shift
            hit = lax.broadcasted_iota(jnp.int32, (64, 128), 0) == lax.broadcasted_iota(
                jnp.int32, (64, 128), 1
            )
            label = jnp.where(hit, 1.0, -1.0)
            w = -label * factor / (1.0 + jnp.exp(label * logits))
            r.weights[rows, cols] = w.astype(BF16)

    near_texts = pl.ds(0, 1536)
    far_texts = pl.ds(1536, 512)

    def image_part(cols):
        r.image_dz[:, cols] = nn(r.weights[:, near_texts], r.texts[near_texts, cols])

    pair_weights(0, 0, 512)
    matching_pairs()
    for p in (1, 3):
        arrived(0, 1, p)
        arrived(0, 3, p)
        text_far_second(0, p)
    for one in shared:
        one.wait_recv()
    pair_weights(0, 512, 512)
    for p in (1, 3):
        arrived(1, 1, p)
        arrived(1, 3, p)
        text_far_second(1, p)
    for half in halves:
        arrived(half, 1, 2)
        arrived(half, 3, 2)
        text_far_second(half, 2)
    pair_weights(1)
    pair_weights(3)
    own_columns = r.mapper.at[:, cols_of(hi, core)]
    map_copies = [copy(own_columns, own_columns, beside), copy(own_columns, own_columns, sibling)]
    loop(4, image_part)
    for p in range(4):
        for half in halves:
            arrived(half, 2, p)

    def last_sibling(cols):
        part = nn(r.weights[512:1024, far_texts], r.texts[far_texts, cols])
        r.cross_out[:, cols] = (part + r.image_dz[512:1024, cols]).astype(BF16)

    def last_own(cols):
        part = nn(r.weights[0:512, far_texts], r.texts[far_texts, cols])
        r.image_dz[0:512, cols] = part + r.image_dz[0:512, cols]

    pair_weights(2, 512, 512)
    loop(2, last_sibling, 512)
    cross = copy(r.cross_out, r.cross_in, sibling)
    pair_weights(2, 0, 512)
    loop(2, last_own, 512)
    cross.wait_recv()

    def image_ring(n):
        def block(k, i):
            return pl.ds(((4 - k) % 4) * 128 + n * 64 + i * 32, 32), slice(None)

        return RingSum(net, r.image_sum, block, r.image_far.at[n], r.image_near.at[n], x_on, x_off)

    image_rings = [image_ring(n) for n in (0, 1)]

    def image_total(s):
        rows = image_slot(s)
        r.image_sum[rows, :] = (r.image_dz[rows, :] + r.cross_in[rows, :].astype(F32)).astype(BF16)

    image_total(2)
    image_rings[0].start_far()
    image_total(1)
    image_total(3)
    image_rings[0].start_near()
    image_rings[1].start_far()
    image_total(0)

    def text_grads(half, *groups):
        for s in groups:
            rows = pl.ds(PLACE[s] * 512 + half * 256, 256)
            r.text_dz[rows, :] = tn(r.weights[:, rows], r.images[...]).astype(BF16)

    def second_ring(half):
        def block(k, i):
            return pl.ds(PLACE[(4 - k) % 4] * 512 + half * 256 + 128 * i, 128), slice(None)

        on, off = rings[half][1]
        return RingSum(net, r.text_dz, block, r.text_far.at[half], r.text_near.at[half], on, off)

    def first_ring(half):
        def block(k, i):
            return pl.ds(half * 256 + ((4 - k) % 4) * 64 + 32 * i, 32), slice(None)

        on, off = rings[half][0]
        return RingSum(net, r.text_sum, block, r.last_far.at[half], r.last_near.at[half], on, off)

    seconds = [second_ring(half) for half in halves]
    firsts = [first_ring(half) for half in halves]

    across_copies, beside_copies = [], []

    def image_finish(n):
        ring = image_rings[n]
        ring.arrive()
        rows = pl.ds(n * 64, 64)
        dz = jnp.concatenate([ring.total(0), ring.total(1)], axis=0)
        unit = r.image_unit[rows, :]
        grad = r.image_scale[rows, :] * (dz - unit * jnp.sum(unit * dz, axis=1, keepdims=True))
        mine = cut(quarter * 128 + n * 64, 64, 64)
        r.image_grad[mine, :] = grad.astype(BF16)
        block = r.image_grad.at[mine]
        across_copies.append(copy(block, block, across))
        beside_copies.append(copy(block, block, sibling))

    text_grads(0, 2, 1, 3)
    seconds[0].start()
    text_grads(1, 2)
    image_rings[0].middle()
    image_rings[1].start_near()
    text_grads(1, 1)
    image_rings[1].middle()
    text_grads(1, 3)
    image_finish(0)
    text_grads(0, 0)
    image_finish(1)
    text_grads(1, 0)

    map_copies[0].wait_recv()
    other_columns = r.mapper.at[:, cols_of(hi + 1, core)]
    map_copies.append(copy(other_columns, other_columns, sibling))
    seconds[0].middle()
    map_copies[1].wait_recv()
    map_copies[2].wait_recv()
    for one in beside_copies:
        one.wait_recv()

    def back_rows(h):
        rows = cut((h % 2) * 256, 256, 256)

        def part(cols):
            r.back[rows, cols] = nt(r.image_grad[rows, :], r.mapper[cols, :]).astype(BF16)

        loop(2, part, 512)

    back_rows(hi)
    here, there = cut(hi * 256, 256, 256), cut((1 - hi) * 256, 256, 256)
    own_cols = cols_of(hi, core)

    def proj_here(cols):
        r.image_dz[cols, 512:768] = tn(final[here, cols], r.image_grad[here, own_cols])

    def down_here(cols):
        r.image_dz[cols, 0:512] = tn(r.active[here, cols], r.back[here, 0:512])

    loop(2, proj_here, 512)
    loop(2, down_here, 512)
    passed = []
    for n in (0, 1):
        across_copies[n].wait_recv()
        block = r.image_grad.at[cut(((1 - hi) * 2 + core) * 128 + n * 64, 64, 64)]
        passed.append(copy(block, block, sibling))
    seconds[1].start()
    for one in passed:
        one.wait_recv()
    back_rows(hi + 1)

    first = (net.z, net.x)
    other = (net.x, net.z)
    along = ((z_on, z_off), (x_on, x_off))
    wide = (pl.ds(0, 512), pl.ds(512, 512))

    def strip_rows(part, k, i=None):
        start = part * PART + ((first[part] + k) % 4) * STRIP
        return cut(start, STRIP) if i is None else cut(start + i * TILE, TILE)

    def side_columns(part, c, k):
        return cut(c * 512 + ((other[part] + k) % 4) * 128, 128, 128)

    def grad_ring(part, c):
        def block(k, i):
            return strip_rows(part, k, i), wide[c]

        n = part * 2 + c
        return RingSum(net, r.grads, block, r.grad_far.at[n], r.grad_near.at[n], *along[part])

    chains = ((1, 0), (1, 1), (0, 0), (0, 1))
    grad_rings = {chain: grad_ring(*chain) for chain in chains}

    def proj_part(cols):
        value = tn(final[there, cols], r.image_grad[there, own_cols])
        value = (value + r.image_dz[cols, 512:768]).astype(BF16)
        r.grads[1024:1152, cols] = value[0:128]
        r.grads[2176:2304, cols] = value[128:256]

    def down(c):
        def part(j, _):
            cols = cut(j * 512, 512, 512)
            if c == 0:
                value = tn(r.active[there, cols], r.back[there, wide[c]]) + r.image_dz[cols, 0:512]
            else:
                value = tn(r.active[:, cols], r.back[:, wide[c]])
            r.grads[cut(PART + j * 512, 512, 128), wide[c]] = value.astype(BF16)
            return 0

        lax.fori_loop(0, 2, part, 0)

    def up(c):
        value = nt(r.back[...], r.second[wide[c], :]) * r.slope[:, wide[c]]
        r.pre[:, wide[c]] = value.astype(BF16)

        def part(rows):
            r.grads[rows, wide[c]] = tn(r.entry[:, rows], r.pre[:, wide[c]]).astype(BF16)

        loop(2, part, 512)

    loop(4, proj_part)
    down(0)
    grad_rings[1, 0].start()
    loads[1].wait()
    loads[2].wait()
    up(0)
    grad_rings[0, 0].start()
    down(1)
    grad_rings[1, 0].middle()
    grad_rings[1, 1].start_far()
    up(1)
    grad_rings[0, 0].middle()
    grad_rings[0, 1].start_far()

    def text_first_sum(half):
        seconds[half].arrive()
        for i in (0, 1):
            r.text_sum[pl.ds(half * 256 + 128 * i, 128), :] = seconds[half].total(i).astype(BF16)
        firsts[half].start()

    seconds[1].middle()
    text_first_sum(0)

    def side_to(part, k):
        return net.at(x=k) if part == 0 else net.at(z=k)

    sides = {}

    def side(part, c):
        ring = grad_rings[part, c]
        ring.arrive()
        sides[part, c] = []
        for n, k in enumerate((2, 1, 3, 0)):
            cols = side_columns(part, c, k)
            near = cut(((other[part] + k) % 4) * 128, 128, 128)
            for i in (0, 1):
                rows = pl.ds(i * TILE, TILE)
                total = ring.total(i, cols, near)
                if k == 0:
                    r.strip[part, rows, wide_tile[c]] = total
                else:
                    r.side_out[part, n, rows, wide_tile[c]] = total.astype(BF16)
            if k:
                sides[part, c].append(
                    copy(
                        r.side_out.at[part, n, :, wide_tile[c]],
                        r.side_in.at[part, n, :, wide_tile[c]],
                        side_to(part, k),
                    )
                )

    wide_tile = (pl.ds(0, 128), pl.ds(128, 128))
    side(1, 0)
    grad_rings[0, 1].start_near()
    side(0, 0)
    grad_rings[1, 1].start_near()
    grad_rings[1, 1].middle()
    grad_rings[0, 1].middle()
    firsts[0].middle()

    kept = cut(net.lo * TILE, TILE)
    given = cut((1 - net.lo) * TILE, TILE)
    tiles = {}

    def tile(part, c):
        for one in sides[part, c]:
            one.wait_recv()
        at = wide_tile[c]

        def total(rows):
            value = r.strip[part, rows, at]
            for n in range(3):
                value = value + r.side_in[part, n, rows, at].astype(F32)
            return value

        r.tile_out[part, :, at] = total(given).astype(BF16)
        tiles[part, c] = copy(r.tile_out.at[part, :, at], r.tile_in.at[part, :, at], pair_lo)
        r.tile[part, :, at] = total(kept)

    spread_tile = {}

    def back_tile(part, c):
        tiles[part, c].wait_recv()
        at = wide_tile[c]
        rows = cut(part * PART + first[part] * STRIP + net.lo * TILE, TILE)
        cols = side_columns(part, c, 0)
        r.done[rows, cols] = (r.tile[part, :, at] + r.tile_in[part, :, at].astype(F32)).astype(BF16)
        block = r.done.at[rows, cols]
        spread_tile[part, c] = copy(block, block, pair_lo)

    spread_side = {}

    def back_side(part, c):
        spread_tile[part, c].wait_recv()
        block = r.done.at[strip_rows(part, 0), side_columns(part, c, 0)]
        spread_side[part, c] = [copy(block, block, side_to(part, k)) for k in (2, 1, 3)]

    spread_strip = {}

    def back_strip(part, c):
        for one in spread_side[part, c]:
            one.wait_recv()
        on, off = along[part]
        spread_strip[part, c] = []
        for i, to in ((0, on), (1, off), (1, on), (0, off)):
            block = r.done.at[strip_rows(part, 0, i), wide[c]]
            spread_strip[part, c].append(copy(block, block, to))

    last = []

    def back_far(part, c):
        on, off = along[part]
        for i, k, to in ((0, 3, on), (1, 1, off)):
            spread_strip[part, c][i].wait_recv()
            block = r.done.at[strip_rows(part, k, i), wide[c]]
            last.append(copy(block, block, to))

    tile(1, 0)
    tile(0, 0)
    back_tile(1, 0)
    text_first_sum(1)
    side(1, 1)
    back_tile(0, 0)
    side(0, 1)
    back_side(1, 0)
    back_side(0, 0)
    firsts[1].middle()
    tile(1, 1)
    tile(0, 1)
    back_strip(1, 0)
    back_strip(0, 0)
    back_tile(1, 1)
    back_tile(0, 1)
    back_side(1, 1)
    back_side(0, 1)
    back_far(1, 0)
    back_far(0, 0)
    back_strip(1, 1)
    back_strip(0, 1)

    for half in halves:
        firsts[half].arrive()
    dz = jnp.concatenate([firsts[half].total(i) for half in halves for i in (0, 1)], axis=0)
    unit = r.text_unit[...]
    text_out[...] = r.text_scale[...] * (dz - unit * jnp.sum(unit * dz, axis=1, keepdims=True))

    back_far(1, 1)
    back_far(0, 1)
    outs = []
    for n, (part, c) in enumerate(((1, 0), (0, 0), (1, 1), (0, 1))):
        for one in spread_strip[part, c][2:] + last[2 * n : 2 * n + 2]:
            one.wait_recv()
        block = (pl.ds(part * PART, PART), wide[c])
        outs.append(pltpu.make_async_copy(r.done.at[block], total_out.at[block], r.load.at[3 + n]))
        outs[-1].start()
    for one in net.started:
        one.wait_send()
    for one in outs:
        one.wait()


SCRATCH = dict(
    caption=((128, 1024), BF16),
    final=((512, 1024), BF16),
    own_mapper=((1024, 256), BF16),
    columns=((512, 256), BF16),
    texts=((2048, 1024), BF16),
    text_unit=((128, 1024), F32),
    text_scale=((128, 1), F32),
    embed=((128, 1024), BF16),
    image_unit=((128, 1024), F32),
    image_scale=((128, 1), F32),
    images=((1024, 1024), BF16),
    mapper=((1024, 1024), BF16),
    latent=((512, 1024), BF16),
    second=((1024, 1024), BF16),
    entry=((512, 1024), BF16),
    active=((512, 1024), BF16),
    slope=((512, 1024), F32),
    weights=((1024, 2048), BF16),
    image_dz=((1024, 1024), F32),
    cross_out=((512, 1024), BF16),
    cross_in=((512, 1024), BF16),
    image_sum=((512, 1024), BF16),
    image_far=((2, 2, 32, 1024), BF16),
    image_near=((2, 2, 64, 1024), BF16),
    text_dz=((2048, 1024), BF16),
    text_far=((2, 2, 128, 1024), BF16),
    text_near=((2, 2, 256, 1024), BF16),
    text_sum=((512, 1024), BF16),
    last_far=((2, 2, 32, 1024), BF16),
    last_near=((2, 2, 64, 1024), BF16),
    image_grad=((512, 1024), BF16),
    back=((512, 1024), BF16),
    pre=((512, 1024), BF16),
    grads=((2 * PART, 1024), BF16),
    done=((2 * PART, 1024), BF16),
    grad_far=((4, 2, TILE, 512), BF16),
    grad_near=((4, 2, STRIP, 512), BF16),
    strip=((2, STRIP, 256), F32),
    side_out=((2, 3, STRIP, 256), BF16),
    side_in=((2, 3, STRIP, 256), BF16),
    tile=((2, TILE, 256), F32),
    tile_out=((2, TILE, 256), BF16),
    tile_in=((2, TILE, 256), BF16),
    send=((COPIES,), None),
    recv=((COPIES,), None),
    load=((10,), None),
)


def step(sharp, offset, caption, final, mapper, latent, second, entry):
    return pl.pallas_call(
        step_kernel,
        name="pairs_and_weight_grads",
        out_shape=(
            jax.ShapeDtypeStruct((2 * PART, 1024), BF16),
            jax.ShapeDtypeStruct((128, 1024), F32),
        ),
        in_specs=[SMEM, SMEM] + [ANY] * 6,
        out_specs=(ANY, VMEM),
        scratch_shapes=[
            pltpu.SemaphoreType.DMA(shape) if kind is None else pltpu.VMEM(shape, kind)
            for shape, kind in SCRATCH.values()
        ],
        compiler_params=pltpu.CompilerParams(
            collective_id=0, has_side_effects=True, vmem_limit_bytes=60 * 2**20
        ),
    )(sharp, offset, caption, final, mapper, latent, second, entry)


LION = dict(
    total=((2 * PART, 1024), BF16),
    w_up=((1024, 1024), BF16),
    w_down=((1024, 1024), BF16),
    w_proj=((1024, 256), BF16),
    m_up=((1024, 1024), BF16),
    m_down=((1024, 1024), BF16),
    m_proj=((1024, 256), BF16),
)
LION_CUTS = 1
LION_OUT = ("u_up", "u_down", "u_proj", "r_up", "r_down", "r_proj")
LION_JOBS = 2 * LION_CUTS + 1


def lion_kernel(
    total, text, w_up, w_down, w_proj, m_up, m_down, m_proj,
    u_up, u_down, u_proj, r_up, r_down, r_proj, text_out, *scratch,
):
    held = dict(zip(LION, scratch))
    kept = dict(zip(LION_OUT, scratch[len(LION) :]))
    arrive, leave = scratch[-2:]
    given = dict(
        total=total, w_up=w_up, w_down=w_down, w_proj=w_proj, m_up=m_up, m_down=m_down, m_proj=m_proj
    )
    results = dict(u_up=u_up, u_down=u_down, u_proj=u_proj, r_up=r_up, r_down=r_down, r_proj=r_proj)
    size = 1024 // LION_CUTS
    whole = slice(None)

    def cuts(name, n):
        if name == "down":
            rows = pl.ds(n * size, size)
            return (rows, whole), [(pl.ds(PART + n * size, size), whole)]
        if name == "up":
            cols = pl.ds(n * size, size)
            return (whole, cols), [(pl.ds(0, 1024), cols)]
        return (whole, whole), [(pl.ds(1024, 128), whole), (pl.ds(PART + 1024, 128), whole)]

    jobs = [("down", n) for n in range(LION_CUTS)] + [("up", n) for n in range(LION_CUTS)]
    jobs.insert(0, ("proj", 0))
    loads = []
    for k, (name, n) in enumerate(jobs):
        at, grads = cuts(name, n)
        mine = [("w_" + name, at), ("m_" + name, at)] + [("total", one) for one in grads]
        loads.append(
            [
                pltpu.make_async_copy(given[key].at[part], held[key].at[part], arrive.at[k, i])
                for i, (key, part) in enumerate(mine)
            ]
        )
    fetched = pltpu.make_async_copy(text, scratch[-3], leave.at[LION_JOBS, 0])
    passed = pltpu.make_async_copy(scratch[-3], text_out, leave.at[LION_JOBS, 1])
    for one in loads[0] + loads[1] + [fetched]:
        one.start()
    for job in loads[2:]:
        for one in job:
            one.start()

    def blend(m, g):
        return 0.9 * m + 0.1 * g

    def finish(name, at, m, g, mix, floor):
        w = held["w_" + name][at].astype(F32)
        kept["u_" + name][at] = (mix * lax.rsqrt(mix * mix + floor) + w).astype(BF16)
        kept["r_" + name][at] = (0.99 * m + 0.01 * g).astype(BF16)

    def column_job(name, cols, width, grad, count):
        def read(j):
            at = (cut(j * 128, 128, 128), cols)
            g = grad(j)
            m = held["m_" + name][at].astype(F32)
            return at, m, g, blend(m, g)

        def add(j, acc):
            mix = read(j)[3]
            return acc + jnp.sum((mix * mix).reshape(16, 8, width), axis=0)

        acc = lax.fori_loop(0, count, add, jnp.zeros((8, width), F32), unroll=True)
        floor = 0.0625 * (jnp.sum(acc, axis=0, keepdims=True) * (1.0 / 1024) + 1e-06)

        def write(j, _):
            at, m, g, mix = read(j)
            finish(name, at, m, g, mix, floor)
            return 0

        lax.fori_loop(0, count, write, 0, unroll=True)

    stores = []
    for k, (name, n) in enumerate(jobs):
        for one in loads[k]:
            one.wait()
        at = cuts(name, n)[0]
        if name == "down":

            def rows(j, _):
                here = cut(n * size + j * 32, 32, 32)
                there = cut(PART + n * size + j * 32, 32, 32)
                m = held["m_down"][here, :].astype(F32)
                g = held["total"][there, :].astype(F32)
                mix = blend(m, g)
                floor = 0.0625 * (jnp.mean(mix * mix, axis=1, keepdims=True) + 1e-06)
                finish("down", (here, whole), m, g, mix, floor)
                return 0

            lax.fori_loop(0, size // 32, rows, 0, unroll=True)
        elif name == "up":
            cols = pl.ds(n * size, size)
            column_job("up", cols, size, lambda j: held["total"][cut(j * 128, 128, 128), cols].astype(F32), 8)
        else:
            def grad(j):
                rows = cut(1024 + (j % 2) * PART, 128, 128)
                return held["total"][rows, cut((j // 2) * 256, 256, 256)].astype(F32)

            column_job("proj", pl.ds(0, 256), 256, grad, 8)
        for i, key in enumerate(("u_" + name, "r_" + name)):
            stores.append(pltpu.make_async_copy(kept[key].at[at], results[key].at[at], leave.at[k, i]))
            stores[-1].start()
        if k == 1:
            fetched.wait()
            passed.start()
    for one in stores:
        one.wait()
    passed.wait()


def lion(total, text, weights, moments):
    square = jax.ShapeDtypeStruct((1024, 1024), BF16)
    narrow = jax.ShapeDtypeStruct((1024, 256), BF16)
    outs = (square, square, narrow, square, square, narrow)
    return pl.pallas_call(
        lion_kernel,
        name="lion",
        out_shape=(*outs, jax.ShapeDtypeStruct(text.shape, F32)),
        in_specs=[ANY] * 8,
        out_specs=(ANY,) * 7,
        scratch_shapes=[pltpu.VMEM(*one) for one in LION.values()]
        + [pltpu.VMEM(one.shape, BF16) for one in outs]
        + [pltpu.VMEM(text.shape, F32)]
        + [pltpu.SemaphoreType.DMA((LION_JOBS, 4)), pltpu.SemaphoreType.DMA((LION_JOBS + 1, 2))],
        compiler_params=pltpu.CompilerParams(vmem_limit_bytes=60 * 2**20),
    )(total, text, *weights, *moments)


def per_device(
    vision_layer_entry,
    latent_preact_values,
    final_layer_result,
    caption_vectors_raw,
    sharpness_factor,
    offset_term,
    first_feedforward_matrix,
    second_feedforward_matrix,
    mapper_matrix,
    first_matrix_velocity,
    second_matrix_velocity,
    mapper_velocity,
):
    total, text_grad = step(
        sharpness_factor,
        offset_term,
        caption_vectors_raw,
        final_layer_result,
        mapper_matrix,
        latent_preact_values,
        second_feedforward_matrix,
        vision_layer_entry,
    )
    return lion(
        total,
        text_grad,
        (first_feedforward_matrix, second_feedforward_matrix, mapper_matrix),
        (first_matrix_velocity, second_matrix_velocity, mapper_velocity),
    )


def solution(mesh):
    return jax.shard_map(
        per_device,
        mesh=mesh,
        in_specs=(
            P("dp", None),
            P("dp", "mp"),
            P("dp", None),
            P(("dp", "mp"), None),
            P(),
            P(),
            P(None, "mp"),
            P("mp", None),
            P(None, "mp"),
            P(None, "mp"),
            P("mp", None),
            P(None, "mp"),
        ),
        out_specs=(
            P(None, "mp"),
            P("mp", None),
            P(None, "mp"),
            P(None, "mp"),
            P("mp", None),
            P(None, "mp"),
            P(("dp", "mp"), None),
        ),
        check_vma=False,
    )
```

```python
import types

import jax
import jax.numpy as jnp
from jax import lax
from jax.experimental import pallas as pl
from jax.experimental.pallas import tpu as pltpu
from jax.sharding import PartitionSpec as P

MESH = pl.DeviceIdType.MESH
F32 = jnp.float32
BF16 = jnp.bfloat16
VMEM = pl.BlockSpec(memory_space=pltpu.VMEM)
SMEM = pl.BlockSpec(memory_space=pltpu.SMEM)
ANY = pl.BlockSpec(memory_space=pl.ANY)

PART = 1152
STRIP = 288
TILE = 144
COPIES = 200
PLACE = (0, 1, 3, 2)


def nn(a, b):
    return jnp.dot(a, b, preferred_element_type=F32)


def nt(a, b):
    return lax.dot_general(a, b, (((1,), (1,)), ((), ())), preferred_element_type=F32)


def tn(a, b):
    return lax.dot_general(a, b, (((0,), (0,)), ((), ())), preferred_element_type=F32)


def cut(start, size, unit=16):
    return pl.ds(start if isinstance(start, int) else pl.multiple_of(start, unit), size)


def loop(count, body, size=256):
    def run(j, _):
        body(cut(j * size, size, size))
        return 0

    lax.fori_loop(0, count, run, 0)


def gelu_parts(value):
    slope = 0.7978845608028654
    square = value * value
    t = jnp.tanh(slope * (value + 0.044715 * (square * value)))
    cdf = 0.5 * (1.0 + t)
    derivative = cdf + 0.5 * value * (1.0 - t * t) * (slope * (1.0 + 3 * 0.044715 * square))
    return value * cdf, derivative


class Links:
    def __init__(self, send, recv):
        d = lax.axis_index("dp")
        m = lax.axis_index("mp")
        self.z, self.x, self.lo = d // 8, (d // 2) % 4, d % 2
        self.hi, self.core = m // 2, m % 2
        self.y = self.hi * 2 + self.lo
        self.send, self.recv = send, recv
        self.started = []
        self.sent = 0

    def at(self, z=0, x=0, y=0, core=0):
        row = (self.y + y) % 4
        dp = (((self.z + z) % 4) * 4 + (self.x + x) % 4) * 2 + row % 2
        return dp, (row // 2) * 2 + (self.core + core) % 2

    def copy(self, src, dst, to):
        k = len(self.started)
        assert k < COPIES
        one = pltpu.make_async_remote_copy(
            src_ref=src,
            dst_ref=dst,
            send_sem=self.send.at[k],
            recv_sem=self.recv.at[k],
            device_id=to,
            device_id_type=MESH,
        )
        one.start()
        self.started.append(one)
        return one

    def all_sent(self, until=None):
        until = len(self.started) if until is None else until
        for one in self.started[self.sent : until]:
            one.wait_send()
        self.sent = until


class RingSum:
    def __init__(self, links, src, block, far_in, near_in, on, off):
        self.links, self.src, self.block = links, src, block
        self.far_in, self.near_in, self.on, self.off = far_in, near_in, on, off
        self.half = far_in.shape[1]

    def part(self, k, i):
        return self.near_in.at[k, pl.ds(i * self.half, self.half)]

    def start(self):
        self.start_far()
        self.start_near()

    def start_far(self):
        copy, src, block = self.links.copy, self.src, self.block
        self.far = [
            copy(src.at[block(2, 0)], self.far_in.at[0], self.on),
            copy(src.at[block(2, 1)], self.far_in.at[1], self.off),
        ]

    def start_near(self):
        copy, src, block = self.links.copy, self.src, self.block
        self.near = [
            copy(src.at[block(1, 1)], self.part(0, 1), self.on),
            copy(src.at[block(3, 0)], self.part(1, 0), self.off),
        ]

    def middle(self):
        for i, k, to in ((0, 1, self.on), (1, 3, self.off)):
            self.far[i].wait_recv()
            at = self.block(k, i)
            self.src[at] = (self.src[at].astype(F32) + self.far_in[i].astype(F32)).astype(BF16)
            self.near.append(self.links.copy(self.src.at[at], self.part(i, i), to))

    def arrive(self):
        for one in self.near:
            one.wait_recv()

    def total(self, i, cols=None, near=slice(None)):
        rows = pl.ds(i * self.half, self.half)
        at = self.block(0, i)
        own = self.src[at] if cols is None else self.src[at[0], cols]
        return (
            own.astype(F32)
            + self.near_in[0, rows, near].astype(F32)
            + self.near_in[1, rows, near].astype(F32)
        )


def step_kernel(
    sharp,
    offset,
    caption_in,
    final_in,
    mapper_in,
    latent_in,
    second_in,
    entry_in,
    total_out,
    text_out,
    *scratch,
):
    r = types.SimpleNamespace(**dict(zip(SCRATCH, scratch)))
    caption, final, mapper = r.caption, r.final, r.own_mapper
    early = [
        pltpu.make_async_copy(src, dst, r.load.at[7 + k])
        for k, (src, dst) in enumerate(((caption_in, caption), (mapper_in, mapper), (final_in, final)))
    ]
    for one in early:
        one.start()
    net = Links(r.send, r.recv)
    hi, core = net.hi, net.core
    copy = net.copy
    sibling = net.at(core=1)
    z_on, z_off = net.at(z=1), net.at(z=3)
    x_on, x_off = net.at(x=1), net.at(x=3)
    y_on, y_off = net.at(y=1), net.at(y=3)
    across = net.at(y=2)
    pair_lo = net.at(y=1 - 2 * net.lo + 4)
    beside = net.at(y=2 * net.lo + 3)
    quarter = hi * 2 + core

    def rows_of(h, c):
        return cut(((h % 2) * 2 + c % 2) * 128, 128, 128)

    def cols_of(h, c):
        return cut(((h % 2) * 2 + c % 2) * 256, 256, 256)

    barrier = pltpu.get_barrier_semaphore()
    partners = [sibling, z_on, z_off, net.at(z=2), x_on, x_off, net.at(x=2), y_on, y_off, across]
    partners.append(net.at(y=2, core=1))
    for one in partners:
        pl.semaphore_signal(barrier, inc=1, device_id=one, device_id_type=MESH)
    loads = [
        pltpu.make_async_copy(src, dst, r.load.at[k])
        for k, (src, dst) in enumerate(
            ((latent_in, r.latent), (second_in, r.second), (entry_in, r.entry))
        )
    ]
    for one in loads:
        one.start()

    early[0].wait()
    raw = caption[...].astype(F32)
    text_scale = lax.rsqrt(jnp.sum(raw * raw, axis=1, keepdims=True) + 1e-06)
    unit = raw * text_scale
    r.text_scale[...] = text_scale
    r.text_unit[...] = unit
    unit = unit.astype(BF16)
    r.texts[0:64, :] = unit[0:64]
    r.texts[256:320, :] = unit[64:128]
    early[1].wait()
    r.mapper[:, cols_of(hi, core)] = mapper[...]
    early[2].wait()
    r.columns[...] = nn(final[...], mapper[...]).astype(BF16)
    r.embed[:, cols_of(hi, core)] = r.columns[rows_of(hi, core), :]
    pl.semaphore_wait(barrier, len(partners))

    def give(h, c, to):
        return copy(r.columns.at[rows_of(h, c)], r.embed.at[:, cols_of(hi, core)], to)

    embed_copies = [
        give(hi + 1, core, across),
        give(hi + 1, core + 1, net.at(y=2, core=1)),
        give(hi, core + 1, sibling),
    ]

    rings = (((y_on, y_off), (z_on, z_off)), ((z_on, z_off), (y_on, y_off)))

    def slot(half, s, p, part=None):
        start = PLACE[s] * 512 + half * 256 + p * 64
        return pl.ds(start, 64) if part is None else pl.ds(start + 32 * part, 32)

    got = {}

    def text_copy(half, src, dst, to, part=None):
        one = copy(r.texts.at[slot(half, *src, part)], r.texts.at[slot(half, *dst, part)], to)
        got.setdefault((half, dst), []).append(one)

    def arrived(half, s, p):
        for one in got[half, (s, p)]:
            one.wait_recv()

    def text_first(half):
        on, off = rings[half][0]
        text_copy(half, (0, 0), (0, 1), on)
        text_copy(half, (0, 0), (0, 3), off)

    def text_second(half, p):
        on, off = rings[half][1]
        text_copy(half, (0, p), (1, p), on)
        text_copy(half, (0, p), (3, p), off)

    def text_far_first(half):
        on, off = rings[half][0]
        text_copy(half, (0, 1), (0, 2), on, 0)
        text_copy(half, (0, 3), (0, 2), off, 1)

    def text_far_second(half, p):
        on, off = rings[half][1]
        text_copy(half, (1, p), (2, p), on, 0)
        text_copy(half, (3, p), (2, p), off, 1)

    halves = (0, 1)
    text_first(1)
    text_second(0, 0)
    text_first(0)
    text_second(1, 0)

    for one in embed_copies:
        one.wait_recv()
    wide = r.embed[...].astype(F32)
    image_scale = lax.rsqrt(jnp.sum(wide * wide, axis=1, keepdims=True) + 1e-06)
    unit = wide * image_scale
    r.images[0:128, :] = unit.astype(BF16)

    def image_slot(s, part=None):
        return pl.ds(s * 128, 128) if part is None else pl.ds(s * 128 + 64 * part, 64)

    def image_copy(src, dst, to, part=None):
        return copy(r.images.at[image_slot(src, part)], r.images.at[image_slot(dst, part)], to)

    image_on = [image_copy(0, 1, x_on, 0)]
    image_off = [image_copy(0, 3, x_off, 1)]
    image_on.append(image_copy(0, 1, x_on, 1))
    image_off.append(image_copy(0, 3, x_off, 0))
    shared = [image_copy(0, 4, sibling)]
    r.image_scale[...] = image_scale
    r.image_unit[...] = unit

    for half in (1, 0):
        arrived(half, 0, 1)
        arrived(half, 0, 3)
        text_far_first(half)
    for half in (0, 1):
        text_second(half, 1)
        text_second(half, 3)
    arrived(0, 1, 0)
    arrived(0, 3, 0)
    text_far_second(0, 0)
    image_on[0].wait_recv()
    image_far = [image_copy(1, 2, x_on, 0)]
    image_off[0].wait_recv()
    image_far.append(image_copy(3, 2, x_off, 1))
    for half in (1, 0):
        arrived(half, 0, 2)
        text_second(half, 2)
    arrived(1, 1, 0)
    arrived(1, 3, 0)
    text_far_second(1, 0)
    image_on[1].wait_recv()
    image_off[1].wait_recv()
    shared += [image_copy(1, 5, sibling), image_copy(3, 7, sibling)]

    loads[0].wait()

    def activate(cols):
        value, derivative = gelu_parts(r.latent[:, cols].astype(F32))
        r.active[:, cols] = value.astype(BF16)
        r.slope[:, cols] = derivative

    loop(4, activate)
    for one in image_far:
        one.wait_recv()
    shared.append(image_copy(2, 6, sibling))

    factor = sharp[0]
    shift = offset[0]

    def pair_weights(s, first=0, count=1024):
        texts = pl.ds(PLACE[s] * 512, 512)

        def chunk(rows):
            logits = factor * nt(r.images[rows, :], r.texts[texts, :]) + shift
            r.weights[rows, texts] = (factor / (1.0 + jnp.exp(-logits))).astype(BF16)

        def run(j, _):
            chunk(cut(first + j * 512, 512, 512))
            return 0

        if count == 512:
            chunk(pl.ds(first, 512))
        else:
            lax.fori_loop(0, 2, run, 0)

    def matching_pairs():
        for half in halves:
            rows = pl.ds(half * 64, 64)
            cols = pl.ds(half * 256, 128)
            logits = factor * nt(r.images[rows, :], r.texts[cols, :]) + shift
            hit = lax.broadcasted_iota(jnp.int32, (64, 128), 0) == lax.broadcasted_iota(
                jnp.int32, (64, 128), 1
            )
            label = jnp.where(hit, 1.0, -1.0)
            w = -label * factor / (1.0 + jnp.exp(label * logits))
            r.weights[rows, cols] = w.astype(BF16)

    near_texts = pl.ds(0, 1536)
    far_texts = pl.ds(1536, 512)

    def image_part(cols):
        r.image_dz[:, cols] = nn(r.weights[:, near_texts], r.texts[near_texts, cols])

    pair_weights(0, 0, 512)
    matching_pairs()
    for p in (1, 3):
        arrived(0, 1, p)
        arrived(0, 3, p)
        text_far_second(0, p)
    for one in shared:
        one.wait_recv()
    pair_weights(0, 512, 512)
    for p in (1, 3):
        arrived(1, 1, p)
        arrived(1, 3, p)
        text_far_second(1, p)
    for half in halves:
        arrived(half, 1, 2)
        arrived(half, 3, 2)
        text_far_second(half, 2)
    pair_weights(1)
    pair_weights(3)
    own_columns = r.mapper.at[:, cols_of(hi, core)]
    map_copies = [copy(own_columns, own_columns, beside), copy(own_columns, own_columns, sibling)]
    loop(2, image_part, 512)
    for p in range(4):
        for half in halves:
            arrived(half, 2, p)

    def last_sibling(cols):
        part = nn(r.weights[512:1024, far_texts], r.texts[far_texts, cols])
        r.cross_out[:, cols] = (part + r.image_dz[512:1024, cols]).astype(BF16)

    def last_own(cols):
        part = nn(r.weights[0:512, far_texts], r.texts[far_texts, cols])
        r.image_dz[0:512, cols] = part + r.image_dz[0:512, cols]

    pair_weights(2, 512, 512)
    loop(2, last_sibling, 512)
    cross = copy(r.cross_out, r.cross_in, sibling)
    pair_weights(2, 0, 512)
    loop(2, last_own, 512)
    cross.wait_recv()

    def image_ring(n):
        def block(k, i):
            return pl.ds(((4 - k) % 4) * 128 + n * 64 + i * 32, 32), slice(None)

        return RingSum(net, r.image_sum, block, r.image_far.at[n], r.image_near.at[n], x_on, x_off)

    image_rings = [image_ring(n) for n in (0, 1)]

    def image_total(s):
        rows = image_slot(s)
        r.image_sum[rows, :] = (r.image_dz[rows, :] + r.cross_in[rows, :].astype(F32)).astype(BF16)

    image_total(2)
    image_rings[0].start_far()
    image_total(1)
    image_total(3)
    image_rings[0].start_near()
    image_rings[1].start_far()
    image_total(0)

    def text_grads(half, *groups):
        for s in groups:
            rows = pl.ds(PLACE[s] * 512 + half * 256, 256)
            r.text_dz[rows, :] = tn(r.weights[:, rows], r.images[...]).astype(BF16)

    def second_ring(half):
        def block(k, i):
            return pl.ds(PLACE[(4 - k) % 4] * 512 + half * 256 + 128 * i, 128), slice(None)

        on, off = rings[half][1]
        return RingSum(net, r.text_dz, block, r.text_far.at[half], r.text_near.at[half], on, off)

    def first_ring(half):
        def block(k, i):
            return pl.ds(half * 256 + ((4 - k) % 4) * 64 + 32 * i, 32), slice(None)

        on, off = rings[half][0]
        return RingSum(net, r.text_sum, block, r.last_far.at[half], r.last_near.at[half], on, off)

    seconds = [second_ring(half) for half in halves]
    firsts = [first_ring(half) for half in halves]

    across_copies, beside_copies = [], []

    def image_finish(n):
        ring = image_rings[n]
        ring.arrive()
        rows = pl.ds(n * 64, 64)
        dz = jnp.concatenate([ring.total(0), ring.total(1)], axis=0)
        unit = r.image_unit[rows, :]
        grad = r.image_scale[rows, :] * (dz - unit * jnp.sum(unit * dz, axis=1, keepdims=True))
        mine = cut(quarter * 128 + n * 64, 64, 64)
        r.image_grad[mine, :] = grad.astype(BF16)
        block = r.image_grad.at[mine]
        across_copies.append(copy(block, block, across))
        beside_copies.append(copy(block, block, sibling))

    text_grads(0, 2, 1, 3)
    seconds[0].start()
    text_grads(1, 2)
    image_rings[0].middle()
    image_rings[1].start_near()
    text_grads(1, 1)
    image_rings[1].middle()
    text_grads(1, 3)
    image_finish(0)
    text_grads(0, 0)
    image_finish(1)
    text_grads(1, 0)

    map_copies[0].wait_recv()
    other_columns = r.mapper.at[:, cols_of(hi + 1, core)]
    map_copies.append(copy(other_columns, other_columns, sibling))
    seconds[0].middle()
    map_copies[1].wait_recv()
    map_copies[2].wait_recv()
    for one in beside_copies:
        one.wait_recv()

    def back_rows(h):
        rows = cut((h % 2) * 256, 256, 256)

        def part(cols):
            r.back[rows, cols] = nt(r.image_grad[rows, :], r.mapper[cols, :]).astype(BF16)

        loop(2, part, 512)

    back_rows(hi)
    here, there = cut(hi * 256, 256, 256), cut((1 - hi) * 256, 256, 256)
    own_cols = cols_of(hi, core)

    def proj_here(cols):
        r.image_dz[cols, 512:768] = tn(final[here, cols], r.image_grad[here, own_cols])

    def down_here(cols):
        r.image_dz[cols, 0:512] = tn(r.active[here, cols], r.back[here, 0:512])

    loop(2, proj_here, 512)
    loop(2, down_here, 512)
    passed = []
    for n in (0, 1):
        across_copies[n].wait_recv()
        block = r.image_grad.at[cut(((1 - hi) * 2 + core) * 128 + n * 64, 64, 64)]
        passed.append(copy(block, block, sibling))
    seconds[1].start()
    for one in passed:
        one.wait_recv()
    back_rows(hi + 1)

    first = (net.x, net.z)
    other = (net.z, net.x)
    along = ((x_on, x_off), (z_on, z_off))
    wide = (pl.ds(0, 512), pl.ds(512, 512))

    def strip_rows(part, k, i=None):
        start = part * PART + ((first[part] + k) % 4) * STRIP
        return cut(start, STRIP) if i is None else cut(start + i * TILE, TILE)

    def side_columns(part, c, k):
        return cut(c * 512 + ((other[part] + k) % 4) * 128, 128, 128)

    def grad_ring(part, c):
        def block(k, i):
            return strip_rows(part, k, i), wide[c]

        n = part * 2 + c
        return RingSum(net, r.grads, block, r.grad_far.at[n], r.grad_near.at[n], *along[part])

    chains = ((1, 0), (1, 1), (0, 0), (0, 1))
    grad_rings = {chain: grad_ring(*chain) for chain in chains}

    def proj_part(cols):
        value = tn(final[there, cols], r.image_grad[there, own_cols])
        value = (value + r.image_dz[cols, 512:768]).astype(BF16)
        r.grads[1024:1152, cols] = value[0:128]
        r.grads[2176:2304, cols] = value[128:256]

    def down(c):
        def part(j, _):
            cols = cut(j * 512, 512, 512)
            if c == 0:
                value = tn(r.active[there, cols], r.back[there, wide[c]]) + r.image_dz[cols, 0:512]
            else:
                value = tn(r.active[:, cols], r.back[:, wide[c]])
            r.grads[cut(PART + j * 512, 512, 128), wide[c]] = value.astype(BF16)
            return 0

        lax.fori_loop(0, 2, part, 0)

    def up(c):
        value = nt(r.back[...], r.second[wide[c], :]) * r.slope[:, wide[c]]
        r.pre[:, wide[c]] = value.astype(BF16)

        def part(rows):
            r.grads[rows, wide[c]] = tn(r.entry[:, rows], r.pre[:, wide[c]]).astype(BF16)

        loop(2, part, 512)

    loop(4, proj_part)
    down(0)
    grad_rings[1, 0].start()
    loads[1].wait()
    loads[2].wait()
    up(0)
    grad_rings[0, 0].start()
    down(1)
    grad_rings[1, 0].middle()
    grad_rings[1, 1].start_far()
    up(1)
    grad_rings[0, 0].middle()
    grad_rings[0, 1].start_far()

    def text_first_sum(half):
        seconds[half].arrive()
        for i in (0, 1):
            r.text_sum[pl.ds(half * 256 + 128 * i, 128), :] = seconds[half].total(i).astype(BF16)
        firsts[half].start()

    seconds[1].middle()
    text_first_sum(0)

    def side_to(part, k):
        return net.at(z=k) if part == 0 else net.at(x=k)

    sides = {}

    def side(part, c):
        ring = grad_rings[part, c]
        ring.arrive()
        sides[part, c] = []
        for n, k in enumerate((2, 1, 3, 0)):
            cols = side_columns(part, c, k)
            near = cut(((other[part] + k) % 4) * 128, 128, 128)
            for i in (0, 1):
                rows = pl.ds(i * TILE, TILE)
                total = ring.total(i, cols, near)
                if k == 0:
                    r.strip[part, rows, wide_tile[c]] = total
                else:
                    r.side_out[part, n, rows, wide_tile[c]] = total.astype(BF16)
            if k:
                sides[part, c].append(
                    copy(
                        r.side_out.at[part, n, :, wide_tile[c]],
                        r.side_in.at[part, n, :, wide_tile[c]],
                        side_to(part, k),
                    )
                )

    wide_tile = (pl.ds(0, 128), pl.ds(128, 128))
    side(1, 0)
    grad_rings[0, 1].start_near()
    side(0, 0)
    grad_rings[1, 1].start_near()
    grad_rings[1, 1].middle()
    grad_rings[0, 1].middle()
    firsts[0].middle()

    kept = cut(net.lo * TILE, TILE)
    given = cut((1 - net.lo) * TILE, TILE)
    tiles = {}

    def tile(part, c):
        for one in sides[part, c]:
            one.wait_recv()
        at = wide_tile[c]

        def total(rows):
            value = r.strip[part, rows, at]
            for n in range(3):
                value = value + r.side_in[part, n, rows, at].astype(F32)
            return value

        r.tile_out[part, :, at] = total(given).astype(BF16)
        tiles[part, c] = copy(r.tile_out.at[part, :, at], r.tile_in.at[part, :, at], pair_lo)
        r.tile[part, :, at] = total(kept)

    spread_tile = {}

    def back_tile(part, c):
        tiles[part, c].wait_recv()
        at = wide_tile[c]
        rows = cut(part * PART + first[part] * STRIP + net.lo * TILE, TILE)
        cols = side_columns(part, c, 0)
        r.done[rows, cols] = (r.tile[part, :, at] + r.tile_in[part, :, at].astype(F32)).astype(BF16)
        block = r.done.at[rows, cols]
        spread_tile[part, c] = copy(block, block, pair_lo)

    spread_side = {}

    def back_side(part, c):
        spread_tile[part, c].wait_recv()
        block = r.done.at[strip_rows(part, 0), side_columns(part, c, 0)]
        spread_side[part, c] = [copy(block, block, side_to(part, k)) for k in (2, 1, 3)]

    spread_strip = {}

    def back_strip(part, c):
        for one in spread_side[part, c]:
            one.wait_recv()
        on, off = along[part]
        spread_strip[part, c] = []
        for i, to in ((0, on), (1, off), (1, on), (0, off)):
            block = r.done.at[strip_rows(part, 0, i), wide[c]]
            spread_strip[part, c].append(copy(block, block, to))

    last = []

    def back_far(part, c):
        on, off = along[part]
        for i, k, to in ((0, 3, on), (1, 1, off)):
            spread_strip[part, c][i].wait_recv()
            block = r.done.at[strip_rows(part, k, i), wide[c]]
            last.append(copy(block, block, to))

    tile(1, 0)
    tile(0, 0)
    back_tile(1, 0)
    text_first_sum(1)
    side(1, 1)
    back_tile(0, 0)
    side(0, 1)
    back_side(1, 0)
    back_side(0, 0)
    firsts[1].middle()
    tile(1, 1)
    tile(0, 1)
    before = len(net.started)
    back_strip(1, 0)
    back_strip(0, 0)
    back_tile(1, 1)
    back_tile(0, 1)
    back_side(1, 1)
    back_side(0, 1)
    back_far(1, 0)
    back_far(0, 0)
    back_strip(1, 1)
    back_strip(0, 1)

    for half in halves:
        firsts[half].arrive()
    dz = jnp.concatenate([firsts[half].total(i) for half in halves for i in (0, 1)], axis=0)
    unit = r.text_unit[...]
    text_out[...] = r.text_scale[...] * (dz - unit * jnp.sum(unit * dz, axis=1, keepdims=True))

    net.all_sent(before)
    back_far(1, 1)
    back_far(0, 1)
    outs = []
    for n, (part, c) in enumerate(((1, 0), (0, 0), (1, 1), (0, 1))):
        for one in spread_strip[part, c][2:] + last[2 * n : 2 * n + 2]:
            one.wait_recv()
        block = (pl.ds(part * PART, PART), wide[c])
        outs.append(pltpu.make_async_copy(r.done.at[block], total_out.at[block], r.load.at[3 + n]))
        outs[-1].start()
    net.all_sent()
    for one in outs:
        one.wait()


SCRATCH = dict(
    caption=((128, 1024), BF16),
    final=((512, 1024), BF16),
    own_mapper=((1024, 256), BF16),
    columns=((512, 256), BF16),
    texts=((2048, 1024), BF16),
    text_unit=((128, 1024), F32),
    text_scale=((128, 1), F32),
    embed=((128, 1024), BF16),
    image_unit=((128, 1024), F32),
    image_scale=((128, 1), F32),
    images=((1024, 1024), BF16),
    mapper=((1024, 1024), BF16),
    latent=((512, 1024), BF16),
    second=((1024, 1024), BF16),
    entry=((512, 1024), BF16),
    active=((512, 1024), BF16),
    slope=((512, 1024), F32),
    weights=((1024, 2048), BF16),
    image_dz=((1024, 1024), F32),
    cross_out=((512, 1024), BF16),
    cross_in=((512, 1024), BF16),
    image_sum=((512, 1024), BF16),
    image_far=((2, 2, 32, 1024), BF16),
    image_near=((2, 2, 64, 1024), BF16),
    text_dz=((2048, 1024), BF16),
    text_far=((2, 2, 128, 1024), BF16),
    text_near=((2, 2, 256, 1024), BF16),
    text_sum=((512, 1024), BF16),
    last_far=((2, 2, 32, 1024), BF16),
    last_near=((2, 2, 64, 1024), BF16),
    image_grad=((512, 1024), BF16),
    back=((512, 1024), BF16),
    pre=((512, 1024), BF16),
    grads=((2 * PART, 1024), BF16),
    done=((2 * PART, 1024), BF16),
    grad_far=((4, 2, TILE, 512), BF16),
    grad_near=((4, 2, STRIP, 512), BF16),
    strip=((2, STRIP, 256), F32),
    side_out=((2, 3, STRIP, 256), BF16),
    side_in=((2, 3, STRIP, 256), BF16),
    tile=((2, TILE, 256), F32),
    tile_out=((2, TILE, 256), BF16),
    tile_in=((2, TILE, 256), BF16),
    send=((COPIES,), None),
    recv=((COPIES,), None),
    load=((10,), None),
)


def step(sharp, offset, caption, final, mapper, latent, second, entry):
    return pl.pallas_call(
        step_kernel,
        name="pairs_and_weight_grads",
        out_shape=(
            jax.ShapeDtypeStruct((2 * PART, 1024), BF16),
            jax.ShapeDtypeStruct((128, 1024), F32),
        ),
        in_specs=[SMEM, SMEM] + [ANY] * 6,
        out_specs=(ANY, VMEM),
        scratch_shapes=[
            pltpu.SemaphoreType.DMA(shape) if kind is None else pltpu.VMEM(shape, kind)
            for shape, kind in SCRATCH.values()
        ],
        compiler_params=pltpu.CompilerParams(
            collective_id=0, has_side_effects=True, vmem_limit_bytes=60 * 2**20
        ),
    )(sharp, offset, caption, final, mapper, latent, second, entry)


LION = dict(
    total=((2 * PART, 1024), BF16),
    w_up=((1024, 1024), BF16),
    w_down=((1024, 1024), BF16),
    w_proj=((1024, 256), BF16),
    m_up=((1024, 1024), BF16),
    m_down=((1024, 1024), BF16),
    m_proj=((1024, 256), BF16),
)
LION_OUT = ("u_up", "u_down", "u_proj", "r_up", "r_down", "r_proj")


def lion_kernel(
    total, text, w_up, w_down, w_proj, m_up, m_down, m_proj,
    u_up, u_down, u_proj, r_up, r_down, r_proj, text_out, *scratch,
):
    held = dict(zip(LION, scratch))
    kept = dict(zip(LION_OUT, scratch[len(LION) :]))
    arrive, leave = scratch[-2:]
    given = dict(
        total=total, w_up=w_up, w_down=w_down, w_proj=w_proj, m_up=m_up, m_down=m_down, m_proj=m_proj
    )
    results = dict(u_up=u_up, u_down=u_down, u_proj=u_proj, r_up=r_up, r_down=r_down, r_proj=r_proj)
    whole = slice(None)

    grads = dict(
        down=[(pl.ds(PART, 1024), whole)],
        up=[(pl.ds(0, 1024), whole)],
        proj=[(pl.ds(1024, 128), whole), (pl.ds(PART + 1024, 128), whole)],
    )
    jobs = ("proj", "down", "up")
    loads = []
    for k, name in enumerate(jobs):
        mine = [("w_" + name, (whole, whole)), ("m_" + name, (whole, whole))]
        mine += [("total", one) for one in grads[name]]
        loads.append(
            [
                pltpu.make_async_copy(given[key].at[part], held[key].at[part], arrive.at[k, i])
                for i, (key, part) in enumerate(mine)
            ]
        )
    fetched = pltpu.make_async_copy(text, scratch[-3], leave.at[3, 0])
    passed = pltpu.make_async_copy(scratch[-3], text_out, leave.at[3, 1])
    for one in loads[0] + loads[1] + [fetched]:
        one.start()
    for job in loads[2:]:
        for one in job:
            one.start()

    def blend(m, g):
        return 0.9 * m + 0.1 * g

    def finish(name, at, m, g, mix, floor):
        w = held["w_" + name][at].astype(F32)
        kept["u_" + name][at] = (mix * lax.rsqrt(mix * mix + floor) + w).astype(BF16)
        kept["r_" + name][at] = (0.99 * m + 0.01 * g).astype(BF16)

    def column_job(name, cols, width, grad, count):
        def read(j):
            at = (cut(j * 128, 128, 128), cols)
            g = grad(j)
            m = held["m_" + name][at].astype(F32)
            return at, m, g, blend(m, g)

        def add(j, acc):
            mix = read(j)[3]
            return acc + jnp.sum((mix * mix).reshape(16, 8, width), axis=0)

        acc = lax.fori_loop(0, count, add, jnp.zeros((8, width), F32), unroll=True)
        floor = 0.0625 * (jnp.sum(acc, axis=0, keepdims=True) * (1.0 / 1024) + 1e-06)

        for j in range(count):
            at, m, g, mix = read(j)
            finish(name, at, m, g, mix, floor)

    stores = []

    def send(name, quarter=None):
        n = LION_OUT.index("u_" + name)
        at = (whole, whole) if quarter is None else (pl.ds(quarter * 256, 256), whole)
        if name == "up":
            at = at[::-1]
        for i, key in enumerate(("u_" + name, "r_" + name)):
            sem = leave.at[n, 2 * (quarter or 0) + i]
            stores.append(pltpu.make_async_copy(kept[key].at[at], results[key].at[at], sem))
            stores[-1].start()

    for k, name in enumerate(jobs):
        for one in loads[k]:
            one.wait()
        if name == "down":

            def rows(j, _):
                here = cut(j * 32, 32, 32)
                m = held["m_down"][here, :].astype(F32)
                g = held["total"][cut(PART + j * 32, 32, 32), :].astype(F32)
                mix = blend(m, g)
                floor = 0.0625 * (jnp.mean(mix * mix, axis=1, keepdims=True) + 1e-06)
                finish("down", (here, whole), m, g, mix, floor)
                return 0

            for quarter in range(4):
                lax.fori_loop(quarter * 8, quarter * 8 + 8, rows, 0, unroll=True)
                send("down", quarter)
            fetched.wait()
            passed.start()
        elif name == "up":
            for quarter in range(4):
                cols = pl.ds(quarter * 256, 256)
                column_job(
                    "up", cols, 256, lambda j: held["total"][cut(j * 128, 128, 128), cols].astype(F32), 8
                )
                send("up", quarter)
        else:
            def grad(j):
                rows = cut(1024 + (j % 2) * PART, 128, 128)
                return held["total"][rows, cut((j // 2) * 256, 256, 256)].astype(F32)

            column_job("proj", pl.ds(0, 256), 256, grad, 8)
            send("proj")
    for one in stores:
        one.wait()
    passed.wait()


def lion(total, text, weights, moments):
    square = jax.ShapeDtypeStruct((1024, 1024), BF16)
    narrow = jax.ShapeDtypeStruct((1024, 256), BF16)
    outs = (square, square, narrow, square, square, narrow)
    return pl.pallas_call(
        lion_kernel,
        name="lion",
        out_shape=(*outs, jax.ShapeDtypeStruct(text.shape, F32)),
        in_specs=[ANY] * 8,
        out_specs=(ANY,) * 7,
        scratch_shapes=[pltpu.VMEM(*one) for one in LION.values()]
        + [pltpu.VMEM(one.shape, BF16) for one in outs]
        + [pltpu.VMEM(text.shape, F32)]
        + [pltpu.SemaphoreType.DMA((3, 4)), pltpu.SemaphoreType.DMA((4, 8))],
        compiler_params=pltpu.CompilerParams(vmem_limit_bytes=60 * 2**20),
    )(total, text, *weights, *moments)


def per_device(
    vision_layer_entry,
    latent_preact_values,
    final_layer_result,
    caption_vectors_raw,
    sharpness_factor,
    offset_term,
    first_feedforward_matrix,
    second_feedforward_matrix,
    mapper_matrix,
    first_matrix_velocity,
    second_matrix_velocity,
    mapper_velocity,
):
    total, text_grad = step(
        sharpness_factor,
        offset_term,
        caption_vectors_raw,
        final_layer_result,
        mapper_matrix,
        latent_preact_values,
        second_feedforward_matrix,
        vision_layer_entry,
    )
    return lion(
        total,
        text_grad,
        (first_feedforward_matrix, second_feedforward_matrix, mapper_matrix),
        (first_matrix_velocity, second_matrix_velocity, mapper_velocity),
    )


def solution(mesh):
    return jax.shard_map(
        per_device,
        mesh=mesh,
        in_specs=(
            P("dp", None),
            P("dp", "mp"),
            P("dp", None),
            P(("dp", "mp"), None),
            P(),
            P(),
            P(None, "mp"),
            P("mp", None),
            P(None, "mp"),
            P(None, "mp"),
            P("mp", None),
            P(None, "mp"),
        ),
        out_specs=(
            P(None, "mp"),
            P("mp", None),
            P(None, "mp"),
            P(None, "mp"),
            P("mp", None),
            P(None, "mp"),
            P(("dp", "mp"), None),
        ),
        check_vma=False,
    )
```

```python
import types

import jax
import jax.numpy as jnp
from jax import lax
from jax.experimental import pallas as pl
from jax.experimental.pallas import tpu as pltpu
from jax.sharding import PartitionSpec as P

MESH = pl.DeviceIdType.MESH
F32 = jnp.float32
BF16 = jnp.bfloat16
VMEM = pl.BlockSpec(memory_space=pltpu.VMEM)
SMEM = pl.BlockSpec(memory_space=pltpu.SMEM)
ANY = pl.BlockSpec(memory_space=pl.ANY)

PART = 1152
STRIP = 288
TILE = 144
COPIES = 200
PLACE = (0, 1, 3, 2)


def nn(a, b):
    return jnp.dot(a, b, preferred_element_type=F32)


def nt(a, b):
    return lax.dot_general(a, b, (((1,), (1,)), ((), ())), preferred_element_type=F32)


def tn(a, b):
    return lax.dot_general(a, b, (((0,), (0,)), ((), ())), preferred_element_type=F32)


def cut(start, size, unit=16):
    return pl.ds(start if isinstance(start, int) else pl.multiple_of(start, unit), size)


def loop(count, body, size=256):
    def run(j, _):
        body(cut(j * size, size, size))
        return 0

    lax.fori_loop(0, count, run, 0)


def gelu_parts(value):
    slope = 0.7978845608028654
    square = value * value
    t = jnp.tanh(slope * (value + 0.044715 * (square * value)))
    cdf = 0.5 * (1.0 + t)
    derivative = cdf + 0.5 * value * (1.0 - t * t) * (slope * (1.0 + 3 * 0.044715 * square))
    return value * cdf, derivative


class Links:
    def __init__(self, send, recv):
        d = lax.axis_index("dp")
        m = lax.axis_index("mp")
        self.z, self.x, self.lo = d // 8, (d // 2) % 4, d % 2
        self.hi, self.core = m // 2, m % 2
        self.y = self.hi * 2 + self.lo
        self.send, self.recv = send, recv
        self.started = []
        self.sent = 0

    def at(self, z=0, x=0, y=0, core=0):
        row = (self.y + y) % 4
        dp = (((self.z + z) % 4) * 4 + (self.x + x) % 4) * 2 + row % 2
        return dp, (row // 2) * 2 + (self.core + core) % 2

    def copy(self, src, dst, to):
        k = len(self.started)
        assert k < COPIES
        one = pltpu.make_async_remote_copy(
            src_ref=src,
            dst_ref=dst,
            send_sem=self.send.at[k],
            recv_sem=self.recv.at[k],
            device_id=to,
            device_id_type=MESH,
        )
        one.start()
        self.started.append(one)
        return one

    def all_sent(self, until=None):
        until = len(self.started) if until is None else until
        for one in self.started[self.sent : until]:
            one.wait_send()
        self.sent = until


class RingSum:
    def __init__(self, links, src, block, far_in, near_in, on, off):
        self.links, self.src, self.block = links, src, block
        self.far_in, self.near_in, self.on, self.off = far_in, near_in, on, off
        self.half = far_in.shape[1]

    def part(self, k, i):
        return self.near_in.at[k, pl.ds(i * self.half, self.half)]

    def start(self):
        self.start_far()
        self.start_near()

    def start_far(self):
        copy, src, block = self.links.copy, self.src, self.block
        self.far = [
            copy(src.at[block(2, 0)], self.far_in.at[0], self.on),
            copy(src.at[block(2, 1)], self.far_in.at[1], self.off),
        ]

    def start_near(self):
        copy, src, block = self.links.copy, self.src, self.block
        self.near = [
            copy(src.at[block(1, 1)], self.part(0, 1), self.on),
            copy(src.at[block(3, 0)], self.part(1, 0), self.off),
        ]

    def middle(self):
        for i, k, to in ((0, 1, self.on), (1, 3, self.off)):
            self.far[i].wait_recv()
            at = self.block(k, i)
            self.src[at] = (self.src[at].astype(F32) + self.far_in[i].astype(F32)).astype(BF16)
            self.near.append(self.links.copy(self.src.at[at], self.part(i, i), to))

    def arrive(self):
        for one in self.near:
            one.wait_recv()

    def total(self, i, cols=None, near=slice(None)):
        rows = pl.ds(i * self.half, self.half)
        at = self.block(0, i)
        own = self.src[at] if cols is None else self.src[at[0], cols]
        return (
            own.astype(F32)
            + self.near_in[0, rows, near].astype(F32)
            + self.near_in[1, rows, near].astype(F32)
        )


def step_kernel(
    sharp,
    offset,
    caption_in,
    final_in,
    mapper_in,
    latent_in,
    second_in,
    entry_in,
    total_out,
    text_out,
    *scratch,
):
    r = types.SimpleNamespace(**dict(zip(SCRATCH, scratch)))
    caption, final, mapper = r.caption, r.final, r.own_mapper
    early = [
        pltpu.make_async_copy(src, dst, r.load.at[7 + k])
        for k, (src, dst) in enumerate(((caption_in, caption), (mapper_in, mapper), (final_in, final)))
    ]
    for one in early:
        one.start()
    net = Links(r.send, r.recv)
    hi, core = net.hi, net.core
    copy = net.copy
    sibling = net.at(core=1)
    z_on, z_off = net.at(z=1), net.at(z=3)
    x_on, x_off = net.at(x=1), net.at(x=3)
    y_on, y_off = net.at(y=1), net.at(y=3)
    across = net.at(y=2)
    pair_lo = net.at(y=1 - 2 * net.lo + 4)
    beside = net.at(y=2 * net.lo + 3)
    quarter = hi * 2 + core

    def rows_of(h, c):
        return cut(((h % 2) * 2 + c % 2) * 128, 128, 128)

    def cols_of(h, c):
        return cut(((h % 2) * 2 + c % 2) * 256, 256, 256)

    barrier = pltpu.get_barrier_semaphore()
    partners = [sibling, z_on, z_off, net.at(z=2), x_on, x_off, net.at(x=2), y_on, y_off, across]
    partners.append(net.at(y=2, core=1))
    for one in partners:
        pl.semaphore_signal(barrier, inc=1, device_id=one, device_id_type=MESH)
    loads = [
        pltpu.make_async_copy(src, dst, r.load.at[k])
        for k, (src, dst) in enumerate(
            ((latent_in, r.latent), (second_in, r.second), (entry_in, r.entry))
        )
    ]
    for one in loads:
        one.start()

    early[0].wait()
    raw = caption[...].astype(F32)
    text_scale = lax.rsqrt(jnp.sum(raw * raw, axis=1, keepdims=True) + 1e-06)
    unit = raw * text_scale
    r.text_scale[...] = text_scale
    r.text_unit[...] = unit
    unit = unit.astype(BF16)
    r.texts[0:64, :] = unit[0:64]
    r.texts[256:320, :] = unit[64:128]
    early[1].wait()
    r.mapper[:, cols_of(hi, core)] = mapper[...]
    early[2].wait()
    r.columns[...] = nn(final[...], mapper[...]).astype(BF16)
    r.embed[:, cols_of(hi, core)] = r.columns[rows_of(hi, core), :]
    pl.semaphore_wait(barrier, len(partners))

    def give(h, c, to):
        return copy(r.columns.at[rows_of(h, c)], r.embed.at[:, cols_of(hi, core)], to)

    embed_copies = [
        give(hi + 1, core, across),
        give(hi + 1, core + 1, net.at(y=2, core=1)),
        give(hi, core + 1, sibling),
    ]

    rings = (((y_on, y_off), (z_on, z_off)), ((z_on, z_off), (y_on, y_off)))

    def slot(half, s, p, part=None):
        start = PLACE[s] * 512 + half * 256 + p * 64
        return pl.ds(start, 64) if part is None else pl.ds(start + 32 * part, 32)

    got = {}

    def text_copy(half, src, dst, to, part=None):
        one = copy(r.texts.at[slot(half, *src, part)], r.texts.at[slot(half, *dst, part)], to)
        got.setdefault((half, dst), []).append(one)

    def arrived(half, s, p):
        for one in got[half, (s, p)]:
            one.wait_recv()

    def text_first(half):
        on, off = rings[half][0]
        text_copy(half, (0, 0), (0, 1), on)
        text_copy(half, (0, 0), (0, 3), off)

    def text_second(half, p):
        on, off = rings[half][1]
        text_copy(half, (0, p), (1, p), on)
        text_copy(half, (0, p), (3, p), off)

    def text_far_first(half):
        on, off = rings[half][0]
        text_copy(half, (0, 1), (0, 2), on, 0)
        text_copy(half, (0, 3), (0, 2), off, 1)

    def text_far_second(half, p):
        on, off = rings[half][1]
        text_copy(half, (1, p), (2, p), on, 0)
        text_copy(half, (3, p), (2, p), off, 1)

    halves = (0, 1)
    text_first(1)
    text_second(0, 0)
    text_first(0)
    text_second(1, 0)

    for one in embed_copies:
        one.wait_recv()
    wide = r.embed[...].astype(F32)
    image_scale = lax.rsqrt(jnp.sum(wide * wide, axis=1, keepdims=True) + 1e-06)
    unit = wide * image_scale
    r.images[0:128, :] = unit.astype(BF16)

    def image_slot(s, part=None):
        return pl.ds(s * 128, 128) if part is None else pl.ds(s * 128 + 64 * part, 64)

    def image_copy(src, dst, to, part=None):
        return copy(r.images.at[image_slot(src, part)], r.images.at[image_slot(dst, part)], to)

    image_on = [image_copy(0, 1, x_on, 0)]
    image_off = [image_copy(0, 3, x_off, 1)]
    image_on.append(image_copy(0, 1, x_on, 1))
    image_off.append(image_copy(0, 3, x_off, 0))
    shared = [image_copy(0, 4, sibling)]
    r.image_scale[...] = image_scale
    r.image_unit[...] = unit

    for half in (1, 0):
        arrived(half, 0, 1)
        arrived(half, 0, 3)
        text_far_first(half)
    for half in (0, 1):
        text_second(half, 1)
        text_second(half, 3)
    arrived(0, 1, 0)
    arrived(0, 3, 0)
    text_far_second(0, 0)
    image_on[0].wait_recv()
    image_far = [image_copy(1, 2, x_on, 0)]
    image_off[0].wait_recv()
    image_far.append(image_copy(3, 2, x_off, 1))
    for half in (1, 0):
        arrived(half, 0, 2)
        text_second(half, 2)
    arrived(1, 1, 0)
    arrived(1, 3, 0)
    text_far_second(1, 0)
    image_on[1].wait_recv()
    image_off[1].wait_recv()
    shared += [image_copy(1, 5, sibling), image_copy(3, 7, sibling)]

    loads[0].wait()

    def activate(cols):
        value, derivative = gelu_parts(r.latent[:, cols].astype(F32))
        r.active[:, cols] = value.astype(BF16)
        r.slope[:, cols] = derivative

    loop(4, activate)
    for one in image_far:
        one.wait_recv()
    shared.append(image_copy(2, 6, sibling))

    factor = sharp[0]
    shift = offset[0]

    def pair_weights(s, first=0, count=1024, width=512):
        texts = pl.ds(PLACE[s] * 512, width)

        def chunk(rows):
            logits = factor * nt(r.images[rows, :], r.texts[texts, :]) + shift
            r.weights[rows, texts] = (factor / (1.0 + jnp.exp(-logits))).astype(BF16)

        def run(j, _):
            chunk(cut(first + j * 512, 512, 512))
            return 0

        if count == 512:
            chunk(pl.ds(first, 512))
        else:
            lax.fori_loop(0, 2, run, 0)

    def matching_pairs():
        for half in halves:
            rows = pl.ds(half * 64, 64)
            cols = pl.ds(half * 256, 128)
            logits = factor * nt(r.images[rows, :], r.texts[cols, :]) + shift
            hit = lax.broadcasted_iota(jnp.int32, (64, 128), 0) == lax.broadcasted_iota(
                jnp.int32, (64, 128), 1
            )
            label = jnp.where(hit, 1.0, -1.0)
            w = -label * factor / (1.0 + jnp.exp(label * logits))
            r.weights[rows, cols] = w.astype(BF16)

    near_texts = pl.ds(0, 1536)
    far_texts = pl.ds(1536, 512)

    def image_part(cols):
        r.image_dz[:, cols] = nn(r.weights[:, near_texts], r.texts[near_texts, cols])

    pair_weights(0, 0, 512)
    matching_pairs()
    for p in (1, 3):
        arrived(0, 1, p)
        arrived(0, 3, p)
        text_far_second(0, p)
    for one in shared:
        one.wait_recv()
    pair_weights(0, 512, 512)
    for p in (1, 3):
        arrived(1, 1, p)
        arrived(1, 3, p)
        text_far_second(1, p)
    for half in halves:
        arrived(half, 1, 2)
        arrived(half, 3, 2)
        text_far_second(half, 2)
    pair_weights(1, width=1024)
    own_columns = r.mapper.at[:, cols_of(hi, core)]
    map_copies = [copy(own_columns, own_columns, beside), copy(own_columns, own_columns, sibling)]
    loop(2, image_part, 512)
    for p in range(4):
        for half in halves:
            arrived(half, 2, p)

    def last_sibling(cols):
        part = nn(r.weights[512:1024, far_texts], r.texts[far_texts, cols])
        r.cross_out[:, cols] = (part + r.image_dz[512:1024, cols]).astype(BF16)

    def last_own(cols):
        part = nn(r.weights[0:512, far_texts], r.texts[far_texts, cols])
        r.image_dz[0:512, cols] = part + r.image_dz[0:512, cols]

    pair_weights(2, 512, 512)
    loop(2, last_sibling, 512)
    cross = copy(r.cross_out, r.cross_in, sibling)
    pair_weights(2, 0, 512)
    loop(2, last_own, 512)
    cross.wait_recv()

    def image_ring(n):
        def block(k, i):
            return pl.ds(((4 - k) % 4) * 128 + n * 64 + i * 32, 32), slice(None)

        return RingSum(net, r.image_sum, block, r.image_far.at[n], r.image_near.at[n], x_on, x_off)

    image_rings = [image_ring(n) for n in (0, 1)]

    def image_total(s):
        rows = image_slot(s)
        r.image_sum[rows, :] = (r.image_dz[rows, :] + r.cross_in[rows, :].astype(F32)).astype(BF16)

    image_total(2)
    image_rings[0].start_far()
    image_total(1)
    image_total(3)
    image_rings[0].start_near()
    image_rings[1].start_far()
    image_total(0)

    def text_grads(half, *groups):
        for s in groups:
            rows = pl.ds(PLACE[s] * 512 + half * 256, 256)
            r.text_dz[rows, :] = tn(r.weights[:, rows], r.images[...]).astype(BF16)

    def second_ring(half):
        def block(k, i):
            return pl.ds(PLACE[(4 - k) % 4] * 512 + half * 256 + 128 * i, 128), slice(None)

        on, off = rings[half][1]
        return RingSum(net, r.text_dz, block, r.text_far.at[half], r.text_near.at[half], on, off)

    def first_ring(half):
        def block(k, i):
            return pl.ds(half * 256 + ((4 - k) % 4) * 64 + 32 * i, 32), slice(None)

        on, off = rings[half][0]
        return RingSum(net, r.text_sum, block, r.last_far.at[half], r.last_near.at[half], on, off)

    seconds = [second_ring(half) for half in halves]
    firsts = [first_ring(half) for half in halves]

    across_copies, beside_copies = [], []

    def image_finish(n):
        ring = image_rings[n]
        ring.arrive()
        rows = pl.ds(n * 64, 64)
        dz = jnp.concatenate([ring.total(0), ring.total(1)], axis=0)
        unit = r.image_unit[rows, :]
        grad = r.image_scale[rows, :] * (dz - unit * jnp.sum(unit * dz, axis=1, keepdims=True))
        mine = cut(quarter * 128 + n * 64, 64, 64)
        r.image_grad[mine, :] = grad.astype(BF16)
        block = r.image_grad.at[mine]
        across_copies.append(copy(block, block, across))
        beside_copies.append(copy(block, block, sibling))

    text_grads(0, 2, 1, 3)
    seconds[0].start()
    text_grads(1, 2)
    image_rings[0].middle()
    image_rings[1].start_near()
    text_grads(1, 1)
    image_rings[1].middle()
    text_grads(1, 3)
    image_finish(0)
    text_grads(0, 0)
    image_finish(1)
    text_grads(1, 0)

    map_copies[0].wait_recv()
    other_columns = r.mapper.at[:, cols_of(hi + 1, core)]
    map_copies.append(copy(other_columns, other_columns, sibling))
    seconds[0].middle()
    map_copies[1].wait_recv()
    map_copies[2].wait_recv()
    for one in beside_copies:
        one.wait_recv()

    def back_rows(h):
        rows = cut((h % 2) * 256, 256, 256)

        def part(cols):
            r.back[rows, cols] = nt(r.image_grad[rows, :], r.mapper[cols, :]).astype(BF16)

        loop(2, part, 512)

    back_rows(hi)
    here, there = cut(hi * 256, 256, 256), cut((1 - hi) * 256, 256, 256)
    own_cols = cols_of(hi, core)

    def proj_here(cols):
        r.image_dz[cols, 512:768] = tn(final[here, cols], r.image_grad[here, own_cols])

    def down_here(cols):
        r.image_dz[cols, 0:512] = tn(r.active[here, cols], r.back[here, 0:512])

    loop(2, proj_here, 512)
    loop(2, down_here, 512)
    passed = []
    for n in (0, 1):
        across_copies[n].wait_recv()
        block = r.image_grad.at[cut(((1 - hi) * 2 + core) * 128 + n * 64, 64, 64)]
        passed.append(copy(block, block, sibling))
    seconds[1].start()
    for one in passed:
        one.wait_recv()
    back_rows(hi + 1)

    first = (net.x, net.z)
    other = (net.z, net.x)
    along = ((x_on, x_off), (z_on, z_off))
    wide = (pl.ds(0, 512), pl.ds(512, 512))

    def strip_rows(part, k, i=None):
        start = part * PART + ((first[part] + k) % 4) * STRIP
        return cut(start, STRIP) if i is None else cut(start + i * TILE, TILE)

    def side_columns(part, c, k):
        return cut(c * 512 + ((other[part] + k) % 4) * 128, 128, 128)

    def grad_ring(part, c):
        def block(k, i):
            return strip_rows(part, k, i), wide[c]

        n = part * 2 + c
        return RingSum(net, r.grads, block, r.grad_far.at[n], r.grad_near.at[n], *along[part])

    chains = ((1, 0), (1, 1), (0, 0), (0, 1))
    grad_rings = {chain: grad_ring(*chain) for chain in chains}

    def proj_part(cols):
        value = tn(final[there, cols], r.image_grad[there, own_cols])
        value = (value + r.image_dz[cols, 512:768]).astype(BF16)
        r.grads[1024:1152, cols] = value[0:128]
        r.grads[2176:2304, cols] = value[128:256]

    def down(c):
        def part(j, _):
            cols = cut(j * 512, 512, 512)
            if c == 0:
                value = tn(r.active[there, cols], r.back[there, wide[c]]) + r.image_dz[cols, 0:512]
            else:
                value = tn(r.active[:, cols], r.back[:, wide[c]])
            r.grads[cut(PART + j * 512, 512, 128), wide[c]] = value.astype(BF16)
            return 0

        lax.fori_loop(0, 2, part, 0)

    def up(c):
        value = nt(r.back[...], r.second[wide[c], :]) * r.slope[:, wide[c]]
        r.pre[:, wide[c]] = value.astype(BF16)

        def part(rows):
            r.grads[rows, wide[c]] = tn(r.entry[:, rows], r.pre[:, wide[c]]).astype(BF16)

        loop(2, part, 512)

    loop(4, proj_part)
    down(0)
    grad_rings[1, 0].start()
    loads[1].wait()
    loads[2].wait()
    up(0)
    grad_rings[0, 0].start()
    down(1)
    grad_rings[1, 0].middle()
    grad_rings[1, 1].start_far()
    up(1)
    grad_rings[0, 0].middle()
    grad_rings[0, 1].start_far()

    def text_first_sum(half):
        seconds[half].arrive()
        for i in (0, 1):
            r.text_sum[pl.ds(half * 256 + 128 * i, 128), :] = seconds[half].total(i).astype(BF16)
        firsts[half].start()

    seconds[1].middle()
    text_first_sum(0)

    def side_to(part, k):
        return net.at(z=k) if part == 0 else net.at(x=k)

    sides = {}

    def side(part, c):
        ring = grad_rings[part, c]
        ring.arrive()
        sides[part, c] = []
        for n, k in enumerate((2, 1, 3, 0)):
            cols = side_columns(part, c, k)
            near = cut(((other[part] + k) % 4) * 128, 128, 128)
            for i in (0, 1):
                rows = pl.ds(i * TILE, TILE)
                total = ring.total(i, cols, near)
                if k == 0:
                    r.strip[part, rows, wide_tile[c]] = total
                else:
                    r.side_out[part, n, rows, wide_tile[c]] = total.astype(BF16)
            if k:
                sides[part, c].append(
                    copy(
                        r.side_out.at[part, n, :, wide_tile[c]],
                        r.side_in.at[part, n, :, wide_tile[c]],
                        side_to(part, k),
                    )
                )

    wide_tile = (pl.ds(0, 128), pl.ds(128, 128))
    side(1, 0)
    grad_rings[0, 1].start_near()
    side(0, 0)
    grad_rings[1, 1].start_near()
    grad_rings[1, 1].middle()
    grad_rings[0, 1].middle()
    firsts[0].middle()

    kept = cut(net.lo * TILE, TILE)
    given = cut((1 - net.lo) * TILE, TILE)
    tiles = {}

    def tile(part, c):
        for one in sides[part, c]:
            one.wait_recv()
        at = wide_tile[c]

        def total(rows):
            value = r.strip[part, rows, at]
            for n in range(3):
                value = value + r.side_in[part, n, rows, at].astype(F32)
            return value

        r.tile_out[part, :, at] = total(given).astype(BF16)
        tiles[part, c] = copy(r.tile_out.at[part, :, at], r.tile_in.at[part, :, at], pair_lo)
        r.tile[part, :, at] = total(kept)

    spread_tile = {}

    def back_tile(part, c):
        tiles[part, c].wait_recv()
        at = wide_tile[c]
        rows = cut(part * PART + first[part] * STRIP + net.lo * TILE, TILE)
        cols = side_columns(part, c, 0)
        r.done[rows, cols] = (r.tile[part, :, at] + r.tile_in[part, :, at].astype(F32)).astype(BF16)
        block = r.done.at[rows, cols]
        spread_tile[part, c] = copy(block, block, pair_lo)

    spread_side = {}

    def back_side(part, c):
        spread_tile[part, c].wait_recv()
        block = r.done.at[strip_rows(part, 0), side_columns(part, c, 0)]
        spread_side[part, c] = [copy(block, block, side_to(part, k)) for k in (2, 1, 3)]

    spread_strip = {}

    def back_strip(part, c):
        for one in spread_side[part, c]:
            one.wait_recv()
        on, off = along[part]
        spread_strip[part, c] = []
        for i, to in ((0, on), (1, off), (1, on), (0, off)):
            block = r.done.at[strip_rows(part, 0, i), wide[c]]
            spread_strip[part, c].append(copy(block, block, to))

    last = []

    def back_far(part, c):
        on, off = along[part]
        for i, k, to in ((0, 3, on), (1, 1, off)):
            spread_strip[part, c][i].wait_recv()
            block = r.done.at[strip_rows(part, k, i), wide[c]]
            last.append(copy(block, block, to))

    tile(1, 0)
    tile(0, 0)
    back_tile(1, 0)
    text_first_sum(1)
    side(1, 1)
    back_tile(0, 0)
    side(0, 1)
    back_side(1, 0)
    back_side(0, 0)
    firsts[1].middle()
    tile(1, 1)
    tile(0, 1)
    before = len(net.started)
    back_strip(1, 0)
    back_strip(0, 0)
    back_tile(1, 1)
    back_tile(0, 1)
    back_side(1, 1)
    back_side(0, 1)
    back_far(1, 0)
    back_far(0, 0)
    back_strip(1, 1)
    back_strip(0, 1)

    for half in halves:
        firsts[half].arrive()
    dz = jnp.concatenate([firsts[half].total(i) for half in halves for i in (0, 1)], axis=0)
    unit = r.text_unit[...]
    text_out[...] = r.text_scale[...] * (dz - unit * jnp.sum(unit * dz, axis=1, keepdims=True))

    net.all_sent(before)
    back_far(1, 1)
    back_far(0, 1)
    outs = []

    def leave(rows, c):
        block = (rows, wide[c])
        outs.append(pltpu.make_async_copy(r.done.at[block], total_out.at[block], r.load.at[10 + len(outs)]))
        outs[-1].start()

    ends = ((1, 0), (0, 0), (1, 1), (0, 1))
    for n, (part, c) in enumerate(ends):
        for one in spread_strip[part, c][2:]:
            one.wait_recv()
        if c == 0:
            for one in last[2 * n : 2 * n + 2]:
                one.wait_recv()
            leave(pl.ds(part * PART, PART), c)
        else:
            for k in (0, 1, 3):
                leave(strip_rows(part, k), c)
    for n, (part, c) in enumerate(ends):
        if c:
            for one in last[2 * n : 2 * n + 2]:
                one.wait_recv()
            leave(strip_rows(part, 2), c)
    net.all_sent()
    for one in outs:
        one.wait()


SCRATCH = dict(
    caption=((128, 1024), BF16),
    final=((512, 1024), BF16),
    own_mapper=((1024, 256), BF16),
    columns=((512, 256), BF16),
    texts=((2048, 1024), BF16),
    text_unit=((128, 1024), F32),
    text_scale=((128, 1), F32),
    embed=((128, 1024), BF16),
    image_unit=((128, 1024), F32),
    image_scale=((128, 1), F32),
    images=((1024, 1024), BF16),
    mapper=((1024, 1024), BF16),
    latent=((512, 1024), BF16),
    second=((1024, 1024), BF16),
    entry=((512, 1024), BF16),
    active=((512, 1024), BF16),
    slope=((512, 1024), F32),
    weights=((1024, 2048), BF16),
    image_dz=((1024, 1024), F32),
    cross_out=((512, 1024), BF16),
    cross_in=((512, 1024), BF16),
    image_sum=((512, 1024), BF16),
    image_far=((2, 2, 32, 1024), BF16),
    image_near=((2, 2, 64, 1024), BF16),
    text_dz=((2048, 1024), BF16),
    text_far=((2, 2, 128, 1024), BF16),
    text_near=((2, 2, 256, 1024), BF16),
    text_sum=((512, 1024), BF16),
    last_far=((2, 2, 32, 1024), BF16),
    last_near=((2, 2, 64, 1024), BF16),
    image_grad=((512, 1024), BF16),
    back=((512, 1024), BF16),
    pre=((512, 1024), BF16),
    grads=((2 * PART, 1024), BF16),
    done=((2 * PART, 1024), BF16),
    grad_far=((4, 2, TILE, 512), BF16),
    grad_near=((4, 2, STRIP, 512), BF16),
    strip=((2, STRIP, 256), F32),
    side_out=((2, 3, STRIP, 256), BF16),
    side_in=((2, 3, STRIP, 256), BF16),
    tile=((2, TILE, 256), F32),
    tile_out=((2, TILE, 256), BF16),
    tile_in=((2, TILE, 256), BF16),
    send=((COPIES,), None),
    recv=((COPIES,), None),
    load=((20,), None),
)


def step(sharp, offset, caption, final, mapper, latent, second, entry):
    return pl.pallas_call(
        step_kernel,
        name="pairs_and_weight_grads",
        out_shape=(
            jax.ShapeDtypeStruct((2 * PART, 1024), BF16),
            jax.ShapeDtypeStruct((128, 1024), F32),
        ),
        in_specs=[SMEM, SMEM] + [ANY] * 6,
        out_specs=(ANY, VMEM),
        scratch_shapes=[
            pltpu.SemaphoreType.DMA(shape) if kind is None else pltpu.VMEM(shape, kind)
            for shape, kind in SCRATCH.values()
        ],
        compiler_params=pltpu.CompilerParams(
            collective_id=0, has_side_effects=True, vmem_limit_bytes=60 * 2**20
        ),
    )(sharp, offset, caption, final, mapper, latent, second, entry)


LION = dict(
    total=((2 * PART, 1024), BF16),
    w_up=((1024, 1024), BF16),
    w_down=((1024, 1024), BF16),
    w_proj=((1024, 256), BF16),
    m_up=((1024, 1024), BF16),
    m_down=((1024, 1024), BF16),
    m_proj=((1024, 256), BF16),
)
LION_OUT = ("u_up", "u_down", "u_proj", "r_up", "r_down", "r_proj")


def lion_kernel(
    total, text, w_up, w_down, w_proj, m_up, m_down, m_proj,
    u_up, u_down, u_proj, r_up, r_down, r_proj, text_out, *scratch,
):
    held = dict(zip(LION, scratch))
    kept = dict(zip(LION_OUT, scratch[len(LION) :]))
    arrive, leave = scratch[-2:]
    given = dict(
        total=total, w_up=w_up, w_down=w_down, w_proj=w_proj, m_up=m_up, m_down=m_down, m_proj=m_proj
    )
    results = dict(u_up=u_up, u_down=u_down, u_proj=u_proj, r_up=r_up, r_down=r_down, r_proj=r_proj)
    whole = slice(None)

    grads = dict(
        down=[(pl.ds(PART, 1024), whole)],
        up=[(pl.ds(0, 1024), whole)],
        proj=[(pl.ds(1024, 128), whole), (pl.ds(PART + 1024, 128), whole)],
    )
    jobs = ("proj", "down", "up")
    loads = []
    for k, name in enumerate(jobs):
        mine = [("w_" + name, (whole, whole)), ("m_" + name, (whole, whole))]
        mine += [("total", one) for one in grads[name]]
        loads.append(
            [
                pltpu.make_async_copy(given[key].at[part], held[key].at[part], arrive.at[k, i])
                for i, (key, part) in enumerate(mine)
            ]
        )
    fetched = pltpu.make_async_copy(text, scratch[-3], leave.at[3, 0])
    passed = pltpu.make_async_copy(scratch[-3], text_out, leave.at[3, 1])
    for one in loads[0] + loads[1] + [fetched]:
        one.start()
    for job in loads[2:]:
        for one in job:
            one.start()

    def blend(m, g):
        return 0.9 * m + 0.1 * g

    def finish(name, at, m, g, mix, floor):
        w = held["w_" + name][at].astype(F32)
        kept["u_" + name][at] = (mix * lax.rsqrt(mix * mix + floor) + w).astype(BF16)
        kept["r_" + name][at] = (0.99 * m + 0.01 * g).astype(BF16)

    def column_job(name, cols, width, grad, count):
        def read(j):
            at = (cut(j * 128, 128, 128), cols)
            g = grad(j)
            m = held["m_" + name][at].astype(F32)
            return at, m, g, blend(m, g)

        def add(j, acc):
            mix = read(j)[3]
            return acc + jnp.sum((mix * mix).reshape(16, 8, width), axis=0)

        acc = lax.fori_loop(0, count, add, jnp.zeros((8, width), F32), unroll=True)
        floor = 0.0625 * (jnp.sum(acc, axis=0, keepdims=True) * (1.0 / 1024) + 1e-06)

        for j in range(count):
            at, m, g, mix = read(j)
            finish(name, at, m, g, mix, floor)

    stores = []

    def send(name, quarter=None):
        n = LION_OUT.index("u_" + name)
        at = (whole, whole) if quarter is None else (pl.ds(quarter * 256, 256), whole)
        if name == "up":
            at = at[::-1]
        for i, key in enumerate(("u_" + name, "r_" + name)):
            sem = leave.at[n, 2 * (quarter or 0) + i]
            stores.append(pltpu.make_async_copy(kept[key].at[at], results[key].at[at], sem))
            stores[-1].start()

    for k, name in enumerate(jobs):
        for one in loads[k]:
            one.wait()
        if name == "down":

            def rows(j, _):
                here = cut(j * 32, 32, 32)
                m = held["m_down"][here, :].astype(F32)
                g = held["total"][cut(PART + j * 32, 32, 32), :].astype(F32)
                mix = blend(m, g)
                floor = 0.0625 * (jnp.mean(mix * mix, axis=1, keepdims=True) + 1e-06)
                finish("down", (here, whole), m, g, mix, floor)
                return 0

            for quarter in range(4):
                lax.fori_loop(quarter * 8, quarter * 8 + 8, rows, 0, unroll=True)
                send("down", quarter)
            fetched.wait()
            passed.start()
        elif name == "up":
            for quarter in range(4):
                cols = pl.ds(quarter * 256, 256)
                column_job(
                    "up", cols, 256, lambda j: held["total"][cut(j * 128, 128, 128), cols].astype(F32), 8
                )
                send("up", quarter)
        else:
            def grad(j):
                rows = cut(1024 + (j % 2) * PART, 128, 128)
                return held["total"][rows, cut((j // 2) * 256, 256, 256)].astype(F32)

            column_job("proj", pl.ds(0, 256), 256, grad, 8)
            send("proj")
    for one in stores:
        one.wait()
    passed.wait()


def lion(total, text, weights, moments):
    square = jax.ShapeDtypeStruct((1024, 1024), BF16)
    narrow = jax.ShapeDtypeStruct((1024, 256), BF16)
    outs = (square, square, narrow, square, square, narrow)
    return pl.pallas_call(
        lion_kernel,
        name="lion",
        out_shape=(*outs, jax.ShapeDtypeStruct(text.shape, F32)),
        in_specs=[ANY] * 8,
        out_specs=(ANY,) * 7,
        scratch_shapes=[pltpu.VMEM(*one) for one in LION.values()]
        + [pltpu.VMEM(one.shape, BF16) for one in outs]
        + [pltpu.VMEM(text.shape, F32)]
        + [pltpu.SemaphoreType.DMA((3, 4)), pltpu.SemaphoreType.DMA((4, 8))],
        compiler_params=pltpu.CompilerParams(vmem_limit_bytes=60 * 2**20),
    )(total, text, *weights, *moments)


def per_device(
    vision_layer_entry,
    latent_preact_values,
    final_layer_result,
    caption_vectors_raw,
    sharpness_factor,
    offset_term,
    first_feedforward_matrix,
    second_feedforward_matrix,
    mapper_matrix,
    first_matrix_velocity,
    second_matrix_velocity,
    mapper_velocity,
):
    total, text_grad = step(
        sharpness_factor,
        offset_term,
        caption_vectors_raw,
        final_layer_result,
        mapper_matrix,
        latent_preact_values,
        second_feedforward_matrix,
        vision_layer_entry,
    )
    return lion(
        total,
        text_grad,
        (first_feedforward_matrix, second_feedforward_matrix, mapper_matrix),
        (first_matrix_velocity, second_matrix_velocity, mapper_velocity),
    )


def solution(mesh):
    return jax.shard_map(
        per_device,
        mesh=mesh,
        in_specs=(
            P("dp", None),
            P("dp", "mp"),
            P("dp", None),
            P(("dp", "mp"), None),
            P(),
            P(),
            P(None, "mp"),
            P("mp", None),
            P(None, "mp"),
            P(None, "mp"),
            P("mp", None),
            P(None, "mp"),
        ),
        out_specs=(
            P(None, "mp"),
            P("mp", None),
            P(None, "mp"),
            P(None, "mp"),
            P("mp", None),
            P(None, "mp"),
            P(("dp", "mp"), None),
        ),
        check_vma=False,
    )
```
